128 devices in a mesh: space: 32 (over z, x, core), head: 4 (over y).
Axes of the slice: x: 4, y: 4, z: 4, core: 2. Of those that a mesh axis runs over, the one named last changes fastest.
Arguments:
- tokens: bfloat16 [32768, 1024], P('space'), may hold values from -70 to 70
- w_qkv: bfloat16 [1024, 3, 1024], P(None, None, 'head'), may hold values from -7 to 7
- w_out: bfloat16 [1024, 1024], P('head'), may hold values from -0.5 to 0.5
- neighbours: int32 [256, 9], P('space'), may hold values from 0 to 71, as said below
- requests: int32 [32, 32, 2], P('space'), may hold values from -1 to 7, as said below
- cotangent: bfloat16 [32768, 1024], P('space', 'head'), may hold values from -6 to 6
Outputs:
- layer_out: bfloat16 [32768, 1024], P('space', 'head')
- grad_tokens: bfloat16 [32768, 1024], P('space', 'head')
- grad_w_qkv: float32 [1024, 3, 1024], P('space', None, 'head')
- grad_w_out: float32 [1024, 1024], P('head', 'space')
The draws below stay inside these ranges and needn't reach their ends.
Inputs may be any that keep to these rules, and one draw needn't show every extreme that they name: `neighbours`: row t starts with t % 8 itself, then 3 other tiles of the same device, then 5 slot entries 8 + p * 2 + c; every slot entry names a filled request of that device, every filled request is named by some tile of that device, and no row names a tile twice. requests[d, p, c] is a tile of device p by its index within p, or -1 for an empty slot; filled slots come first and are distinct, requests[d, d] is empty, and in every draw some device fills all 2 slots towards some other device.
All inputs are finite; a program needn't handle non-finite values.
Results may differ from the reference program's by a relative error of at most 0.02.
The reference program's roundings to bfloat16 on the way (of `normed`, `projected`, `rounded`, `attended`, `grad_attended`, `grad_score`, `far_part` and `grad_qkv`) count: a program that leaves them out, or rounds other values in their place, can miss the bound.
Values may be sent and summed in bfloat16 or wider, within the bound.
A program may use at most 192 MiB of HBM per device.

```python
import jax
import jax.numpy as jnp
from jax import lax

D = 1024
HEADS = 16
HEAD_DIM = 64
TILE = 128
NB_LOCAL = 3
NB_REMOTE = 5
SLOTS = 2
TILES_DEV = 8
HD = 1024
NEIGHBOURS = 9
PEERS = 32
TILES = 256
TOKENS = 32768


def draw_tokens(key, part):
    streams = jax.random.split(jax.random.fold_in(key, 3), 1)
    values = jnp.clip(jax.random.normal(streams[0], (TOKENS, D), jnp.float32), -6.0, 6.0)
    return values.astype(jnp.bfloat16)


def draw_w_qkv(key, part):
    streams = jax.random.split(jax.random.fold_in(key, 5), 1)
    base_rows = jnp.clip(jax.random.normal(streams[0], (D, 3, HD), jnp.float32), -6.0, 6.0) * D ** (-0.5)
    boost = jnp.array([2.5, 1.0, 1.0], jnp.float32)[None, :, None]
    values = base_rows * boost
    return values.astype(jnp.bfloat16)


def layout(key):
    streams = jax.random.split(jax.random.fold_in(key, 11), 6)
    device = jnp.arange(PEERS, dtype=jnp.int32)
    distance = (device[None, :] - device[:, None]) % PEERS
    busy_rate = jax.random.randint(streams[0], (PEERS, 1), 1, 5)
    coin_flip = jax.random.randint(streams[1], (PEERS, PEERS), 0, 4)
    counts = jnp.where(coin_flip < busy_rate, 1, 0)
    counts = jnp.where(distance == 2, 1, counts)
    counts = jnp.where((distance == 1) | (distance == PEERS - 1), SLOTS, counts)
    counts = jnp.where(distance == 0, 0, counts).astype(jnp.int32)
    first_pick = jax.random.randint(streams[2], (PEERS, PEERS), 0, TILES_DEV)
    offset_step = jax.random.randint(streams[3], (PEERS, PEERS), 1, TILES_DEV)
    candidates = jnp.stack([first_pick, (first_pick + offset_step) % TILES_DEV], 2)
    slot_index = jnp.arange(SLOTS, dtype=jnp.int32)
    requests = jnp.where(slot_index[None, None, :] < counts[:, :, None], candidates, -1).astype(jnp.int32)
    request_total = jnp.sum(counts, 1)
    tile_index = jnp.arange(TILES_DEV, dtype=jnp.int32)
    rotation = jax.random.randint(streams[4], (PEERS, 1, 1), 0, TILES_DEV * NB_REMOTE)
    slot_order = (tile_index[None, :, None] * NB_REMOTE + jnp.arange(NB_REMOTE, dtype=jnp.int32)[None, None, :] + rotation) % request_total[:, None, None]
    cumulative = jnp.cumsum(counts, 1)
    source_peer = jnp.sum((cumulative[:, None, None, :] <= slot_order[..., None]).astype(jnp.int32), -1)
    slot_start = jnp.sum(jnp.where(device[None, None, None, :] < source_peer[..., None], counts[:, None, None, :], 0), -1)
    remote_entries = TILES_DEV + source_peer * SLOTS + slot_order - slot_start
    ranking = jax.random.randint(streams[5], (PEERS, TILES_DEV, TILES_DEV - 1), 0, 1 << 20) * TILES_DEV + jnp.arange(TILES_DEV - 1, dtype=jnp.int32)
    offsets = jnp.argsort(ranking, axis=2)[:, :, :NB_LOCAL].astype(jnp.int32) + 1
    local_entries = (tile_index[None, :, None] + offsets) % TILES_DEV
    self_entry = jnp.broadcast_to(tile_index[None, :, None], (PEERS, TILES_DEV, 1))
    neighbours = jnp.concatenate([self_entry, local_entries, remote_entries], 2).reshape(TILES, NEIGHBOURS)
    return (neighbours.astype(jnp.int32), requests)


def draw_neighbours(key, part):
    return layout(key)[0]


def draw_requests(key, part):
    return layout(key)[1]


def shard_levels(stream_key, dims, pieces, smallest, largest):
    level = 1.0
    for dim, blocks in pieces:
        steps = jax.random.uniform(jax.random.fold_in(jax.random.fold_in(stream_key, 6), dim), (blocks,), jnp.float32, smallest / len(pieces), largest / len(pieces))
        level = level * jnp.repeat(jnp.exp(steps), dims[dim] // blocks).reshape((-1,) + (1,) * (len(dims) - 1 - dim))
    return level


def scatter_about(own_key, dims, scale, bound, cuts=(), kind=jnp.bfloat16):
    result = scale * jax.random.normal(own_key, dims, jnp.float32)
    if cuts:
        result = result * shard_levels(own_key, dims, cuts, -0.22, 0.18)
    return jnp.clip(result, -bound, bound).astype(kind)


def setup_inputs(seed: int = 0) -> dict:
    arg_keys = jax.random.split(jax.random.key(seed), 7)
    return {
        "tokens": draw_tokens(jax.random.fold_in(arg_keys[6], 71), 0),
        "w_qkv": draw_w_qkv(jax.random.fold_in(arg_keys[6], 71), 0),
        "w_out": scatter_about(arg_keys[2], (HD, D), (2 * HEAD_DIM) ** -0.5, 0.5, ((0, 4),)),
        "neighbours": draw_neighbours(jax.random.fold_in(arg_keys[6], 71), 0),
        "requests": draw_requests(jax.random.fold_in(arg_keys[6], 71), 0),
        "cotangent": scatter_about(arg_keys[5], (TOKENS, D), 1.0, 6.0, ((0, 32), (1, 4))),
    }


EPSILON = 1e-05

def norm_parts(tokens):
    values = tokens.astype(jnp.float32)
    centred = values - lax.optimization_barrier(jnp.mean(values, axis=1, keepdims=True))
    inverse = lax.rsqrt(lax.optimization_barrier(jnp.mean(centred * centred, axis=1, keepdims=True)) + EPSILON)
    return (centred * inverse, inverse)

def key_table(neighbours, requests):
    owner = (jnp.arange(TILES, dtype=jnp.int32) // TILES_DEV)[:, None]
    slot_index = jnp.maximum(neighbours - TILES_DEV, 0)
    source_peer = slot_index // SLOTS
    fetched = requests[owner, source_peer, slot_index % SLOTS]
    table = jnp.where(neighbours < TILES_DEV, owner * TILES_DEV + neighbours, source_peer * TILES_DEV + fetched)
    return table.astype(jnp.int32)

def reference(tokens, w_qkv, w_out, neighbours, requests, cotangent):
    score_scale = HEAD_DIM ** (-0.5)
    standard, inverse = norm_parts(tokens)
    normed = standard.astype(jnp.bfloat16)
    flat_weight = w_qkv.reshape(D, 3 * HD)
    projected = jnp.dot(normed, flat_weight, preferred_element_type=jnp.float32).astype(jnp.bfloat16)
    projected = projected.reshape(TILES, TILE, 3, HEADS, HEAD_DIM)
    grad_attended = jnp.dot(cotangent, w_out.T, preferred_element_type=jnp.float32).astype(jnp.bfloat16)
    table = key_table(neighbours, requests).reshape(PEERS, TILES_DEV, NEIGHBOURS)
    query_dev = projected[:, :, 0].reshape(PEERS, TILES_DEV, TILE, HEADS, HEAD_DIM)
    key_all = projected[:, :, 1]
    value_all = projected[:, :, 2]
    grads_dev = grad_attended.reshape(PEERS, TILES_DEV, TILE, HEADS, HEAD_DIM)
    entries_dev = neighbours.reshape(PEERS, TILES_DEV, NEIGHBOURS)
    device_ids = jnp.arange(PEERS, dtype=jnp.int32)

    def one_device(carry, inputs):
        device, queries, entries, chosen, grads_out, wanted = inputs
        key_part = key_all[chosen.reshape(-1)].reshape(TILES_DEV, NEIGHBOURS * TILE, HEADS, HEAD_DIM).astype(jnp.float32)
        value_part = value_all[chosen.reshape(-1)].reshape(TILES_DEV, NEIGHBOURS * TILE, HEADS, HEAD_DIM).astype(jnp.float32)
        query_wide = queries.astype(jnp.float32)
        scores = jnp.einsum('tihe,tjhe->thij', query_wide, key_part) * score_scale
        row_top = lax.optimization_barrier(jnp.max(scores, axis=3, keepdims=True))
        weights = jnp.exp(scores - row_top)
        likely = weights / lax.optimization_barrier(jnp.sum(weights, axis=3, keepdims=True))
        rounded = lax.optimization_barrier(likely.astype(jnp.bfloat16)).astype(jnp.float32)
        attended = jnp.einsum('thij,tjhe->tihe', rounded, value_part).astype(jnp.bfloat16)
        grad_wide = grads_out.astype(jnp.float32)
        grad_prob = jnp.einsum('tihe,tjhe->thij', grad_wide, value_part)
        row_delta = lax.optimization_barrier(jnp.sum(likely * grad_prob, axis=3, keepdims=True))
        grad_score = (likely * (grad_prob - row_delta) * score_scale).astype(jnp.bfloat16)
        grad_score = lax.optimization_barrier(grad_score).astype(jnp.float32)
        grad_query = jnp.einsum('thij,tjhe->tihe', grad_score, key_part)
        grad_key = jnp.einsum('thij,tihe->tjhe', grad_score, query_wide)
        grad_value = jnp.einsum('thij,tihe->tjhe', rounded, grad_wide)
        both_parts = jnp.stack([grad_key, grad_value], 2).reshape(TILES_DEV * NEIGHBOURS, TILE, 2, HD)
        summed = jax.ops.segment_sum(both_parts, entries.reshape(-1), num_segments=TILES_DEV + PEERS * SLOTS)
        near_part = summed[:TILES_DEV]
        far_part = lax.optimization_barrier(summed[TILES_DEV:].astype(jnp.bfloat16)).astype(jnp.float32)
        flat_wanted = wanted.reshape(-1)
        owner = jnp.arange(PEERS * SLOTS, dtype=jnp.int32) // SLOTS
        usable = flat_wanted >= 0
        target = jnp.where(usable, owner * TILES_DEV + flat_wanted, 0).astype(jnp.int32)
        far_part = far_part * usable.astype(jnp.float32)[:, None, None, None]
        carry = carry.at[target].add(far_part)
        start_row = (device * TILES_DEV).astype(jnp.int32)
        current = lax.dynamic_slice_in_dim(carry, start_row, TILES_DEV, 0)
        carry = lax.dynamic_update_slice_in_dim(carry, current + near_part, start_row, 0)
        return (carry, (attended, grad_query))
    initial = jnp.zeros((TILES, TILE, 2, HD), jnp.float32)
    pair_grads, (attended, grad_query) = lax.scan(one_device, initial, (device_ids, query_dev, entries_dev, table, grads_dev, requests))
    attended = attended.reshape(TOKENS, HD)
    grad_query = grad_query.reshape(TOKENS, 1, HD)
    grad_qkv = jnp.concatenate([grad_query, pair_grads.reshape(TOKENS, 2, HD)], 1).astype(jnp.bfloat16).reshape(TOKENS, 3 * HD)
    layer_out = (tokens.astype(jnp.float32) + jnp.dot(attended, w_out, preferred_element_type=jnp.float32)).astype(jnp.bfloat16)
    grad_w_qkv = jnp.dot(normed.T, grad_qkv, preferred_element_type=jnp.float32).reshape(D, 3, HD)
    grad_w_out = jnp.dot(attended.T, cotangent, preferred_element_type=jnp.float32)
    grad_normed = jnp.dot(grad_qkv, flat_weight.T, preferred_element_type=jnp.float32)
    first_mean = lax.optimization_barrier(jnp.mean(grad_normed, axis=1, keepdims=True))
    second_mean = lax.optimization_barrier(jnp.mean(grad_normed * standard, axis=1, keepdims=True))
    grad_tokens = (cotangent.astype(jnp.float32) + inverse * (grad_normed - first_mean - standard * second_mean)).astype(jnp.bfloat16)
    return (layer_out, grad_tokens, grad_w_qkv, grad_w_out)
```

```python
import functools

import jax
import jax.numpy as jnp
from jax import lax
from jax.experimental import pallas as pl
from jax.experimental.pallas import tpu as pltpu
from jax.sharding import PartitionSpec as P

HEAD_DIM = 64
NEIGHBOURS = 9
NEAR = 4
EPSILON = 1e-05
F32 = jnp.float32
BF16 = jnp.bfloat16
VMEM_BYTES = 60 * 2**20


def dot(a, b, dims):
    return lax.dot_general(a, b, (dims, ((), ())), preferred_element_type=F32)


def norm_rows(tokens):
    values = tokens.astype(F32)
    mean = jnp.mean(values, axis=1, keepdims=True)
    centred = values - mean
    inverse = lax.rsqrt(jnp.mean(centred * centred, axis=1, keepdims=True) + EPSILON)
    return centred * inverse, mean, inverse


def head_cut(h):
    return slice(h * HEAD_DIM, (h + 1) * HEAD_DIM)


def project_kernel(heads, tokens_ref, w_ref, normed_ref, q_ref, kv_ref, mean_ref, inverse_ref):
    standard, mean, inverse = norm_rows(tokens_ref[...])
    normed = standard.astype(BF16)
    normed_ref[...] = normed
    mean_ref[...] = mean
    inverse_ref[...] = inverse
    q = dot(normed, w_ref[0], ((1,), (0,))).astype(BF16)
    q_ref[...] = (q.astype(F32) * HEAD_DIM ** (-0.5)).astype(BF16)
    k = dot(normed, w_ref[1], ((1,), (0,))).astype(BF16)
    v = dot(normed, w_ref[2], ((1,), (0,))).astype(BF16)
    for h in range(heads):
        pair = jnp.concatenate([k[:, head_cut(h)], v[:, head_cut(h)]], 1)
        kv_ref[:, h] = pair.reshape(kv_ref.shape[0], kv_ref.shape[2], 2 * HEAD_DIM)


def project(tokens, w3, tile_rows):
    rows, width = tokens.shape
    cols = w3.shape[2]
    step = 256
    kv_block = (step // tile_rows, cols // HEAD_DIM, tile_rows, 2 * HEAD_DIM)
    return pl.pallas_call(
        functools.partial(project_kernel, cols // HEAD_DIM),
        grid=(rows // step,),
        in_specs=[
            pl.BlockSpec((step, width), lambda i: (i, 0)),
            pl.BlockSpec((3, width, cols), lambda i: (0, 0, 0)),
        ],
        out_specs=[
            pl.BlockSpec((step, width), lambda i: (i, 0)),
            pl.BlockSpec((step, cols), lambda i: (i, 0)),
            pl.BlockSpec(kv_block, lambda i: (i, 0, 0, 0)),
            pl.BlockSpec((step, 1), lambda i: (i, 0)),
            pl.BlockSpec((step, 1), lambda i: (i, 0)),
        ],
        out_shape=[
            jax.ShapeDtypeStruct((rows, width), BF16),
            jax.ShapeDtypeStruct((rows, cols), BF16),
            jax.ShapeDtypeStruct((rows // tile_rows,) + kv_block[1:], BF16),
            jax.ShapeDtypeStruct((rows, 1), F32),
            jax.ShapeDtypeStruct((rows, 1), F32),
        ],
        compiler_params=pltpu.CompilerParams(vmem_limit_bytes=VMEM_BYTES),
    )(tokens, w3)


def pick_kernel(wanted_ref, kv_ref, out_ref):
    first = pl.program_id(0) * out_ref.shape[0]
    for i in range(out_ref.shape[0]):
        out_ref[i] = kv_ref[jnp.maximum(wanted_ref[first + i], 0)]


def pick_tiles(wanted, kv):
    count = wanted.shape[0]
    step = 8
    return pl.pallas_call(
        pick_kernel,
        grid_spec=pltpu.PrefetchScalarGridSpec(
            num_scalar_prefetch=1,
            grid=(count // step,),
            in_specs=[pl.BlockSpec(kv.shape, lambda i, wanted: (0, 0, 0, 0))],
            out_specs=pl.BlockSpec((step,) + kv.shape[1:], lambda i, wanted: (i, 0, 0, 0)),
        ),
        out_shape=jax.ShapeDtypeStruct((count,) + kv.shape[1:], kv.dtype),
        compiler_params=pltpu.CompilerParams(vmem_limit_bytes=VMEM_BYTES),
    )(wanted, kv)


def attention_kernel(entries_ref, q_ref, cot_ref, w_out_ref, normed_ref, *refs):
    kv_refs = refs[:NEIGHBOURS]
    att_out_ref, near_ref, far_ref, dq_ref, grad_out_ref, grad_q_ref = refs[NEIGHBOURS:-2]
    far_total, held = refs[-2:]
    tile = pl.program_id(0)
    last = pl.num_programs(0) - 1
    heads = q_ref.shape[1] // HEAD_DIM
    own = near_ref.shape[0]

    @pl.when(tile == 0)
    def _():
        near_ref[...] = jnp.zeros_like(near_ref)
        grad_out_ref[...] = jnp.zeros_like(grad_out_ref)
        grad_q_ref[...] = jnp.zeros_like(grad_q_ref)

        @pl.loop(0, far_total.shape[0])
        def _(i):
            far_total[i] = jnp.zeros(far_total.shape[1:], F32)

    cot = cot_ref[...]
    grad_attended = dot(cot, w_out_ref[...], ((1,), (1,))).astype(BF16)
    q = q_ref[...]
    left = lax.broadcasted_iota(jnp.int32, (128, 128), 1) < HEAD_DIM
    mixed_t = []
    for h in range(heads):
        cut = head_cut(h)
        pair = jnp.concatenate([q[:, cut], grad_attended[:, cut]], 1)
        zero = jnp.zeros_like(pair)
        stacked = jnp.concatenate([jnp.where(left, pair, zero), jnp.where(left, zero, pair)], 0)
        kv = jnp.concatenate([r[0, h] for r in kv_refs], 0)
        both = dot(kv, stacked, ((1,), (1,)))
        scores = both[:, :128]
        grad_prob = both[:, 128:]
        weights = jnp.exp(scores - jnp.max(scores, axis=0, keepdims=True))
        inverse = 1.0 / jnp.sum(weights, axis=0, keepdims=True)
        row_delta = jnp.sum(weights * grad_prob, axis=0, keepdims=True) * inverse
        likely = weights * inverse
        grad_score = likely * (grad_prob - row_delta)
        factors = jnp.concatenate([grad_score.astype(BF16), likely.astype(BF16)], 1)
        grad_kv = dot(factors, stacked, ((1,), (0,)))
        for j in range(NEIGHBOURS):
            held[j, h] = grad_kv[j * 128 : (j + 1) * 128]
        mixed_t.append(dot(kv, factors, ((0,), (0,))))

    @pl.loop(0, NEAR)
    def _(j):
        near_ref[entries_ref[tile, j]] += held[j]

    @pl.loop(NEAR, NEIGHBOURS)
    def _(j):
        far_total[entries_ref[tile, j] - own] += held[j]

    dq_t = jnp.concatenate([m[:HEAD_DIM, :128] for m in mixed_t], 0)
    att_t = jnp.concatenate([m[HEAD_DIM:, 128:] for m in mixed_t], 0)
    dq = (dq_t.T * HEAD_DIM ** (-0.5)).astype(BF16)
    attended = att_t.T.astype(BF16)
    dq_ref[...] = dq
    att_out_ref[...] = dot(attended, w_out_ref[...], ((1,), (0,))).astype(BF16)
    grad_out_ref[...] += dot(cot, attended, ((0,), (0,)))
    grad_q_ref[...] += dot(normed_ref[...], dq, ((0,), (0,)))

    @pl.when(tile == last)
    def _():
        @pl.loop(0, far_total.shape[0])
        def _(i):
            far_ref[i] = far_total[i].astype(BF16)


def attention(entries, q, cot, w_out, normed, kv, fetched):
    tiles, heads, rows, mixed = kv.shape
    slots = fetched.shape[0]
    tile_block = (1, heads, rows, mixed)
    cols = q.shape[1]
    width = cot.shape[1]
    whole2 = lambda t, e: (0, 0)
    row2 = lambda t, e: (t, 0)
    kv_specs = []
    for j in range(NEIGHBOURS):
        if j < NEAR:
            kv_specs.append(pl.BlockSpec(tile_block, lambda t, e, j=j: (e[t, j], 0, 0, 0)))
        else:
            kv_specs.append(
                pl.BlockSpec(tile_block, lambda t, e, j=j: (e[t, j] - tiles, 0, 0, 0))
            )
    once = pl.Buffered(1)
    return pl.pallas_call(
        attention_kernel,
        grid_spec=pltpu.PrefetchScalarGridSpec(
            num_scalar_prefetch=1,
            grid=(tiles,),
            in_specs=[
                pl.BlockSpec((rows, cols), row2),
                pl.BlockSpec((rows, width), row2),
                pl.BlockSpec((cols, width), whole2),
                pl.BlockSpec((rows, width), row2),
            ]
            + kv_specs,
            out_specs=[
                pl.BlockSpec((rows, width), row2),
                pl.BlockSpec(kv.shape, lambda t, e: (0, 0, 0, 0), pipeline_mode=once),
                pl.BlockSpec(fetched.shape, lambda t, e: (0, 0, 0, 0), pipeline_mode=once),
                pl.BlockSpec((rows, cols), row2),
                pl.BlockSpec((width, cols), whole2, pipeline_mode=once),
                pl.BlockSpec((width, cols), whole2, pipeline_mode=once),
            ],
            scratch_shapes=[
                pltpu.VMEM(fetched.shape, F32),
                pltpu.VMEM((NEIGHBOURS,) + kv.shape[1:], F32),
            ],
        ),
        out_shape=[
            jax.ShapeDtypeStruct((tiles * rows, width), BF16),
            jax.ShapeDtypeStruct(kv.shape, F32),
            jax.ShapeDtypeStruct(fetched.shape, BF16),
            jax.ShapeDtypeStruct((tiles * rows, cols), BF16),
            jax.ShapeDtypeStruct((width, cols), F32),
            jax.ShapeDtypeStruct((width, cols), F32),
        ],
        compiler_params=pltpu.CompilerParams(vmem_limit_bytes=VMEM_BYTES),
    )(entries, q, cot, w_out, normed, *([kv] * NEAR + [fetched] * (NEIGHBOURS - NEAR)))


def place_kernel(wanted_ref, near_ref, back_ref, grad_kv_ref, total):
    step = pl.program_id(0)
    count = back_ref.shape[0]

    @pl.when(step == 0)
    def _():
        total[...] = near_ref[...]

    for i in range(count):
        tile = wanted_ref[step * count + i]

        @pl.when(tile >= 0)
        def _():
            total[tile] += back_ref[i].astype(F32)

    @pl.when(step == pl.num_programs(0) - 1)
    def _():
        grad_kv_ref[...] = total[...].astype(BF16)


def place(wanted, near, back):
    slots = back.shape[0]
    step = 8
    whole = lambda i, w: (0, 0, 0, 0)
    return pl.pallas_call(
        place_kernel,
        grid_spec=pltpu.PrefetchScalarGridSpec(
            num_scalar_prefetch=1,
            grid=(slots // step,),
            in_specs=[
                pl.BlockSpec(near.shape, whole),
                pl.BlockSpec((step,) + back.shape[1:], lambda i, w: (i, 0, 0, 0)),
            ],
            out_specs=pl.BlockSpec(near.shape, whole),
            scratch_shapes=[pltpu.VMEM(near.shape, F32)],
        ),
        out_shape=jax.ShapeDtypeStruct(near.shape, BF16),
        compiler_params=pltpu.CompilerParams(vmem_limit_bytes=VMEM_BYTES),
    )(wanted, near, back)


def finish_kernel(heads, tokens_ref, dq_ref, grad_kv_ref, w_ref, part_ref, sums_ref, grad_w_ref, total):
    step = pl.program_id(0)

    @pl.when(step == 0)
    def _():
        total[...] = jnp.zeros_like(total)

    standard, _, _ = norm_rows(tokens_ref[...])
    pairs = [grad_kv_ref[:, h].reshape(standard.shape[0], 2 * HEAD_DIM) for h in range(heads)]
    dk = jnp.concatenate([p[:, :HEAD_DIM] for p in pairs], 1)
    dv = jnp.concatenate([p[:, HEAD_DIM:] for p in pairs], 1)
    total[...] += dot(standard.astype(BF16), jnp.concatenate([dk, dv], 1), ((0,), (0,)))
    part = dot(dq_ref[...], w_ref[0], ((1,), (1,)))
    part += dot(dk, w_ref[1], ((1,), (1,)))
    part += dot(dv, w_ref[2], ((1,), (1,)))
    sums = [jnp.sum(part, 1, keepdims=True), jnp.sum(part * standard, 1, keepdims=True)]
    sums_ref[...] = jnp.concatenate(sums, 1)
    part_ref[...] = part.astype(BF16)

    @pl.when(step == pl.num_programs(0) - 1)
    def _():
        grad_w_ref[...] = total[...].astype(BF16)


def finish(tokens, dq, grad_kv, w3):
    rows, width = tokens.shape
    cols = dq.shape[1]
    step = 256
    row2 = lambda i: (i, 0)
    return pl.pallas_call(
        functools.partial(finish_kernel, cols // HEAD_DIM),
        grid=(rows // step,),
        in_specs=[
            pl.BlockSpec((step, width), row2),
            pl.BlockSpec((step, cols), row2),
            pl.BlockSpec((step // grad_kv.shape[2],) + grad_kv.shape[1:], lambda i: (i, 0, 0, 0)),
            pl.BlockSpec((3, width, cols), lambda i: (0, 0, 0)),
        ],
        out_specs=[
            pl.BlockSpec((step, width), row2),
            pl.BlockSpec((step, 2), row2),
            pl.BlockSpec((width, 2 * cols), lambda i: (0, 0)),
        ],
        out_shape=[
            jax.ShapeDtypeStruct((rows, width), BF16),
            jax.ShapeDtypeStruct((rows, 2), F32),
            jax.ShapeDtypeStruct((width, 2 * cols), BF16),
        ],
        scratch_shapes=[pltpu.VMEM((width, 2 * cols), F32)],
        compiler_params=pltpu.CompilerParams(vmem_limit_bytes=VMEM_BYTES),
    )(tokens, dq, grad_kv, w3)


def exchange(array):
    return lax.all_to_all(array, "space", split_axis=0, concat_axis=0, tiled=True)


def sum_rows(part, peers):
    width, cols = part.shape
    arrived = exchange(part.reshape(peers, width // peers, cols))
    return jnp.sum(arrived.astype(F32), 0)


def on_device(tokens, w_qkv, w_out, neighbours, requests, cotangent):
    row_count, width = tokens.shape
    tiles = neighbours.shape[0]
    rows = row_count // tiles
    cols = w_qkv.shape[2]
    peers = lax.axis_size("space")
    slot_count = requests.shape[2]
    share = cotangent.shape[1]
    column = lax.axis_index("head") * share
    w3 = jnp.transpose(w_qkv, (1, 0, 2))

    incoming = exchange(requests.reshape(peers, slot_count)).reshape(-1)
    cot_full = lax.all_gather(cotangent, "head", axis=1, tiled=True)
    normed, q, kv, mean, inverse = project(tokens, w3, rows)
    outgoing = pick_tiles(incoming, kv)
    fetched = exchange(outgoing.reshape((peers, slot_count) + kv.shape[1:]))
    fetched = fetched.reshape(outgoing.shape)
    att_out, near, far, dq, grad_out, grad_q = attention(
        neighbours, q, cot_full, w_out, normed, kv, fetched
    )
    back = exchange(far.reshape((peers, slot_count) + kv.shape[1:]))
    summed = lax.psum_scatter(att_out, "head", scatter_dimension=1, tiled=True)
    early = sum_rows(jnp.concatenate([grad_out, grad_q], 1).astype(BF16), peers)
    grad_kv = place(incoming, near, back.reshape(outgoing.shape))
    part, sums, grad_w_kv = finish(tokens, dq, grad_kv, w3)
    late = sum_rows(grad_w_kv, peers)
    own_part = lax.psum_scatter(part, "head", scatter_dimension=1, tiled=True).astype(F32)
    sums = lax.psum(sums, "head") / width

    own_tokens = lax.dynamic_slice_in_dim(tokens, column, share, 1).astype(F32)
    layer_out = (own_tokens + summed.astype(F32)).astype(BF16)
    own_standard = (own_tokens - mean) * inverse
    grad_tokens = (
        cotangent.astype(F32) + inverse * (own_part - sums[:, :1] - own_standard * sums[:, 1:])
    ).astype(BF16)
    grad_w_qkv = jnp.concatenate([early[:, cols:], late], 1).reshape(-1, 3, cols)
    grad_w_out = early[:, :cols].T
    return (layer_out, grad_tokens, grad_w_qkv, grad_w_out)


def solution(mesh):
    placed = (
        P("space", None),
        P(None, None, "head"),
        P("head", None),
        P("space", None),
        P("space", None, None),
        P("space", "head"),
    )
    return jax.shard_map(
        on_device,
        mesh=mesh,
        in_specs=placed,
        out_specs=(
            P("space", "head"),
            P("space", "head"),
            P("space", None, "head"),
            P("head", "space"),
        ),
        check_vma=False,
    )
```

```python
import functools

import jax
import jax.numpy as jnp
from jax import lax
from jax.experimental import pallas as pl
from jax.experimental.pallas import tpu as pltpu
from jax.sharding import PartitionSpec as P

HEAD_DIM = 64
NEIGHBOURS = 9
NEAR = 4
REACHES = (1, 4)
EPSILON = 1e-05
F32 = jnp.float32
BF16 = jnp.bfloat16
VMEM_BYTES = 60 * 2**20


def dot(a, b, dims):
    return lax.dot_general(a, b, (dims, ((), ())), preferred_element_type=F32)


def norm_rows(tokens):
    values = tokens.astype(F32)
    mean = jnp.mean(values, axis=1, keepdims=True)
    centred = values - mean
    inverse = lax.rsqrt(jnp.mean(centred * centred, axis=1, keepdims=True) + EPSILON)
    return centred * inverse, mean, inverse


def head_cut(h):
    return slice(h * HEAD_DIM, (h + 1) * HEAD_DIM)


def project_kernel(heads, tokens_ref, w_ref, normed_ref, q_ref, kv_ref, mean_ref, inverse_ref):
    standard, mean, inverse = norm_rows(tokens_ref[...])
    normed = standard.astype(BF16)
    normed_ref[...] = normed
    mean_ref[...] = mean
    inverse_ref[...] = inverse
    q = dot(normed, w_ref[0], ((1,), (0,))).astype(BF16)
    q_ref[...] = (q.astype(F32) * HEAD_DIM ** (-0.5)).astype(BF16)
    k = dot(normed, w_ref[1], ((1,), (0,))).astype(BF16)
    v = dot(normed, w_ref[2], ((1,), (0,))).astype(BF16)
    for h in range(heads):
        pair = jnp.concatenate([k[:, head_cut(h)], v[:, head_cut(h)]], 1)
        kv_ref[:, h] = pair.reshape(kv_ref.shape[0], kv_ref.shape[2], 2 * HEAD_DIM)


def project(tokens, w3, tile_rows):
    rows, width = tokens.shape
    cols = w3.shape[2]
    step = 256
    kv_block = (step // tile_rows, cols // HEAD_DIM, tile_rows, 2 * HEAD_DIM)
    return pl.pallas_call(
        functools.partial(project_kernel, cols // HEAD_DIM),
        grid=(rows // step,),
        in_specs=[
            pl.BlockSpec((step, width), lambda i: (i, 0)),
            pl.BlockSpec((3, width, cols), lambda i: (0, 0, 0)),
        ],
        out_specs=[
            pl.BlockSpec((step, width), lambda i: (i, 0)),
            pl.BlockSpec((step, cols), lambda i: (i, 0)),
            pl.BlockSpec(kv_block, lambda i: (i, 0, 0, 0)),
            pl.BlockSpec((step, 1), lambda i: (i, 0)),
            pl.BlockSpec((step, 1), lambda i: (i, 0)),
        ],
        out_shape=[
            jax.ShapeDtypeStruct((rows, width), BF16),
            jax.ShapeDtypeStruct((rows, cols), BF16),
            jax.ShapeDtypeStruct((rows // tile_rows,) + kv_block[1:], BF16),
            jax.ShapeDtypeStruct((rows, 1), F32),
            jax.ShapeDtypeStruct((rows, 1), F32),
        ],
        compiler_params=pltpu.CompilerParams(vmem_limit_bytes=VMEM_BYTES),
    )(tokens, w3)


def copy_to(src, dst, sems, index, device):
    return pltpu.make_async_remote_copy(
        src_ref=src,
        dst_ref=dst,
        send_sem=sems.at[0, index],
        recv_sem=sems.at[1, index],
        device_id=device,
        device_id_type=pl.DeviceIdType.MESH,
    )


def greet(peers, groups):
    barrier = pltpu.get_barrier_semaphore()
    me, group = lax.axis_index("space"), lax.axis_index("head")

    @pl.loop(1, peers)
    def _(r):
        pl.semaphore_signal(
            barrier,
            inc=1,
            device_id={"space": lax.rem(me + r, peers)},
            device_id_type=pl.DeviceIdType.MESH,
        )

    for k in range(1, groups):
        pl.semaphore_signal(
            barrier,
            inc=1,
            device_id={"head": lax.rem(group + k, groups)},
            device_id_type=pl.DeviceIdType.MESH,
        )
    pl.semaphore_wait(barrier, peers + groups - 2)


def slot_ranges(peers, reach):
    if 2 * reach >= peers - 1:
        return [(1, peers, True)]
    return [(1, reach + 1, True), (peers - reach, peers, True), (reach + 1, peers - reach, False)]


def fetch_kernel(peers, groups, reach, wanted_ref, kv_ref, cot_ref, out_ref, cots_ref, staged, sems, row_sems, own_sem):
    me, group = lax.axis_index("space"), lax.axis_index("head")
    greet(peers, groups)
    own = pltpu.make_async_copy(cot_ref, cots_ref.at[group], own_sem)
    own.start()

    def across(k):
        return copy_to(
            cot_ref, cots_ref.at[group], row_sems, k, {"head": lax.rem(group + k, groups)}
        )

    def along(r, wide):
        peer = lax.rem(me + r, peers)
        if wide:
            return copy_to(staged.at[r], out_ref.at[me], sems, r, {"space": peer})
        return copy_to(staged.at[r, 0], out_ref.at[me, 0], sems, r, {"space": peer})

    for k in range(1, groups):
        across(k).start()
    slots = staged.shape[1]
    for low, high, wide in slot_ranges(peers, reach):

        @pl.loop(low, high)
        def _(r, wide=wide):
            peer = lax.rem(me + r, peers)
            for c in range(slots if wide else 1):
                staged[r, c] = kv_ref[jnp.maximum(wanted_ref[peer * slots + c], 0)]
            along(r, wide).start()

    for low, high, wide in slot_ranges(peers, reach):

        @pl.loop(low, high)
        def _(r, wide=wide):
            along(r, wide).wait()

    for k in range(1, groups):
        across(k).wait()
    own.wait()


def fetch(wanted, kv, cot, peers, groups, reach, number):
    slots = wanted.shape[0] // peers
    out = (peers, slots) + kv.shape[1:]
    whole = pl.BlockSpec(memory_space=pl.ANY)
    return pl.pallas_call(
        functools.partial(fetch_kernel, peers, groups, reach),
        in_specs=[
            pl.BlockSpec(memory_space=pltpu.SMEM),
            pl.BlockSpec(memory_space=pltpu.VMEM),
            whole,
        ],
        out_specs=[whole, whole],
        out_shape=[
            jax.ShapeDtypeStruct(out, kv.dtype),
            jax.ShapeDtypeStruct((groups,) + cot.shape, cot.dtype),
        ],
        scratch_shapes=[
            pltpu.VMEM(out, kv.dtype),
            pltpu.SemaphoreType.DMA((2, peers)),
            pltpu.SemaphoreType.DMA((2, groups)),
            pltpu.SemaphoreType.DMA,
        ],
        compiler_params=pltpu.CompilerParams(
            collective_id=number, has_side_effects=True, vmem_limit_bytes=VMEM_BYTES
        ),
    )(wanted, kv, cot)


def swap_kernel(peers, groups, reach, spaces, heads, slotted, *refs):
    me, group = lax.axis_index("space"), lax.axis_index("head")
    count = spaces + heads + slotted
    sources, targets = refs[:count], refs[count : 2 * count]
    sems, head_sems, own_sems = refs[2 * count :]
    greet(peers, groups)
    owns = []
    for i in range(slotted, count):
        at = me if i < slotted + spaces else group
        owns.append(pltpu.make_async_copy(sources[i].at[at], targets[i].at[at], own_sems.at[i]))
        owns[-1].start()

    def across(i, k):
        peer = lax.rem(group + k, groups)
        return copy_to(
            sources[i].at[peer], targets[i].at[group], head_sems.at[i], k, {"head": peer}
        )

    def along(i, r, wide):
        peer = lax.rem(me + r, peers)
        src, dst = sources[i].at[peer], targets[i].at[me]
        if not wide:
            src, dst = sources[i].at[peer, 0], targets[i].at[me, 0]
        return copy_to(src, dst, sems.at[i], r, {"space": peer})

    def each(act):
        for i in range(slotted, slotted + spaces):

            @pl.loop(1, peers)
            def _(r, i=i):
                act(along(i, r, True))

        for i in range(slotted):
            for low, high, wide in slot_ranges(peers, reach):

                @pl.loop(low, high)
                def _(r, i=i, wide=wide):
                    act(along(i, r, wide))

    for i in range(slotted + spaces, count):
        for k in range(1, groups):
            across(i, k).start()
    each(lambda copy: copy.start())
    each(lambda copy: copy.wait())
    for i in range(slotted + spaces, count):
        for k in range(1, groups):
            across(i, k).wait()
    for own in owns:
        own.wait()


def swap(slotted, spaces, heads, peers, groups, reach, number):
    arrays = (*slotted, *spaces, *heads)
    whole = pl.BlockSpec(memory_space=pl.ANY)
    return pl.pallas_call(
        functools.partial(
            swap_kernel, peers, groups, reach, len(spaces), len(heads), len(slotted)
        ),
        in_specs=[whole] * len(arrays),
        out_specs=[whole] * len(arrays),
        out_shape=[jax.ShapeDtypeStruct(a.shape, a.dtype) for a in arrays],
        scratch_shapes=[
            pltpu.SemaphoreType.DMA((len(arrays), 2, peers)),
            pltpu.SemaphoreType.DMA((len(arrays), 2, groups)),
            pltpu.SemaphoreType.DMA((len(arrays),)),
        ],
        compiler_params=pltpu.CompilerParams(collective_id=number, has_side_effects=True),
    )(*arrays)


def attention_kernel(entries_ref, q_ref, cot_ref, w_out_ref, normed_ref, *refs):
    kv_refs = refs[:NEIGHBOURS]
    att_out_ref, near_ref, far_ref, dq_ref, early_ref = refs[NEIGHBOURS:-4]
    far_total, held, grad_out, grad_q = refs[-4:]
    tile = pl.program_id(0)
    last = pl.num_programs(0) - 1
    heads = q_ref.shape[1] // HEAD_DIM
    own = near_ref.shape[0]

    @pl.when(tile == 0)
    def _():
        near_ref[...] = jnp.zeros_like(near_ref)
        grad_out[...] = jnp.zeros_like(grad_out)
        grad_q[...] = jnp.zeros_like(grad_q)

        @pl.loop(0, far_total.shape[0])
        def _(i):
            far_total[i] = jnp.zeros(far_total.shape[1:], F32)

    groups = cot_ref.shape[0]
    share = cot_ref.shape[2]
    cot = jnp.concatenate([cot_ref[g] for g in range(groups)], 1)
    grad_attended = dot(cot, w_out_ref[...], ((1,), (1,))).astype(BF16)
    q = q_ref[...]
    left = lax.broadcasted_iota(jnp.int32, (128, 128), 1) < HEAD_DIM
    mixed_t = []
    for h in range(heads):
        cut = head_cut(h)
        pair = jnp.concatenate([q[:, cut], grad_attended[:, cut]], 1)
        zero = jnp.zeros_like(pair)
        stacked = jnp.concatenate([jnp.where(left, pair, zero), jnp.where(left, zero, pair)], 0)
        kv = jnp.concatenate([r[0, h] for r in kv_refs], 0)
        both = dot(kv, stacked, ((1,), (1,)))
        scores = both[:, :128]
        grad_prob = both[:, 128:]
        weights = jnp.exp(scores - jnp.max(scores, axis=0, keepdims=True))
        inverse = 1.0 / jnp.sum(weights, axis=0, keepdims=True)
        row_delta = jnp.sum(weights * grad_prob, axis=0, keepdims=True) * inverse
        likely = weights * inverse
        grad_score = likely * (grad_prob - row_delta)
        factors = jnp.concatenate([grad_score.astype(BF16), likely.astype(BF16)], 1)
        grad_kv = dot(factors, stacked, ((1,), (0,)))
        for j in range(NEIGHBOURS):
            held[j, h] = grad_kv[j * 128 : (j + 1) * 128]
        mixed_t.append(dot(kv, factors, ((0,), (0,))))

    @pl.loop(0, NEAR)
    def _(j):
        near_ref[entries_ref[tile, j]] += held[j]

    @pl.loop(NEAR, NEIGHBOURS)
    def _(j):
        far_total[entries_ref[tile, j] - own] += held[j]

    dq_t = jnp.concatenate([m[:HEAD_DIM, :128] for m in mixed_t], 0)
    att_t = jnp.concatenate([m[HEAD_DIM:, 128:] for m in mixed_t], 0)
    dq = (dq_t.T * HEAD_DIM ** (-0.5)).astype(BF16)
    attended = att_t.T.astype(BF16)
    dq_ref[...] = dq
    att_out = dot(attended, w_out_ref[...], ((1,), (0,))).astype(BF16)
    for g in range(groups):
        att_out_ref[g] = att_out[:, g * share : (g + 1) * share]
    grad_out[...] += dot(cot, attended, ((0,), (0,)))
    grad_q[...] += dot(normed_ref[...], dq, ((0,), (0,)))

    @pl.when(tile == last)
    def _():
        @pl.loop(0, far_total.shape[0])
        def _(i):
            far_ref[i] = far_total[i].astype(BF16)

        cols = grad_q.shape[1]
        early_ref[:, :cols] = grad_out[...].astype(BF16)
        early_ref[:, cols:] = grad_q[...].astype(BF16)


def attention(entries, q, cot, w_out, normed, kv, fetched):
    tiles, heads, rows, mixed = kv.shape
    slots = fetched.shape[0]
    tile_block = (1, heads, rows, mixed)
    cols = q.shape[1]
    groups, _, share = cot.shape
    width = groups * share
    cot_spec = pl.BlockSpec((groups, rows, share), lambda t, e: (0, t, 0))
    whole2 = lambda t, e: (0, 0)
    row2 = lambda t, e: (t, 0)
    kv_specs = []
    for j in range(NEIGHBOURS):
        if j < NEAR:
            kv_specs.append(pl.BlockSpec(tile_block, lambda t, e, j=j: (e[t, j], 0, 0, 0)))
        else:
            kv_specs.append(
                pl.BlockSpec(tile_block, lambda t, e, j=j: (e[t, j] - tiles, 0, 0, 0))
            )
    once = pl.Buffered(1)
    return pl.pallas_call(
        attention_kernel,
        grid_spec=pltpu.PrefetchScalarGridSpec(
            num_scalar_prefetch=1,
            grid=(tiles,),
            in_specs=[
                pl.BlockSpec((rows, cols), row2),
                cot_spec,
                pl.BlockSpec((cols, width), whole2),
                pl.BlockSpec((rows, width), row2),
            ]
            + kv_specs,
            out_specs=[
                cot_spec,
                pl.BlockSpec(kv.shape, lambda t, e: (0, 0, 0, 0), pipeline_mode=once),
                pl.BlockSpec(fetched.shape, lambda t, e: (0, 0, 0, 0), pipeline_mode=once),
                pl.BlockSpec((rows, cols), row2),
                pl.BlockSpec((width, 2 * cols), whole2, pipeline_mode=once),
            ],
            scratch_shapes=[
                pltpu.VMEM(fetched.shape, F32),
                pltpu.VMEM((NEIGHBOURS,) + kv.shape[1:], F32),
                pltpu.VMEM((width, cols), F32),
                pltpu.VMEM((width, cols), F32),
            ],
        ),
        out_shape=[
            jax.ShapeDtypeStruct(cot.shape, BF16),
            jax.ShapeDtypeStruct(kv.shape, F32),
            jax.ShapeDtypeStruct(fetched.shape, BF16),
            jax.ShapeDtypeStruct((tiles * rows, cols), BF16),
            jax.ShapeDtypeStruct((width, 2 * cols), BF16),
        ],
        compiler_params=pltpu.CompilerParams(vmem_limit_bytes=50 * 2**20),
    )(entries, q, cot, w_out, normed, *([kv] * NEAR + [fetched] * (NEIGHBOURS - NEAR)))


def place_kernel(wanted_ref, near_ref, back_ref, grad_kv_ref, total):
    step = pl.program_id(0)
    count = back_ref.shape[0]

    @pl.when(step == 0)
    def _():
        total[...] = near_ref[...]

    for i in range(count):
        tile = wanted_ref[step * count + i]

        @pl.when(tile >= 0)
        def _():
            total[tile] += back_ref[i].astype(F32)

    @pl.when(step == pl.num_programs(0) - 1)
    def _():
        grad_kv_ref[...] = total[...].astype(BF16)


def place(wanted, near, back):
    slots = back.shape[0]
    step = 8
    whole = lambda i, w: (0, 0, 0, 0)
    return pl.pallas_call(
        place_kernel,
        grid_spec=pltpu.PrefetchScalarGridSpec(
            num_scalar_prefetch=1,
            grid=(slots // step,),
            in_specs=[
                pl.BlockSpec(near.shape, whole),
                pl.BlockSpec((step,) + back.shape[1:], lambda i, w: (i, 0, 0, 0)),
            ],
            out_specs=pl.BlockSpec(near.shape, whole),
            scratch_shapes=[pltpu.VMEM(near.shape, F32)],
        ),
        out_shape=jax.ShapeDtypeStruct(near.shape, BF16),
        compiler_params=pltpu.CompilerParams(vmem_limit_bytes=VMEM_BYTES),
    )(wanted, near, back)


def finish_kernel(heads, tokens_ref, dq_ref, grad_kv_ref, w_ref, part_ref, sums_ref, grad_w_ref, total):
    step = pl.program_id(0)

    @pl.when(step == 0)
    def _():
        total[...] = jnp.zeros_like(total)

    standard, _, _ = norm_rows(tokens_ref[...])
    pairs = [grad_kv_ref[:, h].reshape(standard.shape[0], 2 * HEAD_DIM) for h in range(heads)]
    dk = jnp.concatenate([p[:, :HEAD_DIM] for p in pairs], 1)
    dv = jnp.concatenate([p[:, HEAD_DIM:] for p in pairs], 1)
    total[...] += dot(standard.astype(BF16), jnp.concatenate([dk, dv], 1), ((0,), (0,)))
    part = dot(dq_ref[...], w_ref[0], ((1,), (1,)))
    part += dot(dk, w_ref[1], ((1,), (1,)))
    part += dot(dv, w_ref[2], ((1,), (1,)))
    sums = [jnp.sum(part, 1, keepdims=True), jnp.sum(part * standard, 1, keepdims=True)]
    sums_ref[...] = jnp.concatenate(sums, 1).T
    share = part_ref.shape[2]
    for g in range(part_ref.shape[0]):
        part_ref[g] = part[:, g * share : (g + 1) * share].astype(BF16)

    @pl.when(step == pl.num_programs(0) - 1)
    def _():
        grad_w_ref[...] = total[...].astype(BF16)


def finish(tokens, dq, grad_kv, w3, groups):
    rows, width = tokens.shape
    cols = dq.shape[1]
    step = 256
    row2 = lambda i: (i, 0)
    return pl.pallas_call(
        functools.partial(finish_kernel, cols // HEAD_DIM),
        grid=(rows // step,),
        in_specs=[
            pl.BlockSpec((step, width), row2),
            pl.BlockSpec((step, cols), row2),
            pl.BlockSpec((step // grad_kv.shape[2],) + grad_kv.shape[1:], lambda i: (i, 0, 0, 0)),
            pl.BlockSpec((3, width, cols), lambda i: (0, 0, 0)),
        ],
        out_specs=[
            pl.BlockSpec((groups, step, width // groups), lambda i: (0, i, 0)),
            pl.BlockSpec((2, step), lambda i: (0, i)),
            pl.BlockSpec((width, 2 * cols), lambda i: (0, 0)),
        ],
        out_shape=[
            jax.ShapeDtypeStruct((groups, rows, width // groups), BF16),
            jax.ShapeDtypeStruct((2, rows), F32),
            jax.ShapeDtypeStruct((width, 2 * cols), BF16),
        ],
        scratch_shapes=[pltpu.VMEM((width, 2 * cols), F32)],
        compiler_params=pltpu.CompilerParams(vmem_limit_bytes=VMEM_BYTES),
    )(tokens, dq, grad_kv, w3)


def on_device(tokens, w_qkv, w_out, neighbours, requests, cotangent):
    row_count, width = tokens.shape
    tiles = neighbours.shape[0]
    rows = row_count // tiles
    cols = w_qkv.shape[2]
    peers, groups = lax.axis_size("space"), lax.axis_size("head")
    share = cotangent.shape[1]
    me = lax.axis_index("space")
    column = lax.axis_index("head") * share
    w3 = jnp.transpose(w_qkv, (1, 0, 2))

    table = lax.all_gather(requests[0], "space")
    wanted = lax.dynamic_index_in_dim(table, me, 1, keepdims=False).reshape(-1)
    apart = jnp.abs(jnp.arange(peers)[:, None] - jnp.arange(peers)[None, :])
    apart = jnp.minimum(apart, peers - apart)
    reach = jnp.max(jnp.where(jnp.any(table[:, :, 1:] >= 0, axis=2), apart, 0))
    level = (reach > REACHES[0]).astype(jnp.int32) + (reach > REACHES[1]).astype(jnp.int32)
    reaches = (*REACHES, peers)

    normed, q, kv, mean, inverse = project(tokens, w3, rows)
    fetched, cots = lax.switch(
        level,
        [
            functools.partial(fetch, peers=peers, groups=groups, reach=r, number=n)
            for n, r in enumerate(reaches)
        ],
        wanted,
        kv,
        cotangent,
    )
    attended, near, far, dq, early = attention(
        neighbours, q, cots, w_out, normed, kv, fetched.reshape((-1,) + kv.shape[1:])
    )

    def give_back(far, early, attended, reach, number):
        return swap((far,), (early,), (attended,), peers, groups, reach, number)

    back, early, attended = lax.switch(
        level,
        [
            functools.partial(give_back, reach=r, number=n + len(reaches))
            for n, r in enumerate(reaches)
        ],
        far.reshape(fetched.shape),
        early.reshape(peers, width // peers, 2 * cols),
        attended,
    )
    grad_kv = place(wanted, near, back.reshape(far.shape))
    part, sums, late = finish(tokens, dq, grad_kv, w3, groups)
    sums = jnp.broadcast_to(sums, (groups,) + sums.shape)
    late = late.reshape(peers, width // peers, 2 * cols)
    late, part, sums = swap((), (late,), (part, sums), peers, groups, peers, 2 * len(reaches))

    own_tokens = lax.dynamic_slice_in_dim(tokens, column, share, 1).astype(F32)
    layer_out = (own_tokens + jnp.sum(attended.astype(F32), 0)).astype(BF16)
    own_standard = (own_tokens - mean) * inverse
    own_part = jnp.sum(part.astype(F32), 0)
    means = (jnp.sum(sums, 0) / width)[:, :, None]
    grad_tokens = (
        cotangent.astype(F32) + inverse * (own_part - means[0] - own_standard * means[1])
    ).astype(BF16)
    early = jnp.sum(early.astype(F32), 0)
    late = jnp.sum(late.astype(F32), 0)
    grad_w_qkv = jnp.concatenate([early[:, cols:], late], 1).reshape(-1, 3, cols)
    grad_w_out = early[:, :cols].T
    return (layer_out, grad_tokens, grad_w_qkv, grad_w_out)


def solution(mesh):
    placed = (
        P("space", None),
        P(None, None, "head"),
        P("head", None),
        P("space", None),
        P("space", None, None),
        P("space", "head"),
    )
    return jax.shard_map(
        on_device,
        mesh=mesh,
        in_specs=placed,
        out_specs=(
            P("space", "head"),
            P("space", "head"),
            P("space", None, "head"),
            P("head", "space"),
        ),
        check_vma=False,
    )
```

```python
import functools

import jax
import jax.numpy as jnp
from jax import lax
from jax.experimental import pallas as pl
from jax.experimental.pallas import tpu as pltpu
from jax.sharding import PartitionSpec as P

HEAD_DIM = 64
NEIGHBOURS = 9
NEAR = 4
REACHES = (1, 4)
AT_ONCE = 2
SLOTS = 2
EPSILON = 1e-05
F32 = jnp.float32
BF16 = jnp.bfloat16
VMEM_BYTES = 60 * 2**20


def dot(a, b, dims):
    return lax.dot_general(a, b, (dims, ((), ())), preferred_element_type=F32)


def norm_rows(tokens):
    values = tokens.astype(F32)
    mean = jnp.mean(values, axis=1, keepdims=True)
    centred = values - mean
    inverse = lax.rsqrt(jnp.mean(centred * centred, axis=1, keepdims=True) + EPSILON)
    return centred * inverse, mean, inverse


def head_cut(h):
    return slice(h * HEAD_DIM, (h + 1) * HEAD_DIM)


def project_kernel(heads, tokens_ref, w_ref, normed_ref, q_ref, kv_ref, mean_ref, inverse_ref):
    standard, mean, inverse = norm_rows(tokens_ref[...])
    normed = standard.astype(BF16)
    normed_ref[...] = normed
    mean_ref[...] = mean
    inverse_ref[...] = inverse
    q = dot(normed, w_ref[0], ((1,), (0,))).astype(BF16)
    q_ref[...] = (q.astype(F32) * HEAD_DIM ** (-0.5)).astype(BF16)
    k = dot(normed, w_ref[1], ((1,), (0,))).astype(BF16)
    v = dot(normed, w_ref[2], ((1,), (0,))).astype(BF16)
    for h in range(heads):
        pair = jnp.concatenate([k[:, head_cut(h)], v[:, head_cut(h)]], 1)
        kv_ref[:, h] = pair.reshape(kv_ref.shape[0], kv_ref.shape[2], 2 * HEAD_DIM)


def project(tokens, w3, tile_rows):
    rows, width = tokens.shape
    cols = w3.shape[2]
    step = 256
    kv_block = (step // tile_rows, cols // HEAD_DIM, tile_rows, 2 * HEAD_DIM)
    return pl.pallas_call(
        functools.partial(project_kernel, cols // HEAD_DIM),
        grid=(rows // step,),
        in_specs=[
            pl.BlockSpec((step, width), lambda i: (i, 0)),
            pl.BlockSpec((3, width, cols), lambda i: (0, 0, 0)),
        ],
        out_specs=[
            pl.BlockSpec((step, width), lambda i: (i, 0)),
            pl.BlockSpec((step, cols), lambda i: (i, 0)),
            pl.BlockSpec(kv_block, lambda i: (i, 0, 0, 0)),
            pl.BlockSpec((step, 1), lambda i: (i, 0)),
            pl.BlockSpec((step, 1), lambda i: (i, 0)),
        ],
        out_shape=[
            jax.ShapeDtypeStruct((rows, width), BF16),
            jax.ShapeDtypeStruct((rows, cols), BF16),
            jax.ShapeDtypeStruct((rows // tile_rows,) + kv_block[1:], BF16),
            jax.ShapeDtypeStruct((rows, 1), F32),
            jax.ShapeDtypeStruct((rows, 1), F32),
        ],
        compiler_params=pltpu.CompilerParams(vmem_limit_bytes=VMEM_BYTES),
    )(tokens, w3)


def copy_to(src, dst, sems, index, device):
    return pltpu.make_async_remote_copy(
        src_ref=src,
        dst_ref=dst,
        send_sem=sems.at[0, index],
        recv_sem=sems.at[1, index],
        device_id=device,
        device_id_type=pl.DeviceIdType.MESH,
    )


def greet(peers, groups):
    barrier = pltpu.get_barrier_semaphore()
    me, group = lax.axis_index("space"), lax.axis_index("head")

    @pl.loop(1, peers)
    def _(r):
        pl.semaphore_signal(
            barrier,
            inc=1,
            device_id={"space": lax.rem(me + r, peers)},
            device_id_type=pl.DeviceIdType.MESH,
        )

    for k in range(1, groups):
        pl.semaphore_signal(
            barrier,
            inc=1,
            device_id={"head": lax.rem(group + k, groups)},
            device_id_type=pl.DeviceIdType.MESH,
        )
    pl.semaphore_wait(barrier, peers + groups - 2)


def torus_order():
    near = [(0, 1), (0, 3), (1, 0), (3, 0), (1, 1), (3, 3), (1, 3), (3, 1)]
    far = [(0, 2), (2, 0), (1, 2), (2, 1), (3, 2), (2, 3), (2, 2)]
    order = [(0, 0, 1)]
    for group in (near[:4], near[4:], far[:2], far[2:6], far[6:]):
        order += [(z, x, core) for core in (0, 1) for z, x in group]
    return order


ORDER = torus_order()


def torus_peer(me, step):
    z = lax.rem(me // 8 + step[0], 4)
    x = lax.rem(lax.rem(me // 2, 4) + step[1], 4)
    return z * 8 + x * 2 + lax.rem(lax.rem(me, 2) + step[2], 2)


def second_ranges(peers, reach):
    if 2 * reach >= peers - 1:
        return [(1, peers)]
    return [(1, reach + 1), (peers - reach, peers)]


def fetch_kernel(peers, groups, reach, wanted_ref, kv_ref, cot_ref, out_ref, cots_ref, staged, sems, row_sems, own_sem):
    me, group = lax.axis_index("space"), lax.axis_index("head")
    greet(peers, groups)
    own = pltpu.make_async_copy(cot_ref, cots_ref.at[group], own_sem)
    own.start()

    def across(k):
        return copy_to(
            cot_ref, cots_ref.at[group], row_sems, k, {"head": lax.rem(group + k, groups)}
        )

    def along(c, r, peer):
        return copy_to(
            staged.at[r, c], out_ref.at[me, c], sems, c * peers + r, {"space": peer}
        )

    for k in range(1, groups):
        across(k).start()
    for i, step in enumerate(ORDER):
        peer = torus_peer(me, step)
        staged[i, 0] = kv_ref[jnp.maximum(wanted_ref[peer * SLOTS], 0)]
        along(0, i, peer).start()
    for low, high in second_ranges(peers, reach):

        @pl.loop(low, high)
        def _(r):
            peer = lax.rem(me + r, peers)
            staged[r, 1] = kv_ref[jnp.maximum(wanted_ref[peer * SLOTS + 1], 0)]
            along(1, r, peer).start()

    @pl.loop(0, len(ORDER))
    def _(i):
        along(0, i, lax.rem(me + 1, peers)).wait()

    for low, high in second_ranges(peers, reach):

        @pl.loop(low, high)
        def _(r):
            along(1, r, lax.rem(me + r, peers)).wait()

    for k in range(1, groups):
        across(k).wait()
    own.wait()


def fetch(wanted, kv, cot, peers, groups, reach, number):
    out = (peers, SLOTS) + kv.shape[1:]
    whole = pl.BlockSpec(memory_space=pl.ANY)
    return pl.pallas_call(
        functools.partial(fetch_kernel, peers, groups, reach),
        in_specs=[
            pl.BlockSpec(memory_space=pltpu.SMEM),
            pl.BlockSpec(memory_space=pltpu.VMEM),
            whole,
        ],
        out_specs=[whole, whole],
        out_shape=[
            jax.ShapeDtypeStruct(out, kv.dtype),
            jax.ShapeDtypeStruct((groups,) + cot.shape, cot.dtype),
        ],
        scratch_shapes=[
            pltpu.VMEM(out, kv.dtype),
            pltpu.SemaphoreType.DMA((2, SLOTS * peers)),
            pltpu.SemaphoreType.DMA((2, groups)),
            pltpu.SemaphoreType.DMA,
        ],
        compiler_params=pltpu.CompilerParams(
            collective_id=number, has_side_effects=True, vmem_limit_bytes=VMEM_BYTES
        ),
    )(wanted, kv, cot)


def swap_kernel(peers, groups, reach, spaces, heads, slotted, *refs):
    me, group = lax.axis_index("space"), lax.axis_index("head")
    count = spaces + heads + slotted
    sources, targets = refs[:count], refs[count : 2 * count]
    sems, head_sems, own_sems = refs[2 * count :]
    greet(peers, groups)
    owns = []
    for i in range(slotted, count):
        at = me if i < slotted + spaces else group
        owns.append(pltpu.make_async_copy(sources[i].at[at], targets[i].at[at], own_sems.at[i]))
        owns[-1].start()

    def across(i, k):
        peer = lax.rem(group + k, groups)
        return copy_to(
            sources[i].at[peer], targets[i].at[group], head_sems.at[i], k, {"head": peer}
        )

    def whole(i, r, peer):
        return copy_to(sources[i].at[peer], targets[i].at[me], sems.at[i], r, {"space": peer})

    def along(i, c, r, peer):
        src, dst = sources[i].at[peer, c], targets[i].at[me, c]
        return copy_to(src, dst, sems.at[i], c * peers + r, {"space": peer})

    for i in range(slotted + spaces, count):
        for k in range(1, groups):
            across(i, k).start()
    for r, step in enumerate(ORDER):
        peer = torus_peer(me, step)
        for i in range(slotted):
            along(i, 0, r, peer).start()
        for i in range(slotted, slotted + spaces):
            whole(i, r, peer).start()
    for i in range(slotted):
        for low, high in second_ranges(peers, reach):

            @pl.loop(low, high)
            def _(r, i=i):
                along(i, 1, r, lax.rem(me + r, peers)).start()

    beside = lax.rem(me + 1, peers)

    @pl.loop(0, len(ORDER))
    def _(r):
        for i in range(slotted):
            along(i, 0, r, beside).wait()
        for i in range(slotted, slotted + spaces):
            whole(i, r, beside).wait()

    for i in range(slotted):
        for low, high in second_ranges(peers, reach):

            @pl.loop(low, high)
            def _(r, i=i):
                along(i, 1, r, lax.rem(me + r, peers)).wait()

    for i in range(slotted + spaces, count):
        for k in range(1, groups):
            across(i, k).wait()
    for own in owns:
        own.wait()


def swap(slotted, spaces, heads, peers, groups, reach, number):
    arrays = (*slotted, *spaces, *heads)
    whole = pl.BlockSpec(memory_space=pl.ANY)
    return pl.pallas_call(
        functools.partial(
            swap_kernel, peers, groups, reach, len(spaces), len(heads), len(slotted)
        ),
        in_specs=[whole] * len(arrays),
        out_specs=[whole] * len(arrays),
        out_shape=[jax.ShapeDtypeStruct(a.shape, a.dtype) for a in arrays],
        scratch_shapes=[
            pltpu.SemaphoreType.DMA((len(arrays), 2, SLOTS * peers)),
            pltpu.SemaphoreType.DMA((len(arrays), 2, groups)),
            pltpu.SemaphoreType.DMA((len(arrays),)),
        ],
        compiler_params=pltpu.CompilerParams(collective_id=number, has_side_effects=True),
    )(*arrays)


def attention_kernel(entries_ref, q_ref, cot_ref, w_out_ref, normed_ref, *refs):
    kv_refs = refs[: AT_ONCE * NEIGHBOURS]
    att_out_ref, near_ref, far_ref, dq_ref, early_ref = refs[AT_ONCE * NEIGHBOURS : -4]
    far_total, held, grad_out, grad_q = refs[-4:]
    tile = pl.program_id(0)
    rows = q_ref.shape[0] // AT_ONCE
    last = pl.num_programs(0) - 1
    heads = q_ref.shape[1] // HEAD_DIM
    own = near_ref.shape[0]

    @pl.when(tile == 0)
    def _():
        near_ref[...] = jnp.zeros_like(near_ref)
        grad_out[...] = jnp.zeros_like(grad_out)
        grad_q[...] = jnp.zeros_like(grad_q)

        @pl.loop(0, far_total.shape[0])
        def _(i):
            far_total[i] = jnp.zeros(far_total.shape[1:], F32)

    groups = cot_ref.shape[0]
    share = cot_ref.shape[2]
    cot = jnp.concatenate([cot_ref[g] for g in range(groups)], 1)
    grad_attended = dot(cot, w_out_ref[...], ((1,), (1,))).astype(BF16)
    q = q_ref[...]
    left = lax.broadcasted_iota(jnp.int32, (128, 128), 1) < HEAD_DIM
    upper = lax.broadcasted_iota(jnp.int32, (128, 128), 0) < HEAD_DIM

    def begin(u, h):
        span = slice(u * rows, (u + 1) * rows)
        pair = jnp.concatenate([q[span, head_cut(h)], grad_attended[span, head_cut(h)]], 1)
        pair_t = pair.T
        zero = jnp.zeros_like(pair)
        stacked = jnp.concatenate([jnp.where(left, pair, zero), jnp.where(left, zero, pair)], 0)
        stacked_t = jnp.concatenate(
            [jnp.where(upper, pair_t, zero), jnp.where(upper, zero, pair_t)], 1
        )
        mine = kv_refs[u * NEIGHBOURS : (u + 1) * NEIGHBOURS]
        kv = jnp.concatenate([r[0, h] for r in mine], 0)
        return stacked_t, kv, dot(stacked, kv, ((1,), (1,)))

    mixed = []
    order = [(u, h) for u in range(AT_ONCE) for h in range(heads)]
    following = begin(*order[0])
    for at, (u, h) in enumerate(order):
        stacked_t, kv, both = following
        if at + 1 < len(order):
            following = begin(*order[at + 1])
        scores = both[:128]
        grad_prob = both[128:]
        weights = jnp.exp(scores - jnp.max(scores, axis=1, keepdims=True))
        inverse = 1.0 / jnp.sum(weights, axis=1, keepdims=True)
        row_delta = jnp.sum(weights * grad_prob, axis=1, keepdims=True) * inverse
        likely = weights * inverse
        grad_score = likely * (grad_prob - row_delta)
        factors = jnp.concatenate([grad_score.astype(BF16), likely.astype(BF16)], 0)
        mixed.append(dot(factors, kv, ((1,), (0,))))
        grad_kv_t = dot(stacked_t, factors, ((1,), (0,)))
        for j in range(NEIGHBOURS):
            held[u * NEIGHBOURS + j, h] = grad_kv_t[:, j * 128 : (j + 1) * 128]

    for u in range(AT_ONCE):

        @pl.loop(0, NEAR)
        def _(j, u=u):
            near_ref[entries_ref[tile * AT_ONCE + u, j]] += held[u * NEIGHBOURS + j]

        @pl.loop(NEAR, NEIGHBOURS)
        def _(j, u=u):
            far_total[entries_ref[tile * AT_ONCE + u, j] - own] += held[u * NEIGHBOURS + j]


    def join(parts):
        lines = [jnp.concatenate(parts[i : i + heads], 1) for i in range(0, len(parts), heads)]
        return jnp.concatenate(lines, 0)

    dq = join([m[:128, :HEAD_DIM] for m in mixed])
    dq = (dq * HEAD_DIM ** (-0.5)).astype(BF16)
    attended = join([m[128:, HEAD_DIM:] for m in mixed]).astype(BF16)
    dq_ref[...] = dq
    att_out = dot(attended, w_out_ref[...], ((1,), (0,))).astype(BF16)
    for g in range(groups):
        att_out_ref[g] = att_out[:, g * share : (g + 1) * share]
    grad_out[...] += dot(cot, attended, ((0,), (0,)))
    grad_q[...] += dot(normed_ref[...], dq, ((0,), (0,)))

    @pl.when(tile == last)
    def _():
        @pl.loop(0, far_total.shape[0])
        def _(i):
            far_ref[i] = far_total[i].astype(BF16)

        cols = grad_q.shape[1]
        early_ref[:, :cols] = grad_out[...].astype(BF16)
        early_ref[:, cols:] = grad_q[...].astype(BF16)


def attention(entries, q, cot, w_out, normed, kv, fetched):
    tiles, heads, rows, mixed = kv.shape
    slots = fetched.shape[0]
    tile_block = (1, heads, rows, mixed)
    cols = q.shape[1]
    groups, _, share = cot.shape
    width = groups * share
    lines = AT_ONCE * rows
    cot_spec = pl.BlockSpec((groups, lines, share), lambda t, e: (0, t, 0))
    whole2 = lambda t, e: (0, 0)
    row2 = lambda t, e: (t, 0)
    kv_specs = []
    for u in range(AT_ONCE):
        for j in range(NEIGHBOURS):
            shift = 0 if j < NEAR else tiles
            kv_specs.append(
                pl.BlockSpec(
                    tile_block,
                    lambda t, e, u=u, j=j, shift=shift: (e[t * AT_ONCE + u, j] - shift, 0, 0, 0),
                )
            )
    once = pl.Buffered(1)
    return pl.pallas_call(
        attention_kernel,
        grid_spec=pltpu.PrefetchScalarGridSpec(
            num_scalar_prefetch=1,
            grid=(tiles // AT_ONCE,),
            in_specs=[
                pl.BlockSpec((lines, cols), row2),
                cot_spec,
                pl.BlockSpec((cols, width), whole2),
                pl.BlockSpec((lines, width), row2),
            ]
            + kv_specs,
            out_specs=[
                cot_spec,
                pl.BlockSpec(kv.shape, lambda t, e: (0, 0, 0, 0), pipeline_mode=once),
                pl.BlockSpec(fetched.shape, lambda t, e: (0, 0, 0, 0), pipeline_mode=once),
                pl.BlockSpec((lines, cols), row2),
                pl.BlockSpec((width, 2 * cols), whole2, pipeline_mode=once),
            ],
            scratch_shapes=[
                pltpu.VMEM(fetched.shape, F32),
                pltpu.VMEM((AT_ONCE * NEIGHBOURS,) + kv.shape[1:], F32),
                pltpu.VMEM((width, cols), F32),
                pltpu.VMEM((width, cols), F32),
            ],
        ),
        out_shape=[
            jax.ShapeDtypeStruct(cot.shape, BF16),
            jax.ShapeDtypeStruct(kv.shape, F32),
            jax.ShapeDtypeStruct(fetched.shape, BF16),
            jax.ShapeDtypeStruct((tiles * rows, cols), BF16),
            jax.ShapeDtypeStruct((width, 2 * cols), BF16),
        ],
        compiler_params=pltpu.CompilerParams(vmem_limit_bytes=50 * 2**20),
    )(entries, q, cot, w_out, normed, *(([kv] * NEAR + [fetched] * (NEIGHBOURS - NEAR)) * AT_ONCE))


def place_kernel(wanted_ref, near_ref, back_ref, grad_kv_ref, total):
    step = pl.program_id(0)
    count = back_ref.shape[0]

    @pl.when(step == 0)
    def _():
        total[...] = near_ref[...]

    for i in range(count):
        tile = wanted_ref[step * count + i]

        @pl.when(tile >= 0)
        def _():
            total[tile] += back_ref[i].astype(F32)

    @pl.when(step == pl.num_programs(0) - 1)
    def _():
        grad_kv_ref[...] = total[...].astype(BF16)


def place(wanted, near, back):
    slots = back.shape[0]
    step = 8
    whole = lambda i, w: (0, 0, 0, 0)
    return pl.pallas_call(
        place_kernel,
        grid_spec=pltpu.PrefetchScalarGridSpec(
            num_scalar_prefetch=1,
            grid=(slots // step,),
            in_specs=[
                pl.BlockSpec(near.shape, whole),
                pl.BlockSpec((step,) + back.shape[1:], lambda i, w: (i, 0, 0, 0)),
            ],
            out_specs=pl.BlockSpec(near.shape, whole),
            scratch_shapes=[pltpu.VMEM(near.shape, F32)],
        ),
        out_shape=jax.ShapeDtypeStruct(near.shape, BF16),
        compiler_params=pltpu.CompilerParams(vmem_limit_bytes=VMEM_BYTES),
    )(wanted, near, back)


def finish_kernel(heads, tokens_ref, dq_ref, grad_kv_ref, w_ref, part_ref, sums_ref, grad_w_ref, total):
    step = pl.program_id(0)

    @pl.when(step == 0)
    def _():
        total[...] = jnp.zeros_like(total)

    standard, _, _ = norm_rows(tokens_ref[...])
    pairs = [
        jnp.concatenate([grad_kv_ref[t, h].T for t in range(grad_kv_ref.shape[0])], 0)
        for h in range(heads)
    ]
    dk = jnp.concatenate([p[:, :HEAD_DIM] for p in pairs], 1)
    dv = jnp.concatenate([p[:, HEAD_DIM:] for p in pairs], 1)
    total[...] += dot(standard.astype(BF16), jnp.concatenate([dk, dv], 1), ((0,), (0,)))
    part = dot(dq_ref[...], w_ref[0], ((1,), (1,)))
    part += dot(dk, w_ref[1], ((1,), (1,)))
    part += dot(dv, w_ref[2], ((1,), (1,)))
    sums = [jnp.sum(part, 1, keepdims=True), jnp.sum(part * standard, 1, keepdims=True)]
    sums_ref[...] = jnp.concatenate(sums, 1).T
    share = part_ref.shape[2]
    for g in range(part_ref.shape[0]):
        part_ref[g] = part[:, g * share : (g + 1) * share].astype(BF16)

    @pl.when(step == pl.num_programs(0) - 1)
    def _():
        grad_w_ref[...] = total[...].astype(BF16)


def finish(tokens, dq, grad_kv, w3, groups):
    rows, width = tokens.shape
    cols = dq.shape[1]
    step = 256
    row2 = lambda i: (i, 0)
    return pl.pallas_call(
        functools.partial(finish_kernel, cols // HEAD_DIM),
        grid=(rows // step,),
        in_specs=[
            pl.BlockSpec((step, width), row2),
            pl.BlockSpec((step, cols), row2),
            pl.BlockSpec((step // grad_kv.shape[2],) + grad_kv.shape[1:], lambda i: (i, 0, 0, 0)),
            pl.BlockSpec((3, width, cols), lambda i: (0, 0, 0)),
        ],
        out_specs=[
            pl.BlockSpec((groups, step, width // groups), lambda i: (0, i, 0)),
            pl.BlockSpec((2, step), lambda i: (0, i)),
            pl.BlockSpec((width, 2 * cols), lambda i: (0, 0)),
        ],
        out_shape=[
            jax.ShapeDtypeStruct((groups, rows, width // groups), BF16),
            jax.ShapeDtypeStruct((2, rows), F32),
            jax.ShapeDtypeStruct((width, 2 * cols), BF16),
        ],
        scratch_shapes=[pltpu.VMEM((width, 2 * cols), F32)],
        compiler_params=pltpu.CompilerParams(vmem_limit_bytes=VMEM_BYTES),
    )(tokens, dq, grad_kv, w3)


def on_device(tokens, w_qkv, w_out, neighbours, requests, cotangent):
    row_count, width = tokens.shape
    tiles = neighbours.shape[0]
    rows = row_count // tiles
    cols = w_qkv.shape[2]
    peers, groups = lax.axis_size("space"), lax.axis_size("head")
    share = cotangent.shape[1]
    me = lax.axis_index("space")
    column = lax.axis_index("head") * share
    w3 = jnp.transpose(w_qkv, (1, 0, 2))

    copies = jnp.broadcast_to(requests, (peers,) + requests.shape[1:])
    table = lax.all_to_all(copies, "space", split_axis=0, concat_axis=0, tiled=True)
    wanted = lax.dynamic_index_in_dim(table, me, 1, keepdims=False).reshape(-1)
    apart = jnp.abs(jnp.arange(peers)[:, None] - jnp.arange(peers)[None, :])
    apart = jnp.minimum(apart, peers - apart)
    reach = jnp.max(jnp.where(jnp.any(table[:, :, 1:] >= 0, axis=2), apart, 0))
    level = (reach > REACHES[0]).astype(jnp.int32) + (reach > REACHES[1]).astype(jnp.int32)
    reaches = (*REACHES, peers)

    normed, q, kv, mean, inverse = project(tokens, w3, rows)
    fetched, cots = lax.switch(
        level,
        [
            functools.partial(fetch, peers=peers, groups=groups, reach=r, number=n)
            for n, r in enumerate(reaches)
        ],
        wanted,
        kv,
        cotangent,
    )
    attended, near, far, dq, early = attention(
        neighbours, q, cots, w_out, normed, kv, fetched.reshape((-1,) + kv.shape[1:])
    )

    def give_back(far, early, attended, reach, number):
        return swap((far,), (early,), (attended,), peers, groups, reach, number)

    back, early, attended = lax.switch(
        level,
        [
            functools.partial(give_back, reach=r, number=n + len(reaches))
            for n, r in enumerate(reaches)
        ],
        far.reshape(fetched.shape),
        early.reshape(peers, width // peers, 2 * cols),
        attended,
    )
    grad_kv = place(wanted, near, back.reshape(far.shape))
    part, sums, late = finish(tokens, dq, grad_kv, w3, groups)
    sums = jnp.broadcast_to(sums, (groups,) + sums.shape)
    late = late.reshape(peers, width // peers, 2 * cols)
    late, part, sums = swap((), (late,), (part, sums), peers, groups, peers, 2 * len(reaches))

    own_tokens = lax.dynamic_slice_in_dim(tokens, column, share, 1).astype(F32)
    layer_out = (own_tokens + jnp.sum(attended.astype(F32), 0)).astype(BF16)
    own_standard = (own_tokens - mean) * inverse
    own_part = jnp.sum(part.astype(F32), 0)
    means = (jnp.sum(sums, 0) / width)[:, :, None]
    grad_tokens = (
        cotangent.astype(F32) + inverse * (own_part - means[0] - own_standard * means[1])
    ).astype(BF16)
    early = jnp.sum(early.astype(F32), 0)
    late = jnp.sum(late.astype(F32), 0)
    grad_w_qkv = jnp.concatenate([early[:, cols:], late], 1).reshape(-1, 3, cols)
    grad_w_out = early[:, :cols].T
    return (layer_out, grad_tokens, grad_w_qkv, grad_w_out)


def solution(mesh):
    placed = (
        P("space", None),
        P(None, None, "head"),
        P("head", None),
        P("space", None),
        P("space", None, None),
        P("space", "head"),
    )
    return jax.shard_map(
        on_device,
        mesh=mesh,
        in_specs=placed,
        out_specs=(
            P("space", "head"),
            P("space", "head"),
            P("space", None, "head"),
            P("head", "space"),
        ),
        check_vma=False,
    )
```

```python
import functools

import jax
import jax.numpy as jnp
from jax import lax
from jax.experimental import pallas as pl
from jax.experimental.pallas import tpu as pltpu
from jax.sharding import PartitionSpec as P

HEAD_DIM = 64
NEIGHBOURS = 9
NEAR = 4
REACHES = (1, 4)
AT_ONCE = 2
SLOTS = 2
EPSILON = 1e-05
F32 = jnp.float32
BF16 = jnp.bfloat16
VMEM_BYTES = 60 * 2**20


def dot(a, b, dims):
    return lax.dot_general(a, b, (dims, ((), ())), preferred_element_type=F32)


def norm_rows(tokens):
    values = tokens.astype(F32)
    mean = jnp.mean(values, axis=1, keepdims=True)
    centred = values - mean
    inverse = lax.rsqrt(jnp.mean(centred * centred, axis=1, keepdims=True) + EPSILON)
    return centred * inverse, mean, inverse


def head_cut(h):
    return slice(h * HEAD_DIM, (h + 1) * HEAD_DIM)


def project_kernel(heads, tokens_ref, w_ref, normed_ref, q_ref, kv_ref, stats_ref):
    standard, mean, inverse = norm_rows(tokens_ref[...])
    normed = standard.astype(BF16)
    normed_ref[...] = normed
    stats_ref[...] = jnp.concatenate([mean, inverse], 1).T
    q = dot(normed, w_ref[0], ((1,), (0,))).astype(BF16)
    q_ref[...] = (q.astype(F32) * HEAD_DIM ** (-0.5)).astype(BF16)
    k = dot(normed, w_ref[1], ((1,), (0,))).astype(BF16)
    v = dot(normed, w_ref[2], ((1,), (0,))).astype(BF16)
    for h in range(heads):
        pair = jnp.concatenate([k[:, head_cut(h)], v[:, head_cut(h)]], 1)
        kv_ref[:, h] = pair.reshape(kv_ref.shape[0], kv_ref.shape[2], 2 * HEAD_DIM)


def project(tokens, w3, tile_rows):
    rows, width = tokens.shape
    cols = w3.shape[2]
    step = 256
    kv_block = (step // tile_rows, cols // HEAD_DIM, tile_rows, 2 * HEAD_DIM)
    return pl.pallas_call(
        functools.partial(project_kernel, cols // HEAD_DIM),
        grid=(rows // step,),
        in_specs=[
            pl.BlockSpec((step, width), lambda i: (i, 0)),
            pl.BlockSpec((3, width, cols), lambda i: (0, 0, 0)),
        ],
        out_specs=[
            pl.BlockSpec((step, width), lambda i: (i, 0)),
            pl.BlockSpec((step, cols), lambda i: (i, 0)),
            pl.BlockSpec(kv_block, lambda i: (i, 0, 0, 0)),
            pl.BlockSpec((2, step), lambda i: (0, i)),
        ],
        out_shape=[
            jax.ShapeDtypeStruct((rows, width), BF16),
            jax.ShapeDtypeStruct((rows, cols), BF16),
            jax.ShapeDtypeStruct((rows // tile_rows,) + kv_block[1:], BF16),
            jax.ShapeDtypeStruct((2, rows), F32),
        ],
        compiler_params=pltpu.CompilerParams(vmem_limit_bytes=VMEM_BYTES),
    )(tokens, w3)


def copy_to(src, dst, sems, index, device):
    return pltpu.make_async_remote_copy(
        src_ref=src,
        dst_ref=dst,
        send_sem=sems.at[0, index],
        recv_sem=sems.at[1, index],
        device_id=device,
        device_id_type=pl.DeviceIdType.MESH,
    )


def greet(peers, groups):
    signal_all(peers, groups)
    pl.semaphore_wait(pltpu.get_barrier_semaphore(), peers + groups - 2)


def signal_all(peers, groups):
    barrier = pltpu.get_barrier_semaphore()
    me, group = lax.axis_index("space"), lax.axis_index("head")

    @pl.loop(1, peers)
    def _(r):
        pl.semaphore_signal(
            barrier,
            inc=1,
            device_id={"space": lax.rem(me + r, peers)},
            device_id_type=pl.DeviceIdType.MESH,
        )

    for k in range(1, groups):
        pl.semaphore_signal(
            barrier,
            inc=1,
            device_id={"head": lax.rem(group + k, groups)},
            device_id_type=pl.DeviceIdType.MESH,
        )


def torus_order():
    near = [(0, 1), (0, 3), (1, 0), (3, 0), (1, 1), (3, 3), (1, 3), (3, 1)]
    far = [(0, 2), (2, 0), (1, 2), (2, 1), (3, 2), (2, 3), (2, 2)]
    order = [(0, 0, 1)]
    for group in (near[:4], near[4:], far[:2], far[2:6], far[6:]):
        order += [(z, x, core) for core in (0, 1) for z, x in group]
    return order


ORDER = torus_order()


def torus_peer(me, step):
    z = lax.rem(me // 8 + step[0], 4)
    x = lax.rem(lax.rem(me // 2, 4) + step[1], 4)
    return z * 8 + x * 2 + lax.rem(lax.rem(me, 2) + step[2], 2)


def second_ranges(peers, reach):
    if 2 * reach >= peers - 1:
        return [(1, peers)]
    return [(1, reach + 1), (peers - reach, peers)]


def fetch_kernel(peers, groups, reach, wanted_ref, kv_ref, cot_ref, out_ref, cots_ref, staged, sems, row_sems, own_sem):
    me, group = lax.axis_index("space"), lax.axis_index("head")
    greet(peers, groups)
    own = pltpu.make_async_copy(cot_ref, cots_ref.at[group], own_sem)
    own.start()

    def across(k):
        return copy_to(
            cot_ref, cots_ref.at[group], row_sems, k, {"head": lax.rem(group + k, groups)}
        )

    def along(c, r, peer):
        return copy_to(
            staged.at[r, c], out_ref.at[me, c], sems, c * peers + r, {"space": peer}
        )

    for k in range(1, groups):
        across(k).start()
    for i, step in enumerate(ORDER):
        peer = torus_peer(me, step)
        staged[i, 0] = kv_ref[jnp.maximum(wanted_ref[peer * SLOTS], 0)]
        along(0, i, peer).start()
    for low, high in second_ranges(peers, reach):

        @pl.loop(low, high)
        def _(r):
            peer = lax.rem(me + r, peers)
            staged[r, 1] = kv_ref[jnp.maximum(wanted_ref[peer * SLOTS + 1], 0)]
            along(1, r, peer).start()

    @pl.loop(0, len(ORDER))
    def _(i):
        along(0, i, lax.rem(me + 1, peers)).wait()

    for low, high in second_ranges(peers, reach):

        @pl.loop(low, high)
        def _(r):
            along(1, r, lax.rem(me + r, peers)).wait()

    for k in range(1, groups):
        across(k).wait()
    own.wait()


def fetch(wanted, kv, cot, peers, groups, reach, number):
    out = (peers, SLOTS) + kv.shape[1:]
    whole = pl.BlockSpec(memory_space=pl.ANY)
    return pl.pallas_call(
        functools.partial(fetch_kernel, peers, groups, reach),
        in_specs=[
            pl.BlockSpec(memory_space=pltpu.SMEM),
            pl.BlockSpec(memory_space=pltpu.VMEM),
            whole,
        ],
        out_specs=[whole, whole],
        out_shape=[
            jax.ShapeDtypeStruct(out, kv.dtype),
            jax.ShapeDtypeStruct((groups,) + cot.shape, cot.dtype),
        ],
        scratch_shapes=[
            pltpu.VMEM(out, kv.dtype),
            pltpu.SemaphoreType.DMA((2, SLOTS * peers)),
            pltpu.SemaphoreType.DMA((2, groups)),
            pltpu.SemaphoreType.DMA,
        ],
        compiler_params=pltpu.CompilerParams(
            collective_id=number, has_side_effects=True, vmem_limit_bytes=VMEM_BYTES
        ),
    )(wanted, kv, cot)


def return_kernel(peers, groups, reach, wanted_ref, near_ref, far_ref, att_ref, grad_kv_ref, atts_ref, total, landed, sems, row_sems, own_sem):
    me, group = lax.axis_index("space"), lax.axis_index("head")
    greet(peers, groups)
    own = pltpu.make_async_copy(att_ref.at[group], atts_ref.at[group], own_sem)
    own.start()

    def across(k):
        peer = lax.rem(group + k, groups)
        return copy_to(att_ref.at[peer], atts_ref.at[group], row_sems, k, {"head": peer})

    def along(c, r, peer):
        return copy_to(
            far_ref.at[peer, c], landed.at[r, c], sems, c * peers + r, {"space": peer}
        )

    for i, step in enumerate(ORDER):
        along(0, i, torus_peer(me, step)).start()
    for low, high in second_ranges(peers, reach):

        @pl.loop(low, high)
        def _(r):
            along(1, r, lax.rem(me + r, peers)).start()

    for k in range(1, groups):
        across(k).start()
    total[...] = near_ref[...]

    def add(c, r, source):
        tile = wanted_ref[source * SLOTS + c]
        block = landed[r, c].astype(F32)

        @pl.loop(0, total.shape[0])
        def _(t):
            total[t] += block * jnp.where(tile == t, 1.0, 0.0)

    for i, step in enumerate(ORDER):
        along(0, i, torus_peer(me, step)).wait()
        add(0, i, torus_peer(me, ((4 - step[0]) % 4, (4 - step[1]) % 4, step[2])))
    for low, high in second_ranges(peers, reach):

        @pl.loop(low, high)
        def _(r):
            along(1, r, lax.rem(me + r, peers)).wait()
            add(1, r, lax.rem(me + peers - r, peers))

    grad_kv_ref[...] = total[...].astype(BF16)
    for k in range(1, groups):
        across(k).wait()
    own.wait()


def give_back(wanted, near, far, att, peers, groups, reach, number):
    whole = pl.BlockSpec(memory_space=pl.ANY)
    vmem = pl.BlockSpec(memory_space=pltpu.VMEM)
    return pl.pallas_call(
        functools.partial(return_kernel, peers, groups, reach),
        in_specs=[pl.BlockSpec(memory_space=pltpu.SMEM), vmem, whole, whole],
        out_specs=[vmem, whole],
        out_shape=[
            jax.ShapeDtypeStruct(near.shape, BF16),
            jax.ShapeDtypeStruct(att.shape, att.dtype),
        ],
        scratch_shapes=[
            pltpu.VMEM(near.shape, F32),
            pltpu.VMEM(far.shape, BF16),
            pltpu.SemaphoreType.DMA((2, SLOTS * peers)),
            pltpu.SemaphoreType.DMA((2, groups)),
            pltpu.SemaphoreType.DMA,
        ],
        compiler_params=pltpu.CompilerParams(
            collective_id=number, has_side_effects=True, vmem_limit_bytes=40 * 2**20
        ),
    )(wanted, near, far, att)


def attention_kernel(entries_ref, q_ref, cot_ref, w_out_ref, normed_ref, *refs):
    kv_refs = refs[: AT_ONCE * NEIGHBOURS]
    att_out_ref, near_ref, far_ref, dq_ref, early_ref = refs[AT_ONCE * NEIGHBOURS : -4]
    far_total, held, grad_out, grad_q = refs[-4:]
    tile = pl.program_id(0)
    rows = q_ref.shape[0] // AT_ONCE
    last = pl.num_programs(0) - 1
    heads = q_ref.shape[1] // HEAD_DIM
    own = near_ref.shape[0]

    @pl.when(tile == 0)
    def _():
        near_ref[...] = jnp.zeros_like(near_ref)
        grad_out[...] = jnp.zeros_like(grad_out)
        grad_q[...] = jnp.zeros_like(grad_q)

        @pl.loop(0, far_total.shape[0])
        def _(i):
            far_total[i] = jnp.zeros(far_total.shape[1:], F32)

    groups = cot_ref.shape[0]
    share = cot_ref.shape[2]
    cot = jnp.concatenate([cot_ref[g] for g in range(groups)], 1)
    grad_attended = dot(cot, w_out_ref[...], ((1,), (1,))).astype(BF16)
    q = q_ref[...]
    left = lax.broadcasted_iota(jnp.int32, (128, 128), 1) < HEAD_DIM
    upper = lax.broadcasted_iota(jnp.int32, (128, 128), 0) < HEAD_DIM

    def begin(u, h):
        span = slice(u * rows, (u + 1) * rows)
        pair = jnp.concatenate([q[span, head_cut(h)], grad_attended[span, head_cut(h)]], 1)
        pair_t = pair.T
        zero = jnp.zeros_like(pair)
        stacked = jnp.concatenate([jnp.where(left, pair, zero), jnp.where(left, zero, pair)], 0)
        stacked_t = jnp.concatenate(
            [jnp.where(upper, pair_t, zero), jnp.where(upper, zero, pair_t)], 1
        )
        mine = kv_refs[u * NEIGHBOURS : (u + 1) * NEIGHBOURS]
        kv = jnp.concatenate([r[0, h] for r in mine], 0)
        return stacked_t, kv, dot(stacked, kv, ((1,), (1,)))

    mixed = []
    order = [(u, h) for u in range(AT_ONCE) for h in range(heads)]
    following = begin(*order[0])
    for at, (u, h) in enumerate(order):
        stacked_t, kv, both = following
        if at + 1 < len(order):
            following = begin(*order[at + 1])
        scores = both[:128]
        grad_prob = both[128:]
        weights = jnp.exp(scores - jnp.max(scores, axis=1, keepdims=True))
        inverse = 1.0 / jnp.sum(weights, axis=1, keepdims=True)
        row_delta = jnp.sum(weights * grad_prob, axis=1, keepdims=True) * inverse
        likely = weights * inverse
        grad_score = likely * (grad_prob - row_delta)
        factors = jnp.concatenate([grad_score.astype(BF16), likely.astype(BF16)], 0)
        mixed.append(dot(factors, kv, ((1,), (0,))))
        grad_kv_t = dot(stacked_t, factors, ((1,), (0,)))
        for j in range(NEIGHBOURS):
            held[u * NEIGHBOURS + j, h] = grad_kv_t[:, j * 128 : (j + 1) * 128]

    for u in range(AT_ONCE):

        @pl.loop(0, NEAR)
        def _(j, u=u):
            near_ref[entries_ref[tile * AT_ONCE + u, j]] += held[u * NEIGHBOURS + j]

        @pl.loop(NEAR, NEIGHBOURS)
        def _(j, u=u):
            far_total[entries_ref[tile * AT_ONCE + u, j] - own] += held[u * NEIGHBOURS + j]


    def join(parts):
        lines = [jnp.concatenate(parts[i : i + heads], 1) for i in range(0, len(parts), heads)]
        return jnp.concatenate(lines, 0)

    dq = join([m[:128, :HEAD_DIM] for m in mixed])
    dq = (dq * HEAD_DIM ** (-0.5)).astype(BF16)
    attended = join([m[128:, HEAD_DIM:] for m in mixed]).astype(BF16)
    dq_ref[...] = dq
    att_out = dot(attended, w_out_ref[...], ((1,), (0,))).astype(BF16)
    for g in range(groups):
        att_out_ref[g] = att_out[:, g * share : (g + 1) * share]
    grad_out[...] += dot(cot, attended, ((0,), (0,)))
    grad_q[...] += dot(normed_ref[...], dq, ((0,), (0,)))

    @pl.when(tile == last)
    def _():
        @pl.loop(0, far_total.shape[0])
        def _(i):
            far_ref[i] = far_total[i].astype(BF16)

        cols = grad_q.shape[1]
        early_ref[:, :cols] = grad_out[...].astype(BF16)
        early_ref[:, cols:] = grad_q[...].astype(BF16)


def attention(entries, q, cot, w_out, normed, kv, fetched):
    tiles, heads, rows, mixed = kv.shape
    slots = fetched.shape[0]
    tile_block = (1, heads, rows, mixed)
    cols = q.shape[1]
    groups, _, share = cot.shape
    width = groups * share
    lines = AT_ONCE * rows
    cot_spec = pl.BlockSpec((groups, lines, share), lambda t, e: (0, t, 0))
    whole2 = lambda t, e: (0, 0)
    row2 = lambda t, e: (t, 0)
    kv_specs = []
    for u in range(AT_ONCE):
        for j in range(NEIGHBOURS):
            shift = 0 if j < NEAR else tiles
            kv_specs.append(
                pl.BlockSpec(
                    tile_block,
                    lambda t, e, u=u, j=j, shift=shift: (e[t * AT_ONCE + u, j] - shift, 0, 0, 0),
                )
            )
    once = pl.Buffered(1)
    return pl.pallas_call(
        attention_kernel,
        grid_spec=pltpu.PrefetchScalarGridSpec(
            num_scalar_prefetch=1,
            grid=(tiles // AT_ONCE,),
            in_specs=[
                pl.BlockSpec((lines, cols), row2),
                cot_spec,
                pl.BlockSpec((cols, width), whole2),
                pl.BlockSpec((lines, width), row2),
            ]
            + kv_specs,
            out_specs=[
                cot_spec,
                pl.BlockSpec(kv.shape, lambda t, e: (0, 0, 0, 0), pipeline_mode=once),
                pl.BlockSpec(fetched.shape, lambda t, e: (0, 0, 0, 0), pipeline_mode=once),
                pl.BlockSpec((lines, cols), row2),
                pl.BlockSpec((width, 2 * cols), whole2, pipeline_mode=once),
            ],
            scratch_shapes=[
                pltpu.VMEM(fetched.shape, F32),
                pltpu.VMEM((AT_ONCE * NEIGHBOURS,) + kv.shape[1:], F32),
                pltpu.VMEM((width, cols), F32),
                pltpu.VMEM((width, cols), F32),
            ],
        ),
        out_shape=[
            jax.ShapeDtypeStruct(cot.shape, BF16),
            jax.ShapeDtypeStruct(kv.shape, F32),
            jax.ShapeDtypeStruct(fetched.shape, BF16),
            jax.ShapeDtypeStruct((tiles * rows, cols), BF16),
            jax.ShapeDtypeStruct((width, 2 * cols), BF16),
        ],
        compiler_params=pltpu.CompilerParams(vmem_limit_bytes=50 * 2**20),
    )(entries, q, cot, w_out, normed, *(([kv] * NEAR + [fetched] * (NEIGHBOURS - NEAR)) * AT_ONCE))


def finish_kernel(peers, groups, tokens_ref, dq_ref, grad_kv_ref, w_ref, early_ref, earlies_ref, lates_ref, parts_ref, sums_ref, grads, normed, part, late, sums, stats, sems, row_sems, own_sems):
    me, group = lax.axis_index("space"), lax.axis_index("head")
    signal_all(peers, groups)
    rows, width = tokens_ref.shape
    cols = dq_ref.shape[1]
    share = width // groups
    tiles, heads = grad_kv_ref.shape[:2]
    span = rows // tiles
    step = 256

    @pl.loop(0, rows // step)
    def _(i):
        at = pl.ds(pl.multiple_of(i * step, step), step)
        standard, mean, inverse = norm_rows(tokens_ref[at, :])
        normed[at, :] = standard.astype(BF16)
        stats[0, at, :] = jnp.broadcast_to(mean, (step, 128))
        stats[1, at, :] = jnp.broadcast_to(inverse, (step, 128))
        grads[at, :cols] = dq_ref[at, :]

    for t in range(tiles):
        pairs = [grad_kv_ref[t, h].T for h in range(heads)]
        at = slice(t * span, (t + 1) * span)
        grads[at, cols : 2 * cols] = jnp.concatenate([p[:, :HEAD_DIM] for p in pairs], 1)
        grads[at, 2 * cols :] = jnp.concatenate([p[:, HEAD_DIM:] for p in pairs], 1)

    def chunk(k):
        at_cols = pl.ds(pl.multiple_of(lax.rem(group + k, groups) * share, share), share)

        @pl.loop(0, rows // step)
        def _(i):
            at = pl.ds(pl.multiple_of(i * step, step), step)
            piece = dot(grads[at, :cols], w_ref[0, at_cols, :], ((1,), (1,)))
            for n in (1, 2):
                lanes = slice(n * cols, (n + 1) * cols)
                piece += dot(grads[at, lanes], w_ref[n, at_cols, :], ((1,), (1,)))
            part[k, at, :] = piece.astype(BF16)
            values = tokens_ref[at, at_cols].astype(F32)
            standard = (values - stats[0, at, :1]) * stats[1, at, :1]
            found = [
                jnp.sum(piece, 1, keepdims=True),
                jnp.sum(piece * standard, 1, keepdims=True),
            ]
            found = jnp.concatenate(found, 1).T
            if k == 0:
                sums[:, at] = found
            else:
                sums[:, at] += found

    def across(k):
        return copy_to(
            part.at[k], parts_ref.at[group], row_sems, k, {"head": lax.rem(group + k, groups)}
        )

    def across_sums(k):
        return copy_to(
            sums, sums_ref.at[group], row_sems, groups + k, {"head": lax.rem(group + k, groups)}
        )

    def along(kind, r, peer):
        source, target = ((early_ref, earlies_ref), (late, lates_ref))[kind]
        return copy_to(
            source.at[peer], target.at[me], sems, kind * peers + r, {"space": peer}
        )

    owns = [
        pltpu.make_async_copy(early_ref.at[me], earlies_ref.at[me], own_sems.at[0]),
        pltpu.make_async_copy(late.at[me], lates_ref.at[me], own_sems.at[1]),
        pltpu.make_async_copy(part.at[0], parts_ref.at[group], own_sems.at[2]),
        pltpu.make_async_copy(sums, sums_ref.at[group], own_sems.at[3]),
    ]
    owns[0].start()
    chunk(0)
    owns[2].start()
    pl.semaphore_wait(pltpu.get_barrier_semaphore(), peers + groups - 2)
    for r, torus in enumerate(ORDER):
        along(0, r, torus_peer(me, torus)).start()
    for k in (2, 1, 3):
        chunk(k)
        across(k).start()
    owns[3].start()
    for k in range(1, groups):
        across_sums(k).start()

    piece = width // 4
    for i in range(4):
        made = dot(normed[:, i * piece : (i + 1) * piece], grads[:, cols:], ((0,), (0,)))
        late[i * peers // 4 : (i + 1) * peers // 4] = made.astype(BF16).reshape(
            peers // 4, width // peers, 2 * cols
        )
    owns[1].start()
    for r, torus in enumerate(ORDER):
        along(1, r, torus_peer(me, torus)).start()

    @pl.loop(0, len(ORDER))
    def _(r):
        along(0, r, lax.rem(me + 1, peers)).wait()
        along(1, r, lax.rem(me + 1, peers)).wait()

    for k in range(1, groups):
        across(k).wait()
        across_sums(k).wait()
    for own in owns:
        own.wait()


def finish(tokens, dq, grad_kv, w3, early, peers, groups, number):
    rows, width = tokens.shape
    cols = dq.shape[1]
    whole = pl.BlockSpec(memory_space=pl.ANY)
    vmem = pl.BlockSpec(memory_space=pltpu.VMEM)
    part = (groups, rows, width // groups)
    return pl.pallas_call(
        functools.partial(finish_kernel, peers, groups),
        in_specs=[vmem] * 4 + [whole],
        out_specs=[whole] * 4,
        out_shape=[
            jax.ShapeDtypeStruct(early.shape, BF16),
            jax.ShapeDtypeStruct(early.shape, BF16),
            jax.ShapeDtypeStruct(part, BF16),
            jax.ShapeDtypeStruct((groups, 2, rows), F32),
        ],
        scratch_shapes=[
            pltpu.VMEM((rows, 3 * cols), BF16),
            pltpu.VMEM((rows, width), BF16),
            pltpu.VMEM(part, BF16),
            pltpu.VMEM(early.shape, BF16),
            pltpu.VMEM((2, rows), F32),
            pltpu.VMEM((2, rows, 128), F32),
            pltpu.SemaphoreType.DMA((2, 2 * peers)),
            pltpu.SemaphoreType.DMA((2, 2 * groups)),
            pltpu.SemaphoreType.DMA((4,)),
        ],
        compiler_params=pltpu.CompilerParams(
            collective_id=number, has_side_effects=True, vmem_limit_bytes=40 * 2**20
        ),
    )(tokens, dq, grad_kv, w3, early)


def on_device(tokens, w_qkv, w_out, neighbours, requests, cotangent):
    row_count, width = tokens.shape
    tiles = neighbours.shape[0]
    rows = row_count // tiles
    cols = w_qkv.shape[2]
    peers, groups = lax.axis_size("space"), lax.axis_size("head")
    share = cotangent.shape[1]
    me = lax.axis_index("space")
    column = lax.axis_index("head") * share
    w3 = jnp.transpose(w_qkv, (1, 0, 2))

    copies = jnp.broadcast_to(requests, (peers,) + requests.shape[1:])
    table = lax.all_to_all(copies, "space", split_axis=0, concat_axis=0, tiled=True)
    wanted = lax.dynamic_index_in_dim(table, me, 1, keepdims=False).reshape(-1)
    apart = jnp.abs(jnp.arange(peers)[:, None] - jnp.arange(peers)[None, :])
    apart = jnp.minimum(apart, peers - apart)
    reach = jnp.max(jnp.where(jnp.any(table[:, :, 1:] >= 0, axis=2), apart, 0))
    level = (reach > REACHES[0]).astype(jnp.int32) + (reach > REACHES[1]).astype(jnp.int32)
    reaches = (*REACHES, peers)

    normed, q, kv, stats = project(tokens, w3, rows)
    fetched, cots = lax.switch(
        level,
        [
            functools.partial(fetch, peers=peers, groups=groups, reach=r, number=n)
            for n, r in enumerate(reaches)
        ],
        wanted,
        kv,
        cotangent,
    )
    attended, near, far, dq, early = attention(
        neighbours, q, cots, w_out, normed, kv, fetched.reshape((-1,) + kv.shape[1:])
    )

    grad_kv, attended = lax.switch(
        level,
        [
            functools.partial(
                give_back, peers=peers, groups=groups, reach=r, number=n + len(reaches)
            )
            for n, r in enumerate(reaches)
        ],
        wanted,
        near,
        far.reshape(fetched.shape),
        attended,
    )
    early = early.reshape(peers, width // peers, 2 * cols)
    early, late, part, sums = finish(
        tokens, dq, grad_kv, w3, early, peers, groups, 2 * len(reaches)
    )

    own_tokens = lax.dynamic_slice_in_dim(tokens, column, share, 1).astype(F32)
    layer_out = (own_tokens + jnp.sum(attended.astype(F32), 0)).astype(BF16)
    mean, inverse = stats[0][:, None], stats[1][:, None]
    own_standard = (own_tokens - mean) * inverse
    own_part = jnp.sum(part.astype(F32), 0)
    means = (jnp.sum(sums, 0) / width)[:, :, None]
    grad_tokens = (
        cotangent.astype(F32) + inverse * (own_part - means[0] - own_standard * means[1])
    ).astype(BF16)
    early = jnp.sum(early.astype(F32), 0)
    late = jnp.sum(late.astype(F32), 0)
    grad_w_qkv = jnp.concatenate([early[:, cols:], late], 1).reshape(-1, 3, cols)
    grad_w_out = early[:, :cols].T
    return (layer_out, grad_tokens, grad_w_qkv, grad_w_out)


def solution(mesh):
    placed = (
        P("space", None),
        P(None, None, "head"),
        P("head", None),
        P("space", None),
        P("space", None, None),
        P("space", "head"),
    )
    return jax.shard_map(
        on_device,
        mesh=mesh,
        in_specs=placed,
        out_specs=(
            P("space", "head"),
            P("space", "head"),
            P("space", None, "head"),
            P("head", "space"),
        ),
        check_vma=False,
    )
```

```python
import functools

import jax
import jax.numpy as jnp
from jax import lax
from jax.experimental import pallas as pl
from jax.experimental.pallas import tpu as pltpu
from jax.sharding import PartitionSpec as P

HEAD_DIM = 64
NEIGHBOURS = 9
NEAR = 4
REACHES = (1, 4)
AT_ONCE = 2
SLOTS = 2
EPSILON = 1e-05
F32 = jnp.float32
BF16 = jnp.bfloat16
VMEM_BYTES = 60 * 2**20


def dot(a, b, dims):
    return lax.dot_general(a, b, (dims, ((), ())), preferred_element_type=F32)


def norm_rows(tokens):
    values = tokens.astype(F32)
    mean = jnp.mean(values, axis=1, keepdims=True)
    centred = values - mean
    inverse = lax.rsqrt(jnp.mean(centred * centred, axis=1, keepdims=True) + EPSILON)
    return centred * inverse, mean, inverse


def head_cut(h):
    return slice(h * HEAD_DIM, (h + 1) * HEAD_DIM)


def project_kernel(peers, groups, tokens_ref, w_ref, requests_ref, normed_ref, q_ref, kv_ref, stats_ref, table_ref, sems, own_sem):
    me = lax.axis_index("space")
    step = pl.program_id(0)
    heads = kv_ref.shape[1]
    own = pltpu.make_async_copy(requests_ref, table_ref.at[me], own_sem)

    def along(r, peer):
        return copy_to(requests_ref, table_ref.at[me], sems, r, {"space": peer})

    @pl.when(step == 0)
    def _():
        own.start()
        signal_all(peers, groups)

    standard, mean, inverse = norm_rows(tokens_ref[...])
    normed = standard.astype(BF16)
    normed_ref[...] = normed
    stats_ref[...] = jnp.concatenate([mean, inverse], 1).T
    q = dot(normed, w_ref[0], ((1,), (0,))).astype(BF16)
    q_ref[...] = (q.astype(F32) * HEAD_DIM ** (-0.5)).astype(BF16)
    k = dot(normed, w_ref[1], ((1,), (0,))).astype(BF16)
    v = dot(normed, w_ref[2], ((1,), (0,))).astype(BF16)
    for h in range(heads):
        pair = jnp.concatenate([k[:, head_cut(h)], v[:, head_cut(h)]], 1)
        kv_ref[:, h] = pair.reshape(kv_ref.shape[0], kv_ref.shape[2], 2 * HEAD_DIM)

    @pl.when(step == 2)
    def _():
        pl.semaphore_wait(pltpu.get_barrier_semaphore(), peers + groups - 2)

        @pl.loop(1, peers)
        def _(r):
            along(r, lax.rem(me + r, peers)).start()

    @pl.when(step == pl.num_programs(0) - 1)
    def _():
        @pl.loop(1, peers)
        def _(r):
            along(r, lax.rem(me + r, peers)).wait()

        own.wait()


def project(tokens, w3, requests, tile_rows, peers, groups, number):
    rows, width = tokens.shape
    cols = w3.shape[2]
    step = 256
    kv_block = (step // tile_rows, cols // HEAD_DIM, tile_rows, 2 * HEAD_DIM)
    return pl.pallas_call(
        functools.partial(project_kernel, peers, groups),
        grid=(rows // step,),
        in_specs=[
            pl.BlockSpec((step, width), lambda i: (i, 0)),
            pl.BlockSpec((3, width, cols), lambda i: (0, 0, 0)),
            pl.BlockSpec(memory_space=pl.ANY),
        ],
        out_specs=[
            pl.BlockSpec((step, width), lambda i: (i, 0)),
            pl.BlockSpec((step, cols), lambda i: (i, 0)),
            pl.BlockSpec(kv_block, lambda i: (i, 0, 0, 0)),
            pl.BlockSpec((2, step), lambda i: (0, i)),
            pl.BlockSpec(memory_space=pl.ANY),
        ],
        out_shape=[
            jax.ShapeDtypeStruct((rows, width), BF16),
            jax.ShapeDtypeStruct((rows, cols), BF16),
            jax.ShapeDtypeStruct((rows // tile_rows,) + kv_block[1:], BF16),
            jax.ShapeDtypeStruct((2, rows), F32),
            jax.ShapeDtypeStruct((peers,) + requests.shape, requests.dtype),
        ],
        scratch_shapes=[pltpu.SemaphoreType.DMA((2, peers)), pltpu.SemaphoreType.DMA],
        compiler_params=pltpu.CompilerParams(
            collective_id=number, has_side_effects=True, vmem_limit_bytes=VMEM_BYTES
        ),
    )(tokens, w3, requests)


def copy_to(src, dst, sems, index, device):
    return pltpu.make_async_remote_copy(
        src_ref=src,
        dst_ref=dst,
        send_sem=sems.at[0, index],
        recv_sem=sems.at[1, index],
        device_id=device,
        device_id_type=pl.DeviceIdType.MESH,
    )


def greet(peers, groups):
    signal_all(peers, groups)
    pl.semaphore_wait(pltpu.get_barrier_semaphore(), peers + groups - 2)


def signal_all(peers, groups):
    barrier = pltpu.get_barrier_semaphore()
    me, group = lax.axis_index("space"), lax.axis_index("head")

    @pl.loop(1, peers)
    def _(r):
        pl.semaphore_signal(
            barrier,
            inc=1,
            device_id={"space": lax.rem(me + r, peers)},
            device_id_type=pl.DeviceIdType.MESH,
        )

    for k in range(1, groups):
        pl.semaphore_signal(
            barrier,
            inc=1,
            device_id={"head": lax.rem(group + k, groups)},
            device_id_type=pl.DeviceIdType.MESH,
        )


def torus_order():
    near = [(0, 1), (0, 3), (1, 0), (3, 0), (1, 1), (3, 3), (1, 3), (3, 1)]
    far = [(0, 2), (2, 0), (1, 2), (2, 1), (3, 2), (2, 3), (2, 2)]
    order = [(0, 0, 1)]
    for group in (near[:4], near[4:], far[:2], far[2:6], far[6:]):
        order += [(z, x, core) for core in (0, 1) for z, x in group]
    return order


ORDER = torus_order()


def torus_peer(me, step):
    z = lax.rem(me // 8 + step[0], 4)
    x = lax.rem(lax.rem(me // 2, 4) + step[1], 4)
    return z * 8 + x * 2 + lax.rem(lax.rem(me, 2) + step[2], 2)


def second_ranges(peers, reach):
    if 2 * reach >= peers - 1:
        return [(1, peers)]
    return [(1, reach + 1), (peers - reach, peers)]


def fetch_kernel(peers, groups, reach, wanted_ref, kv_ref, cot_ref, out_ref, cots_ref, staged, sems, row_sems, own_sem):
    me, group = lax.axis_index("space"), lax.axis_index("head")
    greet(peers, groups)
    own = pltpu.make_async_copy(cot_ref, cots_ref.at[group], own_sem)
    own.start()

    def across(k):
        return copy_to(
            cot_ref, cots_ref.at[group], row_sems, k, {"head": lax.rem(group + k, groups)}
        )

    def along(c, r, peer):
        return copy_to(
            staged.at[r, c], out_ref.at[me, c], sems, c * peers + r, {"space": peer}
        )

    for k in range(1, groups):
        across(k).start()
    for i, step in enumerate(ORDER):
        peer = torus_peer(me, step)
        staged[i, 0] = kv_ref[jnp.maximum(wanted_ref[peer], 0)]
        along(0, i, peer).start()
    for low, high in second_ranges(peers, reach):

        @pl.loop(low, high)
        def _(r):
            peer = lax.rem(me + r, peers)
            staged[r, 1] = kv_ref[jnp.maximum(wanted_ref[peers + peer], 0)]
            along(1, r, peer).start()

    @pl.loop(0, len(ORDER))
    def _(i):
        along(0, i, lax.rem(me + 1, peers)).wait()

    for low, high in second_ranges(peers, reach):

        @pl.loop(low, high)
        def _(r):
            along(1, r, lax.rem(me + r, peers)).wait()

    for k in range(1, groups):
        across(k).wait()
    own.wait()


def fetch(wanted, kv, cot, peers, groups, reach, number):
    out = (peers, SLOTS) + kv.shape[1:]
    whole = pl.BlockSpec(memory_space=pl.ANY)
    return pl.pallas_call(
        functools.partial(fetch_kernel, peers, groups, reach),
        in_specs=[
            pl.BlockSpec(memory_space=pltpu.SMEM),
            pl.BlockSpec(memory_space=pltpu.VMEM),
            whole,
        ],
        out_specs=[whole, whole],
        out_shape=[
            jax.ShapeDtypeStruct(out, kv.dtype),
            jax.ShapeDtypeStruct((groups,) + cot.shape, cot.dtype),
        ],
        scratch_shapes=[
            pltpu.VMEM(out, kv.dtype),
            pltpu.SemaphoreType.DMA((2, SLOTS * peers)),
            pltpu.SemaphoreType.DMA((2, groups)),
            pltpu.SemaphoreType.DMA,
        ],
        compiler_params=pltpu.CompilerParams(
            collective_id=number, has_side_effects=True, vmem_limit_bytes=VMEM_BYTES
        ),
    )(wanted, kv, cot)


def return_kernel(peers, groups, reach, wanted_ref, near_ref, far_ref, att_ref, grad_kv_ref, atts_ref, total, landed, sems, row_sems, own_sem):
    me, group = lax.axis_index("space"), lax.axis_index("head")
    greet(peers, groups)
    own = pltpu.make_async_copy(att_ref.at[group], atts_ref.at[group], own_sem)
    own.start()

    def across(k):
        peer = lax.rem(group + k, groups)
        return copy_to(att_ref.at[peer], atts_ref.at[group], row_sems, k, {"head": peer})

    def along(c, r, peer):
        return copy_to(
            far_ref.at[peer, c], landed.at[r, c], sems, c * peers + r, {"space": peer}
        )

    for i, step in enumerate(ORDER):
        along(0, i, torus_peer(me, step)).start()
    for low, high in second_ranges(peers, reach):

        @pl.loop(low, high)
        def _(r):
            along(1, r, lax.rem(me + r, peers)).start()

    for k in range(1, groups):
        across(k).start()
    total[...] = near_ref[...]

    def add(c, r, source):
        tile = wanted_ref[c * peers + source]
        block = landed[r, c].astype(F32)

        @pl.loop(0, total.shape[0])
        def _(t):
            total[t] += block * jnp.where(tile == t, 1.0, 0.0)

    for i, step in enumerate(ORDER):
        along(0, i, torus_peer(me, step)).wait()
        add(0, i, torus_peer(me, ((4 - step[0]) % 4, (4 - step[1]) % 4, step[2])))
    for low, high in second_ranges(peers, reach):

        @pl.loop(low, high)
        def _(r):
            along(1, r, lax.rem(me + r, peers)).wait()
            add(1, r, lax.rem(me + peers - r, peers))

    grad_kv_ref[...] = total[...].astype(BF16)
    for k in range(1, groups):
        across(k).wait()
    own.wait()


def give_back(wanted, near, far, att, peers, groups, reach, number):
    whole = pl.BlockSpec(memory_space=pl.ANY)
    vmem = pl.BlockSpec(memory_space=pltpu.VMEM)
    return pl.pallas_call(
        functools.partial(return_kernel, peers, groups, reach),
        in_specs=[pl.BlockSpec(memory_space=pltpu.SMEM), vmem, whole, whole],
        out_specs=[vmem, whole],
        out_shape=[
            jax.ShapeDtypeStruct(near.shape, BF16),
            jax.ShapeDtypeStruct(att.shape, att.dtype),
        ],
        scratch_shapes=[
            pltpu.VMEM(near.shape, F32),
            pltpu.VMEM(far.shape, BF16),
            pltpu.SemaphoreType.DMA((2, SLOTS * peers)),
            pltpu.SemaphoreType.DMA((2, groups)),
            pltpu.SemaphoreType.DMA,
        ],
        compiler_params=pltpu.CompilerParams(
            collective_id=number, has_side_effects=True, vmem_limit_bytes=VMEM_BYTES
        ),
    )(wanted, near, far, att)


def attention_kernel(entries_ref, q_ref, cot_ref, w_out_ref, normed_ref, *refs):
    kv_refs = refs[: AT_ONCE * NEIGHBOURS]
    att_out_ref, near_ref, far_ref, dq_ref, early_ref = refs[AT_ONCE * NEIGHBOURS : -4]
    far_total, held, grad_out, grad_q = refs[-4:]
    tile = pl.program_id(0)
    rows = q_ref.shape[0] // AT_ONCE
    last = pl.num_programs(0) - 1
    heads = q_ref.shape[1] // HEAD_DIM
    own = near_ref.shape[0]

    @pl.when(tile == 0)
    def _():
        near_ref[...] = jnp.zeros_like(near_ref)
        grad_out[...] = jnp.zeros_like(grad_out)
        grad_q[...] = jnp.zeros_like(grad_q)

        @pl.loop(0, far_total.shape[0])
        def _(i):
            far_total[i] = jnp.zeros(far_total.shape[1:], F32)

    groups = cot_ref.shape[0]
    share = cot_ref.shape[2]
    cot = jnp.concatenate([cot_ref[g] for g in range(groups)], 1)
    grad_attended = dot(cot, w_out_ref[...], ((1,), (1,))).astype(BF16)
    q = q_ref[...]
    left = lax.broadcasted_iota(jnp.int32, (128, 128), 1) < HEAD_DIM
    upper = lax.broadcasted_iota(jnp.int32, (128, 128), 0) < HEAD_DIM

    def begin(u, h):
        span = slice(u * rows, (u + 1) * rows)
        pair = jnp.concatenate([q[span, head_cut(h)], grad_attended[span, head_cut(h)]], 1)
        pair_t = pair.T
        zero = jnp.zeros_like(pair)
        stacked = jnp.concatenate([jnp.where(left, pair, zero), jnp.where(left, zero, pair)], 0)
        stacked_t = jnp.concatenate(
            [jnp.where(upper, pair_t, zero), jnp.where(upper, zero, pair_t)], 1
        )
        mine = kv_refs[u * NEIGHBOURS : (u + 1) * NEIGHBOURS]
        kv = jnp.concatenate([r[0, h] for r in mine], 0)
        return stacked_t, kv, dot(stacked, kv, ((1,), (1,)))

    mixed = []
    order = [(u, h) for u in range(AT_ONCE) for h in range(heads)]
    following = begin(*order[0])
    for at, (u, h) in enumerate(order):
        stacked_t, kv, both = following
        if at + 1 < len(order):
            following = begin(*order[at + 1])
        scores = both[:128]
        grad_prob = both[128:]
        weights = jnp.exp(scores - jnp.max(scores, axis=1, keepdims=True))
        inverse = 1.0 / jnp.sum(weights, axis=1, keepdims=True)
        row_delta = jnp.sum(weights * grad_prob, axis=1, keepdims=True) * inverse
        likely = weights * inverse
        grad_score = likely * (grad_prob - row_delta)
        factors = jnp.concatenate([grad_score.astype(BF16), likely.astype(BF16)], 0)
        mixed.append(dot(factors, kv, ((1,), (0,))))
        grad_kv_t = dot(stacked_t, factors, ((1,), (0,)))
        for j in range(NEIGHBOURS):
            held[u * NEIGHBOURS + j, h] = grad_kv_t[:, j * 128 : (j + 1) * 128]

    for u in range(AT_ONCE):

        @pl.loop(0, NEAR)
        def _(j, u=u):
            near_ref[entries_ref[tile * AT_ONCE + u, j]] += held[u * NEIGHBOURS + j]

        @pl.loop(NEAR, NEIGHBOURS)
        def _(j, u=u):
            far_total[entries_ref[tile * AT_ONCE + u, j] - own] += held[u * NEIGHBOURS + j]


    def join(parts):
        lines = [jnp.concatenate(parts[i : i + heads], 1) for i in range(0, len(parts), heads)]
        return jnp.concatenate(lines, 0)

    dq = join([m[:128, :HEAD_DIM] for m in mixed])
    dq = (dq * HEAD_DIM ** (-0.5)).astype(BF16)
    attended = join([m[128:, HEAD_DIM:] for m in mixed]).astype(BF16)
    dq_ref[...] = dq
    att_out = dot(attended, w_out_ref[...], ((1,), (0,))).astype(BF16)
    for g in range(groups):
        att_out_ref[g] = att_out[:, g * share : (g + 1) * share]
    grad_out[...] += dot(cot, attended, ((0,), (0,)))
    grad_q[...] += dot(normed_ref[...], dq, ((0,), (0,)))

    @pl.when(tile == last)
    def _():
        @pl.loop(0, far_total.shape[0])
        def _(i):
            far_ref[i] = far_total[i].astype(BF16)

        cols = grad_q.shape[1]
        early_ref[:, :cols] = grad_out[...].astype(BF16)
        early_ref[:, cols:] = grad_q[...].astype(BF16)


def attention(entries, q, cot, w_out, normed, kv, fetched):
    tiles, heads, rows, mixed = kv.shape
    slots = fetched.shape[0]
    tile_block = (1, heads, rows, mixed)
    cols = q.shape[1]
    groups, _, share = cot.shape
    width = groups * share
    lines = AT_ONCE * rows
    cot_spec = pl.BlockSpec((groups, lines, share), lambda t, e: (0, t, 0))
    whole2 = lambda t, e: (0, 0)
    row2 = lambda t, e: (t, 0)
    kv_specs = []
    for u in range(AT_ONCE):
        for j in range(NEIGHBOURS):
            shift = 0 if j < NEAR else tiles
            kv_specs.append(
                pl.BlockSpec(
                    tile_block,
                    lambda t, e, u=u, j=j, shift=shift: (e[t * AT_ONCE + u, j] - shift, 0, 0, 0),
                )
            )
    once = pl.Buffered(1)
    return pl.pallas_call(
        attention_kernel,
        grid_spec=pltpu.PrefetchScalarGridSpec(
            num_scalar_prefetch=1,
            grid=(tiles // AT_ONCE,),
            in_specs=[
                pl.BlockSpec((lines, cols), row2),
                cot_spec,
                pl.BlockSpec((cols, width), whole2),
                pl.BlockSpec((lines, width), row2),
            ]
            + kv_specs,
            out_specs=[
                cot_spec,
                pl.BlockSpec(kv.shape, lambda t, e: (0, 0, 0, 0), pipeline_mode=once),
                pl.BlockSpec(fetched.shape, lambda t, e: (0, 0, 0, 0), pipeline_mode=once),
                pl.BlockSpec((lines, cols), row2),
                pl.BlockSpec((width, 2 * cols), whole2, pipeline_mode=once),
            ],
            scratch_shapes=[
                pltpu.VMEM(fetched.shape, F32),
                pltpu.VMEM((AT_ONCE * NEIGHBOURS,) + kv.shape[1:], F32),
                pltpu.VMEM((width, cols), F32),
                pltpu.VMEM((width, cols), F32),
            ],
        ),
        out_shape=[
            jax.ShapeDtypeStruct(cot.shape, BF16),
            jax.ShapeDtypeStruct(kv.shape, F32),
            jax.ShapeDtypeStruct(fetched.shape, BF16),
            jax.ShapeDtypeStruct((tiles * rows, cols), BF16),
            jax.ShapeDtypeStruct((width, 2 * cols), BF16),
        ],
        compiler_params=pltpu.CompilerParams(vmem_limit_bytes=50 * 2**20),
    )(entries, q, cot, w_out, normed, *(([kv] * NEAR + [fetched] * (NEIGHBOURS - NEAR)) * AT_ONCE))


def finish_kernel(peers, groups, tokens_ref, dq_ref, grad_kv_ref, w_ref, early_ref, earlies_ref, lates_ref, parts_ref, sums_ref, grads, normed, part, late, sums, stats, sems, row_sems, own_sems):
    me, group = lax.axis_index("space"), lax.axis_index("head")
    signal_all(peers, groups)
    rows, width = tokens_ref.shape
    cols = dq_ref.shape[1]
    share = width // groups
    tiles, heads = grad_kv_ref.shape[:2]
    span = rows // tiles
    step = 256

    @pl.loop(0, rows // step)
    def _(i):
        at = pl.ds(pl.multiple_of(i * step, step), step)
        standard, mean, inverse = norm_rows(tokens_ref[at, :])
        normed[at, :] = standard.astype(BF16)
        stats[0, at, :] = jnp.broadcast_to(mean, (step, 128))
        stats[1, at, :] = jnp.broadcast_to(inverse, (step, 128))
        grads[at, :cols] = dq_ref[at, :]

    for t in range(tiles):
        pairs = [grad_kv_ref[t, h].T for h in range(heads)]
        at = slice(t * span, (t + 1) * span)
        grads[at, cols : 2 * cols] = jnp.concatenate([p[:, :HEAD_DIM] for p in pairs], 1)
        grads[at, 2 * cols :] = jnp.concatenate([p[:, HEAD_DIM:] for p in pairs], 1)

    def chunk(k):
        at_cols = pl.ds(pl.multiple_of(lax.rem(group + k, groups) * share, share), share)

        @pl.loop(0, rows // step)
        def _(i):
            at = pl.ds(pl.multiple_of(i * step, step), step)
            piece = dot(grads[at, :cols], w_ref[0, at_cols, :], ((1,), (1,)))
            for n in (1, 2):
                lanes = slice(n * cols, (n + 1) * cols)
                piece += dot(grads[at, lanes], w_ref[n, at_cols, :], ((1,), (1,)))
            part[k, at, :] = piece.astype(BF16)
            values = tokens_ref[at, at_cols].astype(F32)
            standard = (values - stats[0, at, :1]) * stats[1, at, :1]
            found = [
                jnp.sum(piece, 1, keepdims=True),
                jnp.sum(piece * standard, 1, keepdims=True),
            ]
            found = jnp.concatenate(found, 1).T
            if k == 0:
                sums[:, at] = found
            else:
                sums[:, at] += found

    def across(k):
        return copy_to(
            part.at[k], parts_ref.at[group], row_sems, k, {"head": lax.rem(group + k, groups)}
        )

    def across_sums(k):
        return copy_to(
            sums, sums_ref.at[group], row_sems, groups + k, {"head": lax.rem(group + k, groups)}
        )

    def along(kind, r, peer):
        source, target = ((early_ref, earlies_ref), (late, lates_ref))[kind]
        return copy_to(
            source.at[peer], target.at[me], sems, kind * peers + r, {"space": peer}
        )

    owns = [
        pltpu.make_async_copy(early_ref.at[me], earlies_ref.at[me], own_sems.at[0]),
        pltpu.make_async_copy(late.at[me], lates_ref.at[me], own_sems.at[1]),
        pltpu.make_async_copy(part.at[0], parts_ref.at[group], own_sems.at[2]),
        pltpu.make_async_copy(sums, sums_ref.at[group], own_sems.at[3]),
    ]
    owns[0].start()
    chunk(0)
    owns[2].start()
    pl.semaphore_wait(pltpu.get_barrier_semaphore(), peers + groups - 2)
    for r, torus in enumerate(ORDER):
        along(0, r, torus_peer(me, torus)).start()
    for k in (2, 1, 3):
        chunk(k)
        across(k).start()
    owns[3].start()
    for k in range(1, groups):
        across_sums(k).start()

    piece = width // 4
    for i in range(4):
        made = dot(normed[:, i * piece : (i + 1) * piece], grads[:, cols:], ((0,), (0,)))
        late[i * peers // 4 : (i + 1) * peers // 4] = made.astype(BF16).reshape(
            peers // 4, width // peers, 2 * cols
        )
    owns[1].start()
    for r, torus in enumerate(ORDER):
        along(1, r, torus_peer(me, torus)).start()

    @pl.loop(0, len(ORDER))
    def _(r):
        along(0, r, lax.rem(me + 1, peers)).wait()
        along(1, r, lax.rem(me + 1, peers)).wait()

    for k in range(1, groups):
        across(k).wait()
        across_sums(k).wait()
    for own in owns:
        own.wait()


def finish(tokens, dq, grad_kv, w3, early, peers, groups, number):
    rows, width = tokens.shape
    cols = dq.shape[1]
    whole = pl.BlockSpec(memory_space=pl.ANY)
    vmem = pl.BlockSpec(memory_space=pltpu.VMEM)
    part = (groups, rows, width // groups)
    return pl.pallas_call(
        functools.partial(finish_kernel, peers, groups),
        in_specs=[vmem] * 4 + [whole],
        out_specs=[whole] * 4,
        out_shape=[
            jax.ShapeDtypeStruct(early.shape, BF16),
            jax.ShapeDtypeStruct(early.shape, BF16),
            jax.ShapeDtypeStruct(part, BF16),
            jax.ShapeDtypeStruct((groups, 2, rows), F32),
        ],
        scratch_shapes=[
            pltpu.VMEM((rows, 3 * cols), BF16),
            pltpu.VMEM((rows, width), BF16),
            pltpu.VMEM(part, BF16),
            pltpu.VMEM(early.shape, BF16),
            pltpu.VMEM((2, rows), F32),
            pltpu.VMEM((2, rows, 128), F32),
            pltpu.SemaphoreType.DMA((2, 2 * peers)),
            pltpu.SemaphoreType.DMA((2, 2 * groups)),
            pltpu.SemaphoreType.DMA((4,)),
        ],
        compiler_params=pltpu.CompilerParams(
            collective_id=number, has_side_effects=True, vmem_limit_bytes=VMEM_BYTES
        ),
    )(tokens, dq, grad_kv, w3, early)


def on_device(tokens, w_qkv, w_out, neighbours, requests, cotangent):
    row_count, width = tokens.shape
    tiles = neighbours.shape[0]
    rows = row_count // tiles
    cols = w_qkv.shape[2]
    peers, groups = lax.axis_size("space"), lax.axis_size("head")
    share = cotangent.shape[1]
    me = lax.axis_index("space")
    column = lax.axis_index("head") * share
    w3 = jnp.transpose(w_qkv, (1, 0, 2))

    normed, q, kv, stats, table = project(
        tokens, w3, requests[0].T, rows, peers, groups, 2 * len(REACHES) + 3
    )
    wanted = lax.dynamic_index_in_dim(table, me, 2, keepdims=False).T.reshape(-1)
    apart = jnp.abs(jnp.arange(peers)[:, None] - jnp.arange(peers)[None, :])
    apart = jnp.minimum(apart, peers - apart)
    reach = jnp.max(jnp.where(jnp.any(table[:, 1:] >= 0, axis=1), apart, 0))
    level = (reach > REACHES[0]).astype(jnp.int32) + (reach > REACHES[1]).astype(jnp.int32)
    reaches = (*REACHES, peers)

    fetched, cots = lax.switch(
        level,
        [
            functools.partial(fetch, peers=peers, groups=groups, reach=r, number=n)
            for n, r in enumerate(reaches)
        ],
        wanted,
        kv,
        cotangent,
    )
    attended, near, far, dq, early = attention(
        neighbours, q, cots, w_out, normed, kv, fetched.reshape((-1,) + kv.shape[1:])
    )

    grad_kv, attended = lax.switch(
        level,
        [
            functools.partial(
                give_back, peers=peers, groups=groups, reach=r, number=n + len(reaches)
            )
            for n, r in enumerate(reaches)
        ],
        wanted,
        near,
        far.reshape(fetched.shape),
        attended,
    )
    early = early.reshape(peers, width // peers, 2 * cols)
    early, late, part, sums = finish(
        tokens, dq, grad_kv, w3, early, peers, groups, 2 * len(reaches)
    )

    own_tokens = lax.dynamic_slice_in_dim(tokens, column, share, 1).astype(F32)
    layer_out = (own_tokens + jnp.sum(attended.astype(F32), 0)).astype(BF16)
    mean, inverse = stats[0][:, None], stats[1][:, None]
    own_standard = (own_tokens - mean) * inverse
    own_part = jnp.sum(part.astype(F32), 0)
    means = (jnp.sum(sums, 0) / width)[:, :, None]
    grad_tokens = (
        cotangent.astype(F32) + inverse * (own_part - means[0] - own_standard * means[1])
    ).astype(BF16)
    early = jnp.sum(early.astype(F32), 0)
    late = jnp.sum(late.astype(F32), 0)
    grad_w_qkv = jnp.concatenate([early[:, cols:], late], 1).reshape(-1, 3, cols)
    grad_w_out = early[:, :cols].T
    return (layer_out, grad_tokens, grad_w_qkv, grad_w_out)


def solution(mesh):
    placed = (
        P("space", None),
        P(None, None, "head"),
        P("head", None),
        P("space", None),
        P("space", None, None),
        P("space", "head"),
    )
    return jax.shard_map(
        on_device,
        mesh=mesh,
        in_specs=placed,
        out_specs=(
            P("space", "head"),
            P("space", "head"),
            P("space", None, "head"),
            P("head", "space"),
        ),
        check_vma=False,
    )
```

```python
import functools

import jax
import jax.numpy as jnp
from jax import lax
from jax.experimental import pallas as pl
from jax.experimental.pallas import tpu as pltpu
from jax.sharding import PartitionSpec as P

HEAD_DIM = 64
NEIGHBOURS = 9
NEAR = 4
REACHES = (1, 4)
AT_ONCE = 4
CORE_VMEM = 62 * 2**20
SLOTS = 2
EPSILON = 1e-05
F32 = jnp.float32
BF16 = jnp.bfloat16
VMEM_BYTES = 60 * 2**20


def dot(a, b, dims):
    return lax.dot_general(a, b, (dims, ((), ())), preferred_element_type=F32)


def norm_rows(tokens):
    values = tokens.astype(F32)
    mean = jnp.mean(values, axis=1, keepdims=True)
    centred = values - mean
    inverse = lax.rsqrt(jnp.mean(centred * centred, axis=1, keepdims=True) + EPSILON)
    return centred * inverse, mean, inverse


def head_cut(h):
    return slice(h * HEAD_DIM, (h + 1) * HEAD_DIM)


def project_kernel(peers, groups, tokens_ref, w_ref, requests_ref, normed_ref, q_ref, kv_ref, stats_ref, table_ref, sems, own_sem):
    me = lax.axis_index("space")
    step = pl.program_id(0)
    heads = kv_ref.shape[1]
    own = pltpu.make_async_copy(requests_ref, table_ref.at[me], own_sem)

    def along(r, peer):
        return copy_to(requests_ref, table_ref.at[me], sems, r, {"space": peer})

    @pl.when(step == 0)
    def _():
        own.start()
        signal_all(peers, groups)

    standard, mean, inverse = norm_rows(tokens_ref[...])
    normed = standard.astype(BF16)
    normed_ref[...] = normed
    stats_ref[...] = jnp.concatenate([mean, inverse], 1).T
    q = dot(normed, w_ref[0], ((1,), (0,))).astype(BF16)
    q_ref[...] = (q.astype(F32) * HEAD_DIM ** (-0.5)).astype(BF16)
    k = dot(normed, w_ref[1], ((1,), (0,))).astype(BF16)
    v = dot(normed, w_ref[2], ((1,), (0,))).astype(BF16)
    for h in range(heads):
        pair = jnp.concatenate([k[:, head_cut(h)], v[:, head_cut(h)]], 1)
        kv_ref[:, h] = pair.reshape(kv_ref.shape[0], kv_ref.shape[2], 2 * HEAD_DIM)

    @pl.when(step == 2)
    def _():
        pl.semaphore_wait(pltpu.get_barrier_semaphore(), peers + groups - 2)

        @pl.loop(1, peers)
        def _(r):
            along(r, lax.rem(me + r, peers)).start()

    @pl.when(step == pl.num_programs(0) - 1)
    def _():
        @pl.loop(1, peers)
        def _(r):
            along(r, lax.rem(me + r, peers)).wait()

        own.wait()


def project(tokens, w3, requests, tile_rows, peers, groups, number):
    rows, width = tokens.shape
    cols = w3.shape[2]
    step = 256
    kv_block = (step // tile_rows, cols // HEAD_DIM, tile_rows, 2 * HEAD_DIM)
    return pl.pallas_call(
        functools.partial(project_kernel, peers, groups),
        grid=(rows // step,),
        in_specs=[
            pl.BlockSpec((step, width), lambda i: (i, 0)),
            pl.BlockSpec((3, width, cols), lambda i: (0, 0, 0)),
            pl.BlockSpec(memory_space=pl.ANY),
        ],
        out_specs=[
            pl.BlockSpec((step, width), lambda i: (i, 0)),
            pl.BlockSpec((step, cols), lambda i: (i, 0)),
            pl.BlockSpec(kv_block, lambda i: (i, 0, 0, 0)),
            pl.BlockSpec((2, step), lambda i: (0, i)),
            pl.BlockSpec(memory_space=pl.ANY),
        ],
        out_shape=[
            jax.ShapeDtypeStruct((rows, width), BF16),
            jax.ShapeDtypeStruct((rows, cols), BF16),
            jax.ShapeDtypeStruct((rows // tile_rows,) + kv_block[1:], BF16),
            jax.ShapeDtypeStruct((2, rows), F32),
            jax.ShapeDtypeStruct((peers,) + requests.shape, requests.dtype),
        ],
        scratch_shapes=[pltpu.SemaphoreType.DMA((2, peers)), pltpu.SemaphoreType.DMA],
        compiler_params=pltpu.CompilerParams(
            collective_id=number, has_side_effects=True, vmem_limit_bytes=VMEM_BYTES
        ),
    )(tokens, w3, requests)


def copy_to(src, dst, sems, index, device):
    return pltpu.make_async_remote_copy(
        src_ref=src,
        dst_ref=dst,
        send_sem=sems.at[0, index],
        recv_sem=sems.at[1, index],
        device_id=device,
        device_id_type=pl.DeviceIdType.MESH,
    )


def greet(peers, groups):
    signal_all(peers, groups)
    pl.semaphore_wait(pltpu.get_barrier_semaphore(), peers + groups - 2)


def signal_all(peers, groups):
    barrier = pltpu.get_barrier_semaphore()
    me, group = lax.axis_index("space"), lax.axis_index("head")

    @pl.loop(1, peers)
    def _(r):
        pl.semaphore_signal(
            barrier,
            inc=1,
            device_id={"space": lax.rem(me + r, peers)},
            device_id_type=pl.DeviceIdType.MESH,
        )

    for k in range(1, groups):
        pl.semaphore_signal(
            barrier,
            inc=1,
            device_id={"head": lax.rem(group + k, groups)},
            device_id_type=pl.DeviceIdType.MESH,
        )


def torus_order():
    near = [(0, 1), (0, 3), (1, 0), (3, 0), (1, 1), (3, 3), (1, 3), (3, 1)]
    far = [(0, 2), (2, 0), (1, 2), (2, 1), (3, 2), (2, 3), (2, 2)]
    order = [(0, 0, 1)]
    for group in (near[:4], near[4:], far[:2], far[2:6], far[6:]):
        order += [(z, x, core) for core in (0, 1) for z, x in group]
    return order


ORDER = torus_order()


def torus_peer(me, step):
    z = lax.rem(me // 8 + step[0], 4)
    x = lax.rem(lax.rem(me // 2, 4) + step[1], 4)
    return z * 8 + x * 2 + lax.rem(lax.rem(me, 2) + step[2], 2)


def second_ranges(peers, reach):
    if 2 * reach >= peers - 1:
        return [(1, peers)]
    return [(1, reach + 1), (peers - reach, peers)]


def core_kernel(peers, groups, reach, wanted_ref, entries_ref, perm_ref, same_ref, last_ref, q_ref, kv_ref, w_out_ref, cot_ref, grad_kv_ref, dq_ref, early_ref, atts_ref, staged0, staged1, got0, got1, landed0, landed1, held, near_runs, far_runs, running, total, cots, grad_att, att, part, kv_sems, back_sems, row_sems, own_sems):
    me, group = lax.axis_index("space"), lax.axis_index("head")
    staged, got, landed = (staged0, staged1), (got0, got1), (landed0, landed1)
    tiles, heads, span = kv_ref.shape[:3]
    cols = q_ref.shape[1]
    share = cot_ref.shape[1]
    rows = q_ref.shape[0]
    half_heads = heads // 2
    near_count = tiles * NEAR
    entry_count = tiles * NEIGHBOURS
    greet(peers, groups)

    def across(kind, k):
        peer = lax.rem(group + k, groups)
        source = cot_ref if kind == 0 else part.at[peer]
        target = (cots, atts_ref)[kind].at[group]
        return copy_to(source, target, row_sems, kind * groups + k, {"head": peer})

    def send(half, c, r, peer):
        return copy_to(
            staged[half].at[c * peers + r],
            got[half].at[me * SLOTS + c],
            kv_sems.at[half],
            c * peers + r,
            {"space": peer},
        )

    def give(half, c, r, peer):
        return copy_to(
            staged[half].at[c * peers + r],
            landed[half].at[c * peers + r],
            back_sems.at[half],
            c * peers + r,
            {"space": peer},
        )

    own_cot = pltpu.make_async_copy(cot_ref, cots.at[group], own_sems.at[0])
    own_cot.start()
    for k in range(1, groups):
        across(0, k).start()
    for half in range(2):
        cut = slice(half * half_heads, (half + 1) * half_heads)
        for i, step in enumerate(ORDER):
            peer = torus_peer(me, step)
            staged[half][i] = kv_ref[jnp.maximum(wanted_ref[peer], 0), cut]
            send(half, 0, i, peer).start()
        for low, high in second_ranges(peers, reach):

            @pl.loop(low, high)
            def _(r, half=half, cut=cut):
                peer = lax.rem(me + r, peers)
                tile = jnp.maximum(wanted_ref[peers + peer], 0)
                staged[half][peers + r] = kv_ref[tile, cut]
                send(half, 1, r, peer).start()

    for k in range(1, groups):
        across(0, k).wait()
    own_cot.wait()
    step_rows = 2 * span

    @pl.loop(0, rows // step_rows)
    def _(i):
        at = pl.ds(pl.multiple_of(i * step_rows, step_rows), step_rows)
        cot = jnp.concatenate([cots[g, at, :] for g in range(groups)], 1)
        grad_att[at, :] = dot(cot, w_out_ref[...], ((1,), (1,))).astype(BF16)

    left = lax.broadcasted_iota(jnp.int32, (128, 128), 1) < HEAD_DIM
    upper = lax.broadcasted_iota(jnp.int32, (128, 128), 0) < HEAD_DIM

    def attend(half):
        @pl.loop(0, tiles // AT_ONCE)
        def _(turn):
            def tile_rows(u):
                return pl.ds(pl.multiple_of((turn * AT_ONCE + u) * span, span), span)

            def begin(u, hh):
                h = half * half_heads + hh
                at = tile_rows(u)
                first = (turn * AT_ONCE + u) * NEIGHBOURS
                pair = jnp.concatenate([q_ref[at, head_cut(h)], grad_att[at, head_cut(h)]], 1)
                pair_t = pair.T
                zero = jnp.zeros_like(pair)
                stacked = jnp.concatenate(
                    [jnp.where(left, pair, zero), jnp.where(left, zero, pair)], 0
                )
                stacked_t = jnp.concatenate(
                    [jnp.where(upper, pair_t, zero), jnp.where(upper, zero, pair_t)], 1
                )
                keys = [kv_ref[entries_ref[first + j], h] for j in range(NEAR)]
                keys += [
                    got[half][jnp.maximum(entries_ref[first + j] - tiles, 0), hh]
                    for j in range(NEAR, NEIGHBOURS)
                ]
                kv = jnp.concatenate(keys, 0)
                return stacked_t, kv, dot(stacked, kv, ((1,), (1,)))

            mixed = {}
            order = [(u, hh) for u in range(AT_ONCE) for hh in range(half_heads)]
            following = begin(*order[0])
            for n, (u, hh) in enumerate(order):
                stacked_t, kv, both = following
                if n + 1 < len(order):
                    following = begin(*order[n + 1])
                scores = both[:128]
                grad_prob = both[128:]
                weights = jnp.exp(scores - jnp.max(scores, axis=1, keepdims=True))
                inverse = 1.0 / jnp.sum(weights, axis=1, keepdims=True)
                row_delta = jnp.sum(weights * grad_prob, axis=1, keepdims=True) * inverse
                likely = weights * inverse
                grad_score = likely * (grad_prob - row_delta)
                factors = jnp.concatenate([grad_score.astype(BF16), likely.astype(BF16)], 0)
                mixed[u, hh] = dot(factors, kv, ((1,), (0,)))
                grad_kv_t = dot(stacked_t, factors, ((1,), (0,)))
                first = (turn * AT_ONCE + u) * NEIGHBOURS
                for j in range(NEIGHBOURS):
                    held[first + j, hh] = grad_kv_t[:, j * 128 : (j + 1) * 128]
            lanes = slice(half * half_heads * HEAD_DIM, (half + 1) * half_heads * HEAD_DIM)
            for u in range(AT_ONCE):
                both = [mixed[u, hh] for hh in range(half_heads)]
                dq = jnp.concatenate([m[:128, :HEAD_DIM] for m in both], 1)
                dq_ref[tile_rows(u), lanes] = (dq * HEAD_DIM ** (-0.5)).astype(BF16)
                attended = jnp.concatenate([m[128:, HEAD_DIM:] for m in both], 1)
                att[tile_rows(u), lanes] = attended.astype(BF16)

        def run(i):
            keep = jnp.where(same_ref[i] > 0, 1.0, 0.0)
            value = running[...] * keep + held[perm_ref[i]]
            running[...] = value
            return value

        running[...] = jnp.zeros_like(running)

        @pl.loop(0, near_count)
        def _(i):
            near_runs[i] = run(i)

        @pl.loop(near_count, entry_count)
        def _(i):
            far_runs[i - near_count] = run(i).astype(BF16)

        for i, step in enumerate(ORDER):
            peer = torus_peer(me, step)
            place = jnp.maximum(last_ref[tiles + peer * SLOTS] - near_count, 0)
            staged[half][i] = far_runs[place]
            give(half, 0, i, peer).start()
        for low, high in second_ranges(peers, reach):

            @pl.loop(low, high)
            def _(r):
                peer = lax.rem(me + r, peers)
                place = jnp.maximum(last_ref[tiles + peer * SLOTS + 1] - near_count, 0)
                staged[half][peers + r] = far_runs[place]
                give(half, 1, r, peer).start()

        @pl.loop(0, tiles)
        def _(t):
            total[half, t] = near_runs[jnp.maximum(last_ref[t], 0)]

    beside = lax.rem(me + 1, peers)
    for half in range(2):

        @pl.loop(0, len(ORDER))
        def _(i, half=half):
            send(half, 0, i, beside).wait()

        for low, high in second_ranges(peers, reach):

            @pl.loop(low, high)
            def _(r, half=half):
                send(half, 1, r, beside).wait()

        attend(half)

    own_att = pltpu.make_async_copy(part.at[group], atts_ref.at[group], own_sems.at[1])
    for g in range(groups):

        @pl.loop(0, rows // step_rows)
        def _(i, g=g):
            at = pl.ds(pl.multiple_of(i * step_rows, step_rows), step_rows)
            lanes = slice(g * share, (g + 1) * share)
            made = dot(att[at, :], w_out_ref[:, lanes], ((1,), (0,)))
            part[g, at, :] = made.astype(BF16)

    own_att.start()
    for k in range(1, groups):
        across(1, k).start()
    for g in range(groups):
        made = dot(cots[g], att[...], ((0,), (0,)))
        early_ref[g * share : (g + 1) * share, :] = made.astype(BF16)

    for half in range(2):

        def add(c, r, source, half=half):
            tile = wanted_ref[c * peers + source]
            block = landed[half][c * peers + r].astype(F32)

            @pl.loop(0, tiles)
            def _(t):
                total[half, t] += block * jnp.where(tile == t, 1.0, 0.0)

        for i, step in enumerate(ORDER):
            give(half, 0, i, torus_peer(me, step)).wait()
            add(0, i, torus_peer(me, ((4 - step[0]) % 4, (4 - step[1]) % 4, step[2])))
        for low, high in second_ranges(peers, reach):

            @pl.loop(low, high)
            def _(r, half=half, add=add):
                give(half, 1, r, lax.rem(me + r, peers)).wait()
                add(1, r, lax.rem(me + peers - r, peers))

        grad_kv_ref[:, half * half_heads : (half + 1) * half_heads] = total[half].astype(BF16)
    for k in range(1, groups):
        across(1, k).wait()
    own_att.wait()


def core(wanted, entries, perm, same, last, q, kv, w_out, cot, peers, groups, reach, number):
    tiles, heads, span, mixed = kv.shape
    rows, cols = q.shape
    width = w_out.shape[1]
    half = (heads // 2, span, mixed)
    slots = pltpu.VMEM((peers * SLOTS,) + half, BF16)
    smem = pl.BlockSpec(memory_space=pltpu.SMEM)
    vmem = pl.BlockSpec(memory_space=pltpu.VMEM)
    whole = pl.BlockSpec(memory_space=pl.ANY)
    parts = (groups,) + cot.shape
    return pl.pallas_call(
        functools.partial(core_kernel, peers, groups, reach),
        in_specs=[smem] * 5 + [vmem] * 3 + [whole],
        out_specs=[vmem] * 3 + [whole],
        out_shape=[
            jax.ShapeDtypeStruct(kv.shape, BF16),
            jax.ShapeDtypeStruct(q.shape, BF16),
            jax.ShapeDtypeStruct((width, cols), BF16),
            jax.ShapeDtypeStruct(parts, BF16),
        ],
        scratch_shapes=[slots] * 6
        + [
            pltpu.VMEM((tiles * NEIGHBOURS,) + half, F32),
            pltpu.VMEM((tiles * NEAR,) + half, F32),
            pltpu.VMEM((tiles * (NEIGHBOURS - NEAR),) + half, BF16),
            pltpu.VMEM(half, F32),
            pltpu.VMEM((2, tiles) + half, F32),
            pltpu.VMEM(parts, BF16),
            pltpu.VMEM(q.shape, BF16),
            pltpu.VMEM(q.shape, BF16),
            pltpu.VMEM(parts, BF16),
            pltpu.SemaphoreType.DMA((2, 2, SLOTS * peers)),
            pltpu.SemaphoreType.DMA((2, 2, SLOTS * peers)),
            pltpu.SemaphoreType.DMA((2, 2 * groups)),
            pltpu.SemaphoreType.DMA((2,)),
        ],
        compiler_params=pltpu.CompilerParams(
            collective_id=number, has_side_effects=True, vmem_limit_bytes=CORE_VMEM
        ),
    )(wanted, entries, perm, same, last, q, kv, w_out, cot)


def finish_kernel(peers, groups, tokens_ref, dq_ref, grad_kv_ref, w_ref, early_ref, earlies_ref, lates_ref, parts_ref, sums_ref, grads, normed, part, late, sums, stats, sems, row_sems, own_sems):
    me, group = lax.axis_index("space"), lax.axis_index("head")
    signal_all(peers, groups)
    rows, width = tokens_ref.shape
    cols = dq_ref.shape[1]
    share = width // groups
    tiles, heads = grad_kv_ref.shape[:2]
    span = rows // tiles
    step = 256

    @pl.loop(0, rows // step)
    def _(i):
        at = pl.ds(pl.multiple_of(i * step, step), step)
        standard, mean, inverse = norm_rows(tokens_ref[at, :])
        normed[at, :] = standard.astype(BF16)
        stats[0, at, :] = jnp.broadcast_to(mean, (step, 128))
        stats[1, at, :] = jnp.broadcast_to(inverse, (step, 128))
        grads[at, :cols] = dq_ref[at, :]

    for t in range(tiles):
        pairs = [grad_kv_ref[t, h].T for h in range(heads)]
        at = slice(t * span, (t + 1) * span)
        grads[at, cols : 2 * cols] = jnp.concatenate([p[:, :HEAD_DIM] for p in pairs], 1)
        grads[at, 2 * cols :] = jnp.concatenate([p[:, HEAD_DIM:] for p in pairs], 1)

    def chunk(k):
        at_cols = pl.ds(pl.multiple_of(lax.rem(group + k, groups) * share, share), share)

        @pl.loop(0, rows // step)
        def _(i):
            at = pl.ds(pl.multiple_of(i * step, step), step)
            piece = dot(grads[at, :cols], w_ref[0, at_cols, :], ((1,), (1,)))
            for n in (1, 2):
                lanes = slice(n * cols, (n + 1) * cols)
                piece += dot(grads[at, lanes], w_ref[n, at_cols, :], ((1,), (1,)))
            part[k, at, :] = piece.astype(BF16)
            values = tokens_ref[at, at_cols].astype(F32)
            standard = (values - stats[0, at, :1]) * stats[1, at, :1]
            found = [
                jnp.sum(piece, 1, keepdims=True),
                jnp.sum(piece * standard, 1, keepdims=True),
            ]
            found = jnp.concatenate(found, 1).T
            if k == 2:
                sums[:, at] = found
            else:
                sums[:, at] += found

    def across(k):
        return copy_to(
            part.at[k], parts_ref.at[group], row_sems, k, {"head": lax.rem(group + k, groups)}
        )

    def across_sums(k):
        return copy_to(
            sums, sums_ref.at[group], row_sems, groups + k, {"head": lax.rem(group + k, groups)}
        )

    def along(kind, r, peer):
        source, target = ((early_ref, earlies_ref), (late, lates_ref))[kind]
        return copy_to(
            source.at[peer], target.at[me], sems, kind * peers + r, {"space": peer}
        )

    owns = [
        pltpu.make_async_copy(early_ref.at[me], earlies_ref.at[me], own_sems.at[0]),
        pltpu.make_async_copy(late.at[me], lates_ref.at[me], own_sems.at[1]),
        pltpu.make_async_copy(part.at[0], parts_ref.at[group], own_sems.at[2]),
        pltpu.make_async_copy(sums, sums_ref.at[group], own_sems.at[3]),
    ]
    owns[0].start()
    pl.semaphore_wait(pltpu.get_barrier_semaphore(), peers + groups - 2)
    for r, torus in enumerate(ORDER):
        along(0, r, torus_peer(me, torus)).start()
    chunk(2)
    across(2).start()
    piece = width // 4
    for i in range(4):
        made = dot(normed[:, i * piece : (i + 1) * piece], grads[...], ((0,), (0,)))
        late[i * peers // 4 : (i + 1) * peers // 4] = made.astype(BF16).reshape(
            peers // 4, width // peers, 3 * cols
        )
    owns[1].start()
    for r, torus in enumerate(ORDER):
        along(1, r, torus_peer(me, torus)).start()
    for k in (1, 3):
        chunk(k)
        across(k).start()
    chunk(0)
    owns[2].start()
    owns[3].start()
    for k in range(1, groups):
        across_sums(k).start()

    @pl.loop(0, len(ORDER))
    def _(r):
        along(0, r, lax.rem(me + 1, peers)).wait()
        along(1, r, lax.rem(me + 1, peers)).wait()

    for k in range(1, groups):
        across(k).wait()
        across_sums(k).wait()
    for own in owns:
        own.wait()


def finish(tokens, dq, grad_kv, w3, early, peers, groups, number):
    rows, width = tokens.shape
    cols = dq.shape[1]
    whole = pl.BlockSpec(memory_space=pl.ANY)
    vmem = pl.BlockSpec(memory_space=pltpu.VMEM)
    part = (groups, rows, width // groups)
    late = (peers, width // peers, 3 * cols)
    return pl.pallas_call(
        functools.partial(finish_kernel, peers, groups),
        in_specs=[vmem] * 4 + [whole],
        out_specs=[whole] * 4,
        out_shape=[
            jax.ShapeDtypeStruct(early.shape, BF16),
            jax.ShapeDtypeStruct(late, BF16),
            jax.ShapeDtypeStruct(part, BF16),
            jax.ShapeDtypeStruct((groups, 2, rows), F32),
        ],
        scratch_shapes=[
            pltpu.VMEM((rows, 3 * cols), BF16),
            pltpu.VMEM((rows, width), BF16),
            pltpu.VMEM(part, BF16),
            pltpu.VMEM(late, BF16),
            pltpu.VMEM((2, rows), F32),
            pltpu.VMEM((2, rows, 128), F32),
            pltpu.SemaphoreType.DMA((2, 2 * peers)),
            pltpu.SemaphoreType.DMA((2, 2 * groups)),
            pltpu.SemaphoreType.DMA((4,)),
        ],
        compiler_params=pltpu.CompilerParams(
            collective_id=number, has_side_effects=True, vmem_limit_bytes=VMEM_BYTES
        ),
    )(tokens, dq, grad_kv, w3, early)


def on_device(tokens, w_qkv, w_out, neighbours, requests, cotangent):
    row_count, width = tokens.shape
    tiles = neighbours.shape[0]
    rows = row_count // tiles
    cols = w_qkv.shape[2]
    peers, groups = lax.axis_size("space"), lax.axis_size("head")
    share = cotangent.shape[1]
    me = lax.axis_index("space")
    column = lax.axis_index("head") * share
    w3 = jnp.transpose(w_qkv, (1, 0, 2))

    normed, q, kv, stats, table = project(
        tokens, w3, requests[0].T, rows, peers, groups, 2 * len(REACHES) + 3
    )
    wanted = lax.dynamic_index_in_dim(table, me, 2, keepdims=False).T.reshape(-1)
    apart = jnp.abs(jnp.arange(peers)[:, None] - jnp.arange(peers)[None, :])
    apart = jnp.minimum(apart, peers - apart)
    reach = jnp.max(jnp.where(jnp.any(table[:, 1:] >= 0, axis=1), apart, 0))
    level = (reach > REACHES[0]).astype(jnp.int32) + (reach > REACHES[1]).astype(jnp.int32)
    reaches = (*REACHES, peers)

    entries = neighbours.reshape(-1)
    count = entries.shape[0]
    place = jnp.arange(count, dtype=jnp.int32)
    lower = entries[None, :] < entries[:, None]
    lower |= (entries[None, :] == entries[:, None]) & (place[None, :] < place[:, None])
    rank = jnp.sum(lower.astype(jnp.int32), 1)
    ranked = (rank[None, :] == place[:, None]).astype(jnp.int32)
    perm = jnp.sum(ranked * place[None, :], 1)
    keys = jnp.arange(tiles + peers * SLOTS, dtype=jnp.int32)
    below = (entries[None, :] < keys[:, None]).astype(jnp.int32)
    last = jnp.sum((entries[None, :] <= keys[:, None]).astype(jnp.int32), 1) - 1
    starts = jnp.sum(below, 1)
    same = 1 - jnp.max((starts[None, :] == place[:, None]).astype(jnp.int32), 1)
    grad_kv, dq, early, attended = lax.switch(
        level,
        [
            functools.partial(core, peers=peers, groups=groups, reach=r, number=n)
            for n, r in enumerate(reaches)
        ],
        *(wanted, entries, perm, same, last, q, kv, w_out, cotangent),
    )
    early = early.reshape(peers, width // peers, cols)
    early, late, part, sums = finish(
        tokens, dq, grad_kv, w3, early, peers, groups, 2 * len(reaches)
    )

    own_tokens = lax.dynamic_slice_in_dim(tokens, column, share, 1).astype(F32)
    layer_out = (own_tokens + jnp.sum(attended.astype(F32), 0)).astype(BF16)
    mean, inverse = stats[0][:, None], stats[1][:, None]
    own_standard = (own_tokens - mean) * inverse
    own_part = jnp.sum(part.astype(F32), 0)
    means = (jnp.sum(sums, 0) / width)[:, :, None]
    grad_tokens = (
        cotangent.astype(F32) + inverse * (own_part - means[0] - own_standard * means[1])
    ).astype(BF16)
    grad_w_out = jnp.sum(early.astype(F32), 0).T
    grad_w_qkv = jnp.sum(late.astype(F32), 0).reshape(-1, 3, cols)
    return (layer_out, grad_tokens, grad_w_qkv, grad_w_out)


def solution(mesh):
    placed = (
        P("space", None),
        P(None, None, "head"),
        P("head", None),
        P("space", None),
        P("space", None, None),
        P("space", "head"),
    )
    return jax.shard_map(
        on_device,
        mesh=mesh,
        in_specs=placed,
        out_specs=(
            P("space", "head"),
            P("space", "head"),
            P("space", None, "head"),
            P("head", "space"),
        ),
        check_vma=False,
    )
```

```python
import functools

import jax
import jax.numpy as jnp
from jax import lax
from jax.experimental import pallas as pl
from jax.experimental.pallas import tpu as pltpu
from jax.sharding import PartitionSpec as P

HEAD_DIM = 64
NEIGHBOURS = 9
NEAR = 4
REACHES = (1,)
AT_ONCE = 2
CORE_VMEM = 62 * 2**20
SLOTS = 2
EPSILON = 1e-05
F32 = jnp.float32
BF16 = jnp.bfloat16
VMEM_BYTES = 60 * 2**20


def dot(a, b, dims):
    return lax.dot_general(a, b, (dims, ((), ())), preferred_element_type=F32)


def norm_rows(tokens):
    values = tokens.astype(F32)
    mean = jnp.mean(values, axis=1, keepdims=True)
    centred = values - mean
    inverse = lax.rsqrt(jnp.mean(centred * centred, axis=1, keepdims=True) + EPSILON)
    return centred * inverse, mean, inverse


def head_cut(h):
    return slice(h * HEAD_DIM, (h + 1) * HEAD_DIM)


def project_kernel(peers, groups, tokens_ref, w_ref, requests_ref, normed_ref, q_ref, kv_ref, stats_ref, table_ref, sems, own_sem):
    me = lax.axis_index("space")
    step = pl.program_id(0)
    heads = kv_ref.shape[1]
    own = pltpu.make_async_copy(requests_ref, table_ref.at[me], own_sem)

    def along(r, peer):
        return copy_to(requests_ref, table_ref.at[me], sems, r, {"space": peer})

    @pl.when(step == 0)
    def _():
        own.start()
        signal_all(peers, groups)

    standard, mean, inverse = norm_rows(tokens_ref[...])
    normed = standard.astype(BF16)
    normed_ref[...] = normed
    stats_ref[...] = jnp.concatenate([mean, inverse], 1).T
    q = dot(normed, w_ref[0], ((1,), (0,))).astype(BF16)
    q_ref[...] = (q.astype(F32) * HEAD_DIM ** (-0.5)).astype(BF16)
    k = dot(normed, w_ref[1], ((1,), (0,))).astype(BF16)
    v = dot(normed, w_ref[2], ((1,), (0,))).astype(BF16)
    for h in range(heads):
        pair = jnp.concatenate([k[:, head_cut(h)], v[:, head_cut(h)]], 1)
        kv_ref[:, h] = pair.reshape(kv_ref.shape[0], kv_ref.shape[2], 2 * HEAD_DIM)

    @pl.when(step == 2)
    def _():
        pl.semaphore_wait(pltpu.get_barrier_semaphore(), peers + groups - 2)

        @pl.loop(1, peers)
        def _(r):
            along(r, lax.rem(me + r, peers)).start()

    @pl.when(step == pl.num_programs(0) - 1)
    def _():
        @pl.loop(1, peers)
        def _(r):
            along(r, lax.rem(me + r, peers)).wait()

        own.wait()


def project(tokens, w3, requests, tile_rows, peers, groups, number):
    rows, width = tokens.shape
    cols = w3.shape[2]
    step = 256
    kv_block = (step // tile_rows, cols // HEAD_DIM, tile_rows, 2 * HEAD_DIM)
    return pl.pallas_call(
        functools.partial(project_kernel, peers, groups),
        grid=(rows // step,),
        in_specs=[
            pl.BlockSpec((step, width), lambda i: (i, 0)),
            pl.BlockSpec((3, width, cols), lambda i: (0, 0, 0)),
            pl.BlockSpec(memory_space=pl.ANY),
        ],
        out_specs=[
            pl.BlockSpec((step, width), lambda i: (i, 0)),
            pl.BlockSpec((step, cols), lambda i: (i, 0)),
            pl.BlockSpec(kv_block, lambda i: (i, 0, 0, 0)),
            pl.BlockSpec((2, step), lambda i: (0, i)),
            pl.BlockSpec(memory_space=pl.ANY),
        ],
        out_shape=[
            jax.ShapeDtypeStruct((rows, width), BF16),
            jax.ShapeDtypeStruct((rows, cols), BF16),
            jax.ShapeDtypeStruct((rows // tile_rows,) + kv_block[1:], BF16),
            jax.ShapeDtypeStruct((2, rows), F32),
            jax.ShapeDtypeStruct((peers,) + requests.shape, requests.dtype),
        ],
        scratch_shapes=[pltpu.SemaphoreType.DMA((2, peers)), pltpu.SemaphoreType.DMA],
        compiler_params=pltpu.CompilerParams(
            collective_id=number, has_side_effects=True, vmem_limit_bytes=VMEM_BYTES
        ),
    )(tokens, w3, requests)


def copy_to(src, dst, sems, index, device):
    return pltpu.make_async_remote_copy(
        src_ref=src,
        dst_ref=dst,
        send_sem=sems.at[0, index],
        recv_sem=sems.at[1, index],
        device_id=device,
        device_id_type=pl.DeviceIdType.MESH,
    )


def greet(peers, groups):
    signal_all(peers, groups)
    pl.semaphore_wait(pltpu.get_barrier_semaphore(), peers + groups - 2)


def signal_all(peers, groups):
    barrier = pltpu.get_barrier_semaphore()
    me, group = lax.axis_index("space"), lax.axis_index("head")

    @pl.loop(1, peers)
    def _(r):
        pl.semaphore_signal(
            barrier,
            inc=1,
            device_id={"space": lax.rem(me + r, peers)},
            device_id_type=pl.DeviceIdType.MESH,
        )

    for k in range(1, groups):
        pl.semaphore_signal(
            barrier,
            inc=1,
            device_id={"head": lax.rem(group + k, groups)},
            device_id_type=pl.DeviceIdType.MESH,
        )


def axis_steps(q):
    far = 1 + 2 * lax.rem(q, 2)
    return (q // 2) * far, (1 - q // 2) * far


def corner_steps(q):
    return 1 + 2 * lax.rem(q, 2), 1 + 2 * lax.rem(lax.rem(q, 2) + q // 2, 2)


def across_steps(q):
    return 2 * q, 2 - 2 * q


def knight_steps(q):
    odd = lax.rem(q, 2)
    return 2 * odd + (1 - odd) * (1 + q), 2 * (1 - odd) + odd * q


def opposite_steps(q):
    return 2 + 0 * q, 2 + 0 * q


GROUPS = (
    (4, axis_steps),
    (4, corner_steps),
    (2, across_steps),
    (4, knight_steps),
    (1, opposite_steps),
)


def each_peer(act):
    act(0, (0, 0, 1))
    base = 1
    for size, steps in GROUPS:

        @pl.loop(0, 2 * size)
        def _(n, size=size, steps=steps, base=base):
            act(base + n, (*steps(lax.rem(n, size)), n // size))

        base += 2 * size


def torus_peer(me, step):
    z = lax.rem(me // 8 + step[0], 4)
    x = lax.rem(lax.rem(me // 2, 4) + step[1], 4)
    return z * 8 + x * 2 + lax.rem(lax.rem(me, 2) + step[2], 2)


def torus_source(me, step):
    return torus_peer(me, (4 - step[0], 4 - step[1], step[2]))


def second_ranges(peers, reach):
    if 2 * reach >= peers - 1:
        return [(1, peers)]
    return [(1, reach + 1), (peers - reach, peers)]


def core_kernel(peers, groups, reach, wanted_ref, entries_ref, perm_ref, same_ref, last_ref, q_ref, kv_ref, w_out_ref, cot_ref, grad_kv_ref, dq_ref, early_ref, atts_ref, staged0, staged1, got0, got1, landed0, landed1, held, near_runs, far_runs, running, total, cots, grad_att, att, part, kv_sems, back_sems, row_sems, own_sems):
    me, group = lax.axis_index("space"), lax.axis_index("head")
    staged, got, landed = (staged0, staged1), (got0, got1), (landed0, landed1)
    tiles, heads, span = kv_ref.shape[:3]
    cols = q_ref.shape[1]
    share = cot_ref.shape[1]
    rows = q_ref.shape[0]
    half_heads = heads // 2
    near_count = tiles * NEAR
    entry_count = tiles * NEIGHBOURS
    greet(peers, groups)

    def across(kind, k):
        peer = lax.rem(group + k, groups)
        source = cot_ref if kind == 0 else part.at[peer]
        target = (cots, atts_ref)[kind].at[group]
        return copy_to(source, target, row_sems, kind * groups + k, {"head": peer})

    def send(half, c, r, peer):
        return copy_to(
            staged[half].at[c * peers + r],
            got[half].at[me * SLOTS + c],
            kv_sems.at[half],
            c * peers + r,
            {"space": peer},
        )

    def give(half, c, r, peer):
        return copy_to(
            staged[half].at[c * peers + r],
            landed[half].at[c * peers + r],
            back_sems.at[half],
            c * peers + r,
            {"space": peer},
        )

    own_cot = pltpu.make_async_copy(cot_ref, cots.at[group], own_sems.at[0])
    own_cot.start()
    for k in range(1, groups):
        across(0, k).start()
    for half in range(2):
        cut = slice(half * half_heads, (half + 1) * half_heads)

        @each_peer
        def _(i, step, half=half, cut=cut):
            peer = torus_peer(me, step)
            staged[half][i] = kv_ref[jnp.maximum(wanted_ref[peer], 0), cut]
            send(half, 0, i, peer).start()

        for low, high in second_ranges(peers, reach):

            @pl.loop(low, high)
            def _(r, half=half, cut=cut):
                peer = lax.rem(me + r, peers)
                tile = jnp.maximum(wanted_ref[peers + peer], 0)
                staged[half][peers + r] = kv_ref[tile, cut]
                send(half, 1, r, peer).start()

    for k in range(1, groups):
        across(0, k).wait()
    own_cot.wait()
    step_rows = 2 * span

    @pl.loop(0, rows // step_rows)
    def _(i):
        at = pl.ds(pl.multiple_of(i * step_rows, step_rows), step_rows)
        cot = jnp.concatenate([cots[g, at, :] for g in range(groups)], 1)
        grad_att[at, :] = dot(cot, w_out_ref[...], ((1,), (1,))).astype(BF16)

    left = lax.broadcasted_iota(jnp.int32, (128, 128), 1) < HEAD_DIM
    upper = lax.broadcasted_iota(jnp.int32, (128, 128), 0) < HEAD_DIM

    def attend(half):
        @pl.loop(0, tiles // AT_ONCE)
        def _(turn):
            def tile_rows(u):
                return pl.ds(pl.multiple_of((turn * AT_ONCE + u) * span, span), span)

            def begin(u, hh):
                h = half * half_heads + hh
                at = tile_rows(u)
                first = (turn * AT_ONCE + u) * NEIGHBOURS
                pair = jnp.concatenate([q_ref[at, head_cut(h)], grad_att[at, head_cut(h)]], 1)
                pair_t = pair.T
                zero = jnp.zeros_like(pair)
                stacked = jnp.concatenate(
                    [jnp.where(left, pair, zero), jnp.where(left, zero, pair)], 0
                )
                stacked_t = jnp.concatenate(
                    [jnp.where(upper, pair_t, zero), jnp.where(upper, zero, pair_t)], 1
                )
                keys = [kv_ref[entries_ref[first + j], h] for j in range(NEAR)]
                keys += [
                    got[half][jnp.maximum(entries_ref[first + j] - tiles, 0), hh]
                    for j in range(NEAR, NEIGHBOURS)
                ]
                kv = jnp.concatenate(keys, 0)
                return stacked_t, kv, dot(stacked, kv, ((1,), (1,)))

            mixed = {}
            order = [(u, hh) for u in range(AT_ONCE) for hh in range(half_heads)]
            following = begin(*order[0])
            for n, (u, hh) in enumerate(order):
                stacked_t, kv, both = following
                if n + 1 < len(order):
                    following = begin(*order[n + 1])
                scores = both[:128]
                grad_prob = both[128:]
                weights = jnp.exp(scores - jnp.max(scores, axis=1, keepdims=True))
                inverse = 1.0 / jnp.sum(weights, axis=1, keepdims=True)
                row_delta = jnp.sum(weights * grad_prob, axis=1, keepdims=True) * inverse
                likely = weights * inverse
                grad_score = likely * (grad_prob - row_delta)
                factors = jnp.concatenate([grad_score.astype(BF16), likely.astype(BF16)], 0)
                mixed[u, hh] = dot(factors, kv, ((1,), (0,)))
                grad_kv_t = dot(stacked_t, factors, ((1,), (0,)))
                first = (turn * AT_ONCE + u) * NEIGHBOURS
                for j in range(NEIGHBOURS):
                    held[first + j, hh] = grad_kv_t[:, j * 128 : (j + 1) * 128]
            lanes = slice(half * half_heads * HEAD_DIM, (half + 1) * half_heads * HEAD_DIM)
            for u in range(AT_ONCE):
                both = [mixed[u, hh] for hh in range(half_heads)]
                dq = jnp.concatenate([m[:128, :HEAD_DIM] for m in both], 1)
                dq_ref[tile_rows(u), lanes] = (dq * HEAD_DIM ** (-0.5)).astype(BF16)
                attended = jnp.concatenate([m[128:, HEAD_DIM:] for m in both], 1)
                att[tile_rows(u), lanes] = attended.astype(BF16)

        def run(i):
            keep = jnp.where(same_ref[i] > 0, 1.0, 0.0)
            value = running[...] * keep + held[perm_ref[i]]
            running[...] = value
            return value

        running[...] = jnp.zeros_like(running)

        @pl.loop(0, near_count)
        def _(i):
            near_runs[i] = run(i)

        @pl.loop(near_count, entry_count)
        def _(i):
            far_runs[i - near_count] = run(i).astype(BF16)

        @each_peer
        def _(i, step):
            peer = torus_peer(me, step)
            place = jnp.maximum(last_ref[tiles + peer * SLOTS] - near_count, 0)
            staged[half][i] = far_runs[place]
            give(half, 0, i, peer).start()

        for low, high in second_ranges(peers, reach):

            @pl.loop(low, high)
            def _(r):
                peer = lax.rem(me + r, peers)
                place = jnp.maximum(last_ref[tiles + peer * SLOTS + 1] - near_count, 0)
                staged[half][peers + r] = far_runs[place]
                give(half, 1, r, peer).start()

        @pl.loop(0, tiles)
        def _(t):
            total[half, t] = near_runs[jnp.maximum(last_ref[t], 0)]

    beside = lax.rem(me + 1, peers)
    for half in range(2):

        @pl.loop(0, (peers - 1))
        def _(i, half=half):
            send(half, 0, i, beside).wait()

        for low, high in second_ranges(peers, reach):

            @pl.loop(low, high)
            def _(r, half=half):
                send(half, 1, r, beside).wait()

        attend(half)

    own_att = pltpu.make_async_copy(part.at[group], atts_ref.at[group], own_sems.at[1])
    for g in range(groups):

        @pl.loop(0, rows // step_rows)
        def _(i, g=g):
            at = pl.ds(pl.multiple_of(i * step_rows, step_rows), step_rows)
            lanes = slice(g * share, (g + 1) * share)
            made = dot(att[at, :], w_out_ref[:, lanes], ((1,), (0,)))
            part[g, at, :] = made.astype(BF16)

    own_att.start()
    for k in range(1, groups):
        across(1, k).start()
    for g in range(groups):
        made = dot(cots[g], att[...], ((0,), (0,)))
        early_ref[g * share : (g + 1) * share, :] = made.astype(BF16)

    for half in range(2):

        def add(c, r, source, half=half):
            tile = wanted_ref[c * peers + source]
            block = landed[half][c * peers + r].astype(F32)

            @pl.loop(0, tiles)
            def _(t):
                total[half, t] += block * jnp.where(tile == t, 1.0, 0.0)

        @each_peer
        def _(i, step, half=half, add=add):
            give(half, 0, i, torus_peer(me, step)).wait()
            add(0, i, torus_source(me, step))

        for low, high in second_ranges(peers, reach):

            @pl.loop(low, high)
            def _(r, half=half, add=add):
                give(half, 1, r, lax.rem(me + r, peers)).wait()
                add(1, r, lax.rem(me + peers - r, peers))

        grad_kv_ref[:, half * half_heads : (half + 1) * half_heads] = total[half].astype(BF16)
    for k in range(1, groups):
        across(1, k).wait()
    own_att.wait()


def core(wanted, entries, perm, same, last, q, kv, w_out, cot, peers, groups, reach, number):
    tiles, heads, span, mixed = kv.shape
    rows, cols = q.shape
    width = w_out.shape[1]
    half = (heads // 2, span, mixed)
    slots = pltpu.VMEM((peers * SLOTS,) + half, BF16)
    smem = pl.BlockSpec(memory_space=pltpu.SMEM)
    vmem = pl.BlockSpec(memory_space=pltpu.VMEM)
    whole = pl.BlockSpec(memory_space=pl.ANY)
    parts = (groups,) + cot.shape
    return pl.pallas_call(
        functools.partial(core_kernel, peers, groups, reach),
        in_specs=[smem] * 5 + [vmem] * 3 + [whole],
        out_specs=[vmem] * 3 + [whole],
        out_shape=[
            jax.ShapeDtypeStruct(kv.shape, BF16),
            jax.ShapeDtypeStruct(q.shape, BF16),
            jax.ShapeDtypeStruct((width, cols), BF16),
            jax.ShapeDtypeStruct(parts, BF16),
        ],
        scratch_shapes=[slots] * 6
        + [
            pltpu.VMEM((tiles * NEIGHBOURS,) + half, F32),
            pltpu.VMEM((tiles * NEAR,) + half, F32),
            pltpu.VMEM((tiles * (NEIGHBOURS - NEAR),) + half, BF16),
            pltpu.VMEM(half, F32),
            pltpu.VMEM((2, tiles) + half, F32),
            pltpu.VMEM(parts, BF16),
            pltpu.VMEM(q.shape, BF16),
            pltpu.VMEM(q.shape, BF16),
            pltpu.VMEM(parts, BF16),
            pltpu.SemaphoreType.DMA((2, 2, SLOTS * peers)),
            pltpu.SemaphoreType.DMA((2, 2, SLOTS * peers)),
            pltpu.SemaphoreType.DMA((2, 2 * groups)),
            pltpu.SemaphoreType.DMA((2,)),
        ],
        compiler_params=pltpu.CompilerParams(
            collective_id=number, has_side_effects=True, vmem_limit_bytes=CORE_VMEM
        ),
    )(wanted, entries, perm, same, last, q, kv, w_out, cot)


def finish_kernel(peers, groups, tokens_ref, dq_ref, grad_kv_ref, w_ref, early_ref, earlies_ref, lates_ref, parts_ref, sums_ref, grads, normed, part, late, sums, stats, sems, row_sems, own_sems):
    me, group = lax.axis_index("space"), lax.axis_index("head")
    signal_all(peers, groups)
    rows, width = tokens_ref.shape
    cols = dq_ref.shape[1]
    share = width // groups
    tiles, heads = grad_kv_ref.shape[:2]
    span = rows // tiles
    step = 256

    @pl.loop(0, rows // step)
    def _(i):
        at = pl.ds(pl.multiple_of(i * step, step), step)
        standard, mean, inverse = norm_rows(tokens_ref[at, :])
        normed[at, :] = standard.astype(BF16)
        stats[0, at, :] = jnp.broadcast_to(mean, (step, 128))
        stats[1, at, :] = jnp.broadcast_to(inverse, (step, 128))
        grads[at, :cols] = dq_ref[at, :]

    for t in range(tiles):
        pairs = [grad_kv_ref[t, h].T for h in range(heads)]
        at = slice(t * span, (t + 1) * span)
        grads[at, cols : 2 * cols] = jnp.concatenate([p[:, :HEAD_DIM] for p in pairs], 1)
        grads[at, 2 * cols :] = jnp.concatenate([p[:, HEAD_DIM:] for p in pairs], 1)

    def chunk(k):
        at_cols = pl.ds(pl.multiple_of(lax.rem(group + k, groups) * share, share), share)

        @pl.loop(0, rows // step)
        def _(i):
            at = pl.ds(pl.multiple_of(i * step, step), step)
            piece = dot(grads[at, :cols], w_ref[0, at_cols, :], ((1,), (1,)))
            for n in (1, 2):
                lanes = slice(n * cols, (n + 1) * cols)
                piece += dot(grads[at, lanes], w_ref[n, at_cols, :], ((1,), (1,)))
            part[k, at, :] = piece.astype(BF16)
            values = tokens_ref[at, at_cols].astype(F32)
            standard = (values - stats[0, at, :1]) * stats[1, at, :1]
            found = [
                jnp.sum(piece, 1, keepdims=True),
                jnp.sum(piece * standard, 1, keepdims=True),
            ]
            found = jnp.concatenate(found, 1).T
            if k == 2:
                sums[:, at] = found
            else:
                sums[:, at] += found

    def across(k):
        return copy_to(
            part.at[k], parts_ref.at[group], row_sems, k, {"head": lax.rem(group + k, groups)}
        )

    def across_sums(k):
        return copy_to(
            sums, sums_ref.at[group], row_sems, groups + k, {"head": lax.rem(group + k, groups)}
        )

    def along(kind, r, peer):
        source, target = ((early_ref, earlies_ref), (late, lates_ref))[kind]
        return copy_to(
            source.at[peer], target.at[me], sems, kind * peers + r, {"space": peer}
        )

    owns = [
        pltpu.make_async_copy(early_ref.at[me], earlies_ref.at[me], own_sems.at[0]),
        pltpu.make_async_copy(late.at[me], lates_ref.at[me], own_sems.at[1]),
        pltpu.make_async_copy(part.at[0], parts_ref.at[group], own_sems.at[2]),
        pltpu.make_async_copy(sums, sums_ref.at[group], own_sems.at[3]),
    ]
    owns[0].start()
    pl.semaphore_wait(pltpu.get_barrier_semaphore(), peers + groups - 2)
    each_peer(lambda r, torus: along(0, r, torus_peer(me, torus)).start())
    chunk(2)
    across(2).start()
    piece = width // 4
    for i in range(4):
        made = dot(normed[:, i * piece : (i + 1) * piece], grads[...], ((0,), (0,)))
        late[i * peers // 4 : (i + 1) * peers // 4] = made.astype(BF16).reshape(
            peers // 4, width // peers, 3 * cols
        )
    owns[1].start()
    each_peer(lambda r, torus: along(1, r, torus_peer(me, torus)).start())
    for k in (1, 3):
        chunk(k)
        across(k).start()
    chunk(0)
    owns[2].start()
    owns[3].start()
    for k in range(1, groups):
        across_sums(k).start()

    @pl.loop(0, (peers - 1))
    def _(r):
        along(0, r, lax.rem(me + 1, peers)).wait()
        along(1, r, lax.rem(me + 1, peers)).wait()

    for k in range(1, groups):
        across(k).wait()
        across_sums(k).wait()
    for own in owns:
        own.wait()


def finish(tokens, dq, grad_kv, w3, early, peers, groups, number):
    rows, width = tokens.shape
    cols = dq.shape[1]
    whole = pl.BlockSpec(memory_space=pl.ANY)
    vmem = pl.BlockSpec(memory_space=pltpu.VMEM)
    part = (groups, rows, width // groups)
    late = (peers, width // peers, 3 * cols)
    return pl.pallas_call(
        functools.partial(finish_kernel, peers, groups),
        in_specs=[vmem] * 4 + [whole],
        out_specs=[whole] * 4,
        out_shape=[
            jax.ShapeDtypeStruct(early.shape, BF16),
            jax.ShapeDtypeStruct(late, BF16),
            jax.ShapeDtypeStruct(part, BF16),
            jax.ShapeDtypeStruct((groups, 2, rows), F32),
        ],
        scratch_shapes=[
            pltpu.VMEM((rows, 3 * cols), BF16),
            pltpu.VMEM((rows, width), BF16),
            pltpu.VMEM(part, BF16),
            pltpu.VMEM(late, BF16),
            pltpu.VMEM((2, rows), F32),
            pltpu.VMEM((2, rows, 128), F32),
            pltpu.SemaphoreType.DMA((2, 2 * peers)),
            pltpu.SemaphoreType.DMA((2, 2 * groups)),
            pltpu.SemaphoreType.DMA((4,)),
        ],
        compiler_params=pltpu.CompilerParams(
            collective_id=number, has_side_effects=True, vmem_limit_bytes=VMEM_BYTES
        ),
    )(tokens, dq, grad_kv, w3, early)


def on_device(tokens, w_qkv, w_out, neighbours, requests, cotangent):
    row_count, width = tokens.shape
    tiles = neighbours.shape[0]
    rows = row_count // tiles
    cols = w_qkv.shape[2]
    peers, groups = lax.axis_size("space"), lax.axis_size("head")
    share = cotangent.shape[1]
    me = lax.axis_index("space")
    column = lax.axis_index("head") * share
    w3 = jnp.transpose(w_qkv, (1, 0, 2))

    normed, q, kv, stats, table = project(
        tokens, w3, requests[0].T, rows, peers, groups, 2 * len(REACHES) + 3
    )
    wanted = lax.dynamic_index_in_dim(table, me, 2, keepdims=False).T.reshape(-1)
    apart = jnp.abs(jnp.arange(peers)[:, None] - jnp.arange(peers)[None, :])
    apart = jnp.minimum(apart, peers - apart)
    reach = jnp.max(jnp.where(jnp.any(table[:, 1:] >= 0, axis=1), apart, 0))
    level = sum((reach > r).astype(jnp.int32) for r in REACHES)
    reaches = (*REACHES, peers)

    entries = neighbours.reshape(-1)
    count = entries.shape[0]
    place = jnp.arange(count, dtype=jnp.int32)
    lower = entries[None, :] < entries[:, None]
    lower |= (entries[None, :] == entries[:, None]) & (place[None, :] < place[:, None])
    rank = jnp.sum(lower.astype(jnp.int32), 1)
    ranked = (rank[None, :] == place[:, None]).astype(jnp.int32)
    perm = jnp.sum(ranked * place[None, :], 1)
    keys = jnp.arange(tiles + peers * SLOTS, dtype=jnp.int32)
    below = (entries[None, :] < keys[:, None]).astype(jnp.int32)
    last = jnp.sum((entries[None, :] <= keys[:, None]).astype(jnp.int32), 1) - 1
    starts = jnp.sum(below, 1)
    same = 1 - jnp.max((starts[None, :] == place[:, None]).astype(jnp.int32), 1)
    grad_kv, dq, early, attended = lax.switch(
        level,
        [
            functools.partial(core, peers=peers, groups=groups, reach=r, number=n)
            for n, r in enumerate(reaches)
        ],
        *(wanted, entries, perm, same, last, q, kv, w_out, cotangent),
    )
    early = early.reshape(peers, width // peers, cols)
    early, late, part, sums = finish(
        tokens, dq, grad_kv, w3, early, peers, groups, 2 * len(reaches)
    )

    own_tokens = lax.dynamic_slice_in_dim(tokens, column, share, 1).astype(F32)
    layer_out = (own_tokens + jnp.sum(attended.astype(F32), 0)).astype(BF16)
    mean, inverse = stats[0][:, None], stats[1][:, None]
    own_standard = (own_tokens - mean) * inverse
    own_part = jnp.sum(part.astype(F32), 0)
    means = (jnp.sum(sums, 0) / width)[:, :, None]
    grad_tokens = (
        cotangent.astype(F32) + inverse * (own_part - means[0] - own_standard * means[1])
    ).astype(BF16)
    grad_w_out = jnp.sum(early.astype(F32), 0).T
    grad_w_qkv = jnp.sum(late.astype(F32), 0).reshape(-1, 3, cols)
    return (layer_out, grad_tokens, grad_w_qkv, grad_w_out)


def solution(mesh):
    placed = (
        P("space", None),
        P(None, None, "head"),
        P("head", None),
        P("space", None),
        P("space", None, None),
        P("space", "head"),
    )
    return jax.shard_map(
        on_device,
        mesh=mesh,
        in_specs=placed,
        out_specs=(
            P("space", "head"),
            P("space", "head"),
            P("space", None, "head"),
            P("head", "space"),
        ),
        check_vma=False,
    )
```

```python
import functools

import jax
import jax.numpy as jnp
from jax import lax
from jax.experimental import pallas as pl
from jax.experimental.pallas import tpu as pltpu
from jax.sharding import PartitionSpec as P

HEAD_DIM = 64
NEIGHBOURS = 9
NEAR = 4
REACHES = (1,)
AT_ONCE = 2
CORE_VMEM = 62 * 2**20
SLOTS = 2
EPSILON = 1e-05
F32 = jnp.float32
BF16 = jnp.bfloat16
VMEM_BYTES = 60 * 2**20


def dot(a, b, dims):
    return lax.dot_general(a, b, (dims, ((), ())), preferred_element_type=F32)


def norm_rows(tokens):
    values = tokens.astype(F32)
    mean = jnp.mean(values, axis=1, keepdims=True)
    centred = values - mean
    inverse = lax.rsqrt(jnp.mean(centred * centred, axis=1, keepdims=True) + EPSILON)
    return centred * inverse, mean, inverse


def head_cut(h):
    return slice(h * HEAD_DIM, (h + 1) * HEAD_DIM)


def project_kernel(peers, groups, tokens_ref, w_ref, requests_ref, q_ref, kv_ref, stats_ref, wanted_out_ref, reach_ref, table_ref, sems, own_sem):
    me = lax.axis_index("space")
    step = pl.program_id(0)
    heads = kv_ref.shape[1]
    own = pltpu.make_async_copy(requests_ref, table_ref.at[me], own_sem)

    def along(r, peer):
        return copy_to(requests_ref, table_ref.at[me], sems, r, {"space": peer})

    @pl.when(step == 0)
    def _():
        own.start()
        signal_all(peers, groups)

    standard, mean, inverse = norm_rows(tokens_ref[...])
    normed = standard.astype(BF16)
    stats_ref[...] = jnp.concatenate([mean, inverse], 1).T
    q = dot(normed, w_ref[0], ((1,), (0,))).astype(BF16)
    q_ref[...] = (q.astype(F32) * HEAD_DIM ** (-0.5)).astype(BF16)
    k = dot(normed, w_ref[1], ((1,), (0,))).astype(BF16)
    v = dot(normed, w_ref[2], ((1,), (0,))).astype(BF16)
    for h in range(heads):
        pair = jnp.concatenate([k[:, head_cut(h)], v[:, head_cut(h)]], 1)
        kv_ref[:, h] = pair.reshape(kv_ref.shape[0], kv_ref.shape[2], 2 * HEAD_DIM)

    @pl.when(step == 2)
    def _():
        pl.semaphore_wait(pltpu.get_barrier_semaphore(), peers + groups - 2)

        @pl.loop(1, peers)
        def _(r):
            along(r, lax.rem(me + r, peers)).start()

    @pl.when(step == pl.num_programs(0) - 1)
    def _():
        @pl.loop(1, peers)
        def _(r):
            along(r, lax.rem(me + r, peers)).wait()

        own.wait()
        source = lax.broadcasted_iota(jnp.int32, (peers, peers), 0)
        target = lax.broadcasted_iota(jnp.int32, (peers, peers), 1)
        found = []
        for c in range(SLOTS):
            asked = table_ref[:, c, :].astype(F32)
            found.append(jnp.sum(jnp.where(target == me, asked, 0.0), 1, keepdims=True))
        wanted_out_ref[...] = jnp.concatenate(found, 1).astype(jnp.int32)
        apart = jnp.abs(source - target)
        apart = jnp.minimum(apart, peers - apart).astype(F32)
        apart = jnp.where(table_ref[:, 1, :] >= 0, apart, 0.0)
        apart = jnp.max(jnp.max(apart, 1, keepdims=True), 0, keepdims=True)
        reach_ref[...] = apart.astype(jnp.int32)


def project(tokens, w3, requests, tile_rows, peers, groups, number):
    rows, width = tokens.shape
    cols = w3.shape[2]
    step = 256
    kv_block = (step // tile_rows, cols // HEAD_DIM, tile_rows, 2 * HEAD_DIM)
    return pl.pallas_call(
        functools.partial(project_kernel, peers, groups),
        grid=(rows // step,),
        in_specs=[
            pl.BlockSpec((step, width), lambda i: (i, 0)),
            pl.BlockSpec((3, width, cols), lambda i: (0, 0, 0)),
            pl.BlockSpec(memory_space=pl.ANY),
        ],
        out_specs=[
            pl.BlockSpec((step, cols), lambda i: (i, 0)),
            pl.BlockSpec(kv_block, lambda i: (i, 0, 0, 0)),
            pl.BlockSpec((2, step), lambda i: (0, i)),
            pl.BlockSpec((peers, SLOTS), lambda i: (0, 0)),
            pl.BlockSpec((1, 1), lambda i: (0, 0)),
        ],
        out_shape=[
            jax.ShapeDtypeStruct((rows, cols), BF16),
            jax.ShapeDtypeStruct((rows // tile_rows,) + kv_block[1:], BF16),
            jax.ShapeDtypeStruct((2, rows), F32),
            jax.ShapeDtypeStruct((peers, SLOTS), requests.dtype),
            jax.ShapeDtypeStruct((1, 1), requests.dtype),
        ],
        scratch_shapes=[
            pltpu.VMEM((peers,) + requests.shape, requests.dtype),
            pltpu.SemaphoreType.DMA((2, peers)),
            pltpu.SemaphoreType.DMA,
        ],
        compiler_params=pltpu.CompilerParams(
            collective_id=number, has_side_effects=True, vmem_limit_bytes=VMEM_BYTES
        ),
    )(tokens, w3, requests)


def copy_to(src, dst, sems, index, device):
    return pltpu.make_async_remote_copy(
        src_ref=src,
        dst_ref=dst,
        send_sem=sems.at[0, index],
        recv_sem=sems.at[1, index],
        device_id=device,
        device_id_type=pl.DeviceIdType.MESH,
    )


def greet(peers, groups):
    signal_all(peers, groups)
    pl.semaphore_wait(pltpu.get_barrier_semaphore(), peers + groups - 2)


def signal_all(peers, groups):
    barrier = pltpu.get_barrier_semaphore()
    me, group = lax.axis_index("space"), lax.axis_index("head")

    @pl.loop(1, peers)
    def _(r):
        pl.semaphore_signal(
            barrier,
            inc=1,
            device_id={"space": lax.rem(me + r, peers)},
            device_id_type=pl.DeviceIdType.MESH,
        )

    for k in range(1, groups):
        pl.semaphore_signal(
            barrier,
            inc=1,
            device_id={"head": lax.rem(group + k, groups)},
            device_id_type=pl.DeviceIdType.MESH,
        )


def axis_steps(q):
    far = 1 + 2 * lax.rem(q, 2)
    return (q // 2) * far, (1 - q // 2) * far


def corner_steps(q):
    return 1 + 2 * lax.rem(q, 2), 1 + 2 * lax.rem(lax.rem(q, 2) + q // 2, 2)


def across_steps(q):
    return 2 * q, 2 - 2 * q


def knight_steps(q):
    odd = lax.rem(q, 2)
    return 2 * odd + (1 - odd) * (1 + q), 2 * (1 - odd) + odd * q


def opposite_steps(q):
    return 2 + 0 * q, 2 + 0 * q


GROUPS = (
    (4, axis_steps),
    (4, corner_steps),
    (2, across_steps),
    (4, knight_steps),
    (1, opposite_steps),
)


def each_peer(act):
    act(0, (0, 0, 1))
    base = 1
    for size, steps in GROUPS:

        @pl.loop(0, 2 * size)
        def _(n, size=size, steps=steps, base=base):
            act(base + n, (*steps(lax.rem(n, size)), n // size))

        base += 2 * size


def torus_peer(me, step):
    z = lax.rem(me // 8 + step[0], 4)
    x = lax.rem(lax.rem(me // 2, 4) + step[1], 4)
    return z * 8 + x * 2 + lax.rem(lax.rem(me, 2) + step[2], 2)


def torus_source(me, step):
    return torus_peer(me, (4 - step[0], 4 - step[1], step[2]))


def second_ranges(peers, reach):
    if 2 * reach >= peers - 1:
        return [(1, peers)]
    return [(1, reach + 1), (peers - reach, peers)]


def core_kernel(peers, groups, reach, wanted_ref, entries_ref, perm_ref, same_ref, last_ref, q_ref, kv_ref, w_out_ref, cot_ref, grad_kv_ref, dq_ref, early_ref, atts_ref, staged0, staged1, got0, got1, landed0, landed1, held, near_runs, far_runs, running, total, cots, grad_att, att, part, kv_sems, back_sems, row_sems, own_sems):
    me, group = lax.axis_index("space"), lax.axis_index("head")
    staged, got, landed = (staged0, staged1), (got0, got1), (landed0, landed1)
    tiles, heads, span = kv_ref.shape[:3]
    cols = q_ref.shape[1]
    share = cot_ref.shape[1]
    rows = q_ref.shape[0]
    half_heads = heads // 2
    near_count = tiles * NEAR
    entry_count = tiles * NEIGHBOURS
    greet(peers, groups)

    def across(kind, k):
        peer = lax.rem(group + k, groups)
        source = cot_ref if kind == 0 else part.at[peer]
        target = (cots, atts_ref)[kind].at[group]
        return copy_to(source, target, row_sems, kind * groups + k, {"head": peer})

    def send(half, c, r, peer):
        return copy_to(
            staged[half].at[c * peers + r],
            got[half].at[me * SLOTS + c],
            kv_sems.at[half],
            c * peers + r,
            {"space": peer},
        )

    def give(half, c, r, peer):
        return copy_to(
            staged[half].at[c * peers + r],
            landed[half].at[c * peers + r],
            back_sems.at[half],
            c * peers + r,
            {"space": peer},
        )

    own_cot = pltpu.make_async_copy(cot_ref, cots.at[group], own_sems.at[0])
    own_cot.start()
    for k in range(1, groups):
        across(0, k).start()
    for half in range(2):
        cut = slice(half * half_heads, (half + 1) * half_heads)

        @each_peer
        def _(i, step, half=half, cut=cut):
            peer = torus_peer(me, step)
            staged[half][i] = kv_ref[jnp.maximum(wanted_ref[peer, 0], 0), cut]
            send(half, 0, i, peer).start()

        for low, high in second_ranges(peers, reach):

            @pl.loop(low, high)
            def _(r, half=half, cut=cut):
                peer = lax.rem(me + r, peers)
                tile = jnp.maximum(wanted_ref[peer, 1], 0)
                staged[half][peers + r] = kv_ref[tile, cut]
                send(half, 1, r, peer).start()

    for k in range(1, groups):
        across(0, k).wait()
    own_cot.wait()
    step_rows = 2 * span

    @pl.loop(0, rows // step_rows)
    def _(i):
        at = pl.ds(pl.multiple_of(i * step_rows, step_rows), step_rows)
        cot = jnp.concatenate([cots[g, at, :] for g in range(groups)], 1)
        grad_att[at, :] = dot(cot, w_out_ref[...], ((1,), (1,))).astype(BF16)

    left = lax.broadcasted_iota(jnp.int32, (128, 128), 1) < HEAD_DIM
    upper = lax.broadcasted_iota(jnp.int32, (128, 128), 0) < HEAD_DIM

    def attend(half):
        @pl.loop(0, tiles // AT_ONCE)
        def _(turn):
            def tile_rows(u):
                return pl.ds(pl.multiple_of((turn * AT_ONCE + u) * span, span), span)

            def begin(u, hh):
                h = half * half_heads + hh
                at = tile_rows(u)
                first = (turn * AT_ONCE + u) * NEIGHBOURS
                pair = jnp.concatenate([q_ref[at, head_cut(h)], grad_att[at, head_cut(h)]], 1)
                pair_t = pair.T
                zero = jnp.zeros_like(pair)
                stacked = jnp.concatenate(
                    [jnp.where(left, pair, zero), jnp.where(left, zero, pair)], 0
                )
                stacked_t = jnp.concatenate(
                    [jnp.where(upper, pair_t, zero), jnp.where(upper, zero, pair_t)], 1
                )
                keys = [kv_ref[entries_ref[first + j], h] for j in range(NEAR)]
                keys += [
                    got[half][jnp.maximum(entries_ref[first + j] - tiles, 0), hh]
                    for j in range(NEAR, NEIGHBOURS)
                ]
                kv = jnp.concatenate(keys, 0)
                return stacked_t, kv, dot(stacked, kv, ((1,), (1,)))

            mixed = {}
            order = [(u, hh) for u in range(AT_ONCE) for hh in range(half_heads)]
            following = begin(*order[0])
            for n, (u, hh) in enumerate(order):
                stacked_t, kv, both = following
                if n + 1 < len(order):
                    following = begin(*order[n + 1])
                scores = both[:128]
                grad_prob = both[128:]
                weights = jnp.exp(scores - jnp.max(scores, axis=1, keepdims=True))
                inverse = 1.0 / jnp.sum(weights, axis=1, keepdims=True)
                row_delta = jnp.sum(weights * grad_prob, axis=1, keepdims=True) * inverse
                likely = weights * inverse
                grad_score = likely * (grad_prob - row_delta)
                factors = jnp.concatenate([grad_score.astype(BF16), likely.astype(BF16)], 0)
                mixed[u, hh] = dot(factors, kv, ((1,), (0,)))
                grad_kv_t = dot(stacked_t, factors, ((1,), (0,)))
                first = (turn * AT_ONCE + u) * NEIGHBOURS
                for j in range(NEIGHBOURS):
                    held[first + j, hh] = grad_kv_t[:, j * 128 : (j + 1) * 128]
            lanes = slice(half * half_heads * HEAD_DIM, (half + 1) * half_heads * HEAD_DIM)
            for u in range(AT_ONCE):
                both = [mixed[u, hh] for hh in range(half_heads)]
                dq = jnp.concatenate([m[:128, :HEAD_DIM] for m in both], 1)
                dq_ref[tile_rows(u), lanes] = (dq * HEAD_DIM ** (-0.5)).astype(BF16)
                attended = jnp.concatenate([m[128:, HEAD_DIM:] for m in both], 1)
                att[tile_rows(u), lanes] = attended.astype(BF16)

        def run(i):
            keep = jnp.where(same_ref[i] > 0, 1.0, 0.0)
            value = running[...] * keep + held[perm_ref[i]]
            running[...] = value
            return value

        running[...] = jnp.zeros_like(running)

        @pl.loop(0, near_count)
        def _(i):
            near_runs[i] = run(i)

        @pl.loop(near_count, entry_count)
        def _(i):
            far_runs[i - near_count] = run(i).astype(BF16)

        @each_peer
        def _(i, step):
            peer = torus_peer(me, step)
            place = jnp.maximum(last_ref[tiles + peer * SLOTS] - near_count, 0)
            staged[half][i] = far_runs[place]
            give(half, 0, i, peer).start()

        for low, high in second_ranges(peers, reach):

            @pl.loop(low, high)
            def _(r):
                peer = lax.rem(me + r, peers)
                place = jnp.maximum(last_ref[tiles + peer * SLOTS + 1] - near_count, 0)
                staged[half][peers + r] = far_runs[place]
                give(half, 1, r, peer).start()

        @pl.loop(0, tiles)
        def _(t):
            total[half, t] = near_runs[jnp.maximum(last_ref[t], 0)]

    beside = lax.rem(me + 1, peers)
    for half in range(2):

        @pl.loop(0, (peers - 1))
        def _(i, half=half):
            send(half, 0, i, beside).wait()

        for low, high in second_ranges(peers, reach):

            @pl.loop(low, high)
            def _(r, half=half):
                send(half, 1, r, beside).wait()

        attend(half)

    own_att = pltpu.make_async_copy(part.at[group], atts_ref.at[group], own_sems.at[1])
    for g in range(groups):

        @pl.loop(0, rows // step_rows)
        def _(i, g=g):
            at = pl.ds(pl.multiple_of(i * step_rows, step_rows), step_rows)
            lanes = slice(g * share, (g + 1) * share)
            made = dot(att[at, :], w_out_ref[:, lanes], ((1,), (0,)))
            part[g, at, :] = made.astype(BF16)

    own_att.start()
    for k in range(1, groups):
        across(1, k).start()
    for g in range(groups):
        made = dot(cots[g], att[...], ((0,), (0,)))
        early_ref[g * share : (g + 1) * share, :] = made.astype(BF16)

    for half in range(2):

        def add(c, r, source, half=half):
            tile = wanted_ref[source, c]
            block = landed[half][c * peers + r].astype(F32)

            @pl.loop(0, tiles)
            def _(t):
                total[half, t] += block * jnp.where(tile == t, 1.0, 0.0)

        @each_peer
        def _(i, step, half=half, add=add):
            give(half, 0, i, torus_peer(me, step)).wait()
            add(0, i, torus_source(me, step))

        for low, high in second_ranges(peers, reach):

            @pl.loop(low, high)
            def _(r, half=half, add=add):
                give(half, 1, r, lax.rem(me + r, peers)).wait()
                add(1, r, lax.rem(me + peers - r, peers))

        grad_kv_ref[:, half * half_heads : (half + 1) * half_heads] = total[half].astype(BF16)
    for k in range(1, groups):
        across(1, k).wait()
    own_att.wait()


def core(wanted, entries, perm, same, last, q, kv, w_out, cot, peers, groups, reach, number):
    tiles, heads, span, mixed = kv.shape
    rows, cols = q.shape
    width = w_out.shape[1]
    half = (heads // 2, span, mixed)
    slots = pltpu.VMEM((peers * SLOTS,) + half, BF16)
    smem = pl.BlockSpec(memory_space=pltpu.SMEM)
    vmem = pl.BlockSpec(memory_space=pltpu.VMEM)
    whole = pl.BlockSpec(memory_space=pl.ANY)
    parts = (groups,) + cot.shape
    return pl.pallas_call(
        functools.partial(core_kernel, peers, groups, reach),
        in_specs=[smem] * 5 + [vmem] * 3 + [whole],
        out_specs=[vmem] * 3 + [whole],
        out_shape=[
            jax.ShapeDtypeStruct(kv.shape, BF16),
            jax.ShapeDtypeStruct(q.shape, BF16),
            jax.ShapeDtypeStruct((width, cols), BF16),
            jax.ShapeDtypeStruct(parts, BF16),
        ],
        scratch_shapes=[slots] * 6
        + [
            pltpu.VMEM((tiles * NEIGHBOURS,) + half, F32),
            pltpu.VMEM((tiles * NEAR,) + half, F32),
            pltpu.VMEM((tiles * (NEIGHBOURS - NEAR),) + half, BF16),
            pltpu.VMEM(half, F32),
            pltpu.VMEM((2, tiles) + half, F32),
            pltpu.VMEM(parts, BF16),
            pltpu.VMEM(q.shape, BF16),
            pltpu.VMEM(q.shape, BF16),
            pltpu.VMEM(parts, BF16),
            pltpu.SemaphoreType.DMA((2, 2, SLOTS * peers)),
            pltpu.SemaphoreType.DMA((2, 2, SLOTS * peers)),
            pltpu.SemaphoreType.DMA((2, 2 * groups)),
            pltpu.SemaphoreType.DMA((2,)),
        ],
        compiler_params=pltpu.CompilerParams(
            collective_id=number, has_side_effects=True, vmem_limit_bytes=CORE_VMEM
        ),
    )(wanted, entries, perm, same, last, q, kv, w_out, cot)


def finish_kernel(peers, groups, tokens_ref, dq_ref, grad_kv_ref, w_ref, early_ref, earlies_ref, lates_ref, parts_ref, sums_ref, grads, normed, part, late, sums, stats, sems, row_sems, own_sems):
    me, group = lax.axis_index("space"), lax.axis_index("head")
    signal_all(peers, groups)
    rows, width = tokens_ref.shape
    cols = dq_ref.shape[1]
    share = width // groups
    tiles, heads = grad_kv_ref.shape[:2]
    span = rows // tiles
    step = 256

    @pl.loop(0, rows // step)
    def _(i):
        at = pl.ds(pl.multiple_of(i * step, step), step)
        standard, mean, inverse = norm_rows(tokens_ref[at, :])
        normed[at, :] = standard.astype(BF16)
        stats[0, at, :] = jnp.broadcast_to(mean, (step, 128))
        stats[1, at, :] = jnp.broadcast_to(inverse, (step, 128))
        grads[at, :cols] = dq_ref[at, :]

    for t in range(tiles):
        pairs = [grad_kv_ref[t, h].T for h in range(heads)]
        at = slice(t * span, (t + 1) * span)
        grads[at, cols : 2 * cols] = jnp.concatenate([p[:, :HEAD_DIM] for p in pairs], 1)
        grads[at, 2 * cols :] = jnp.concatenate([p[:, HEAD_DIM:] for p in pairs], 1)

    def chunk(k):
        at_cols = pl.ds(pl.multiple_of(lax.rem(group + k, groups) * share, share), share)

        @pl.loop(0, rows // step)
        def _(i):
            at = pl.ds(pl.multiple_of(i * step, step), step)
            piece = dot(grads[at, :cols], w_ref[0, at_cols, :], ((1,), (1,)))
            for n in (1, 2):
                lanes = slice(n * cols, (n + 1) * cols)
                piece += dot(grads[at, lanes], w_ref[n, at_cols, :], ((1,), (1,)))
            part[k, at, :] = piece.astype(BF16)
            values = tokens_ref[at, at_cols].astype(F32)
            standard = (values - stats[0, at, :1]) * stats[1, at, :1]
            found = [
                jnp.sum(piece, 1, keepdims=True),
                jnp.sum(piece * standard, 1, keepdims=True),
            ]
            found = jnp.concatenate(found, 1).T
            if k == 2:
                sums[:, at] = found
            else:
                sums[:, at] += found

    def across(k):
        return copy_to(
            part.at[k], parts_ref.at[group], row_sems, k, {"head": lax.rem(group + k, groups)}
        )

    def across_sums(k):
        return copy_to(
            sums, sums_ref.at[group], row_sems, groups + k, {"head": lax.rem(group + k, groups)}
        )

    def along(kind, r, peer):
        source, target = ((early_ref, earlies_ref), (late, lates_ref))[kind]
        return copy_to(
            source.at[peer], target.at[me], sems, kind * peers + r, {"space": peer}
        )

    owns = [
        pltpu.make_async_copy(early_ref.at[me], earlies_ref.at[me], own_sems.at[0]),
        pltpu.make_async_copy(late.at[me], lates_ref.at[me], own_sems.at[1]),
        pltpu.make_async_copy(part.at[0], parts_ref.at[group], own_sems.at[2]),
        pltpu.make_async_copy(sums, sums_ref.at[group], own_sems.at[3]),
    ]
    owns[0].start()
    pl.semaphore_wait(pltpu.get_barrier_semaphore(), peers + groups - 2)
    each_peer(lambda r, torus: along(0, r, torus_peer(me, torus)).start())
    chunk(2)
    across(2).start()
    piece = width // 4
    for i in range(4):
        made = dot(normed[:, i * piece : (i + 1) * piece], grads[...], ((0,), (0,)))
        late[i * peers // 4 : (i + 1) * peers // 4] = made.astype(BF16).reshape(
            peers // 4, width // peers, 3 * cols
        )
    owns[1].start()
    each_peer(lambda r, torus: along(1, r, torus_peer(me, torus)).start())
    for k in (1, 3):
        chunk(k)
        across(k).start()
    chunk(0)
    owns[2].start()
    owns[3].start()
    for k in range(1, groups):
        across_sums(k).start()

    @pl.loop(0, (peers - 1))
    def _(r):
        along(0, r, lax.rem(me + 1, peers)).wait()
        along(1, r, lax.rem(me + 1, peers)).wait()

    for k in range(1, groups):
        across(k).wait()
        across_sums(k).wait()
    for own in owns:
        own.wait()


def finish(tokens, dq, grad_kv, w3, early, peers, groups, number):
    rows, width = tokens.shape
    cols = dq.shape[1]
    whole = pl.BlockSpec(memory_space=pl.ANY)
    vmem = pl.BlockSpec(memory_space=pltpu.VMEM)
    part = (groups, rows, width // groups)
    late = (peers, width // peers, 3 * cols)
    return pl.pallas_call(
        functools.partial(finish_kernel, peers, groups),
        in_specs=[vmem] * 4 + [whole],
        out_specs=[whole] * 4,
        out_shape=[
            jax.ShapeDtypeStruct(early.shape, BF16),
            jax.ShapeDtypeStruct(late, BF16),
            jax.ShapeDtypeStruct(part, BF16),
            jax.ShapeDtypeStruct((groups, 2, rows), F32),
        ],
        scratch_shapes=[
            pltpu.VMEM((rows, 3 * cols), BF16),
            pltpu.VMEM((rows, width), BF16),
            pltpu.VMEM(part, BF16),
            pltpu.VMEM(late, BF16),
            pltpu.VMEM((2, rows), F32),
            pltpu.VMEM((2, rows, 128), F32),
            pltpu.SemaphoreType.DMA((2, 2 * peers)),
            pltpu.SemaphoreType.DMA((2, 2 * groups)),
            pltpu.SemaphoreType.DMA((4,)),
        ],
        compiler_params=pltpu.CompilerParams(
            collective_id=number, has_side_effects=True, vmem_limit_bytes=VMEM_BYTES
        ),
    )(tokens, dq, grad_kv, w3, early)


def add_up(pieces):
    return sum(pieces[i].astype(F32) for i in range(pieces.shape[0]))


def on_device(tokens, w_qkv, w_out, neighbours, requests, cotangent):
    row_count, width = tokens.shape
    tiles = neighbours.shape[0]
    rows = row_count // tiles
    cols = w_qkv.shape[2]
    peers, groups = lax.axis_size("space"), lax.axis_size("head")
    share = cotangent.shape[1]
    column = lax.axis_index("head") * share
    w3 = jnp.transpose(w_qkv, (1, 0, 2))

    q, kv, stats, wanted, reach = project(
        tokens, w3, requests[0].T, rows, peers, groups, 2 * len(REACHES) + 3
    )
    level = sum((reach[0, 0] > r).astype(jnp.int32) for r in REACHES)
    reaches = (*REACHES, peers)

    entries = neighbours.reshape(-1)
    count = entries.shape[0]
    place = jnp.arange(count, dtype=jnp.int32)
    lower = entries[None, :] < entries[:, None]
    lower |= (entries[None, :] == entries[:, None]) & (place[None, :] < place[:, None])
    rank = jnp.sum(lower.astype(jnp.int32), 1)
    ranked = (rank[None, :] == place[:, None]).astype(jnp.int32)
    perm = jnp.sum(ranked * place[None, :], 1)
    keys = jnp.arange(tiles + peers * SLOTS, dtype=jnp.int32)
    below = (entries[None, :] < keys[:, None]).astype(jnp.int32)
    last = jnp.sum((entries[None, :] <= keys[:, None]).astype(jnp.int32), 1) - 1
    starts = jnp.sum(below, 1)
    same = 1 - jnp.max((starts[None, :] == place[:, None]).astype(jnp.int32), 1)
    grad_kv, dq, early, attended = lax.switch(
        level,
        [
            functools.partial(core, peers=peers, groups=groups, reach=r, number=n)
            for n, r in enumerate(reaches)
        ],
        *(wanted, entries, perm, same, last, q, kv, w_out, cotangent),
    )
    early = early.reshape(peers, width // peers, cols)
    early, late, part, sums = finish(
        tokens, dq, grad_kv, w3, early, peers, groups, 2 * len(reaches)
    )

    own_tokens = lax.dynamic_slice_in_dim(tokens, column, share, 1).astype(F32)
    layer_out = (own_tokens + add_up(attended)).astype(BF16)
    mean, inverse = stats[0][:, None], stats[1][:, None]
    own_standard = (own_tokens - mean) * inverse
    own_part = add_up(part)
    means = (add_up(sums) / width)[:, :, None]
    grad_tokens = (
        cotangent.astype(F32) + inverse * (own_part - means[0] - own_standard * means[1])
    ).astype(BF16)
    grad_w_out = jnp.sum(early.astype(F32), 0).T
    grad_w_qkv = jnp.sum(late.astype(F32), 0).reshape(-1, 3, cols)
    return (layer_out, grad_tokens, grad_w_qkv, grad_w_out)


def solution(mesh):
    placed = (
        P("space", None),
        P(None, None, "head"),
        P("head", None),
        P("space", None),
        P("space", None, None),
        P("space", "head"),
    )
    return jax.shard_map(
        on_device,
        mesh=mesh,
        in_specs=placed,
        out_specs=(
            P("space", "head"),
            P("space", "head"),
            P("space", None, "head"),
            P("head", "space"),
        ),
        check_vma=False,
    )
```

```python
import functools

import jax
import jax.numpy as jnp
from jax import lax
from jax.experimental import pallas as pl
from jax.experimental.pallas import tpu as pltpu
from jax.sharding import PartitionSpec as P

HEAD_DIM = 64
NEIGHBOURS = 9
NEAR = 4
REACHES = (1,)
AT_ONCE = 1
CORE_VMEM = 62 * 2**20
SLOTS = 2
EPSILON = 1e-05
F32 = jnp.float32
BF16 = jnp.bfloat16
VMEM_BYTES = 60 * 2**20


def dot(a, b, dims):
    return lax.dot_general(a, b, (dims, ((), ())), preferred_element_type=F32)


def norm_rows(tokens):
    values = tokens.astype(F32)
    mean = jnp.mean(values, axis=1, keepdims=True)
    centred = values - mean
    inverse = lax.rsqrt(jnp.mean(centred * centred, axis=1, keepdims=True) + EPSILON)
    return centred * inverse, mean, inverse


def head_cut(h):
    return slice(h * HEAD_DIM, (h + 1) * HEAD_DIM)


def project_kernel(peers, groups, tokens_ref, w_ref, requests_ref, q_ref, kv_ref, stats_ref, wanted_out_ref, reach_ref, table_ref, sems, own_sem):
    me = lax.axis_index("space")
    step = pl.program_id(0)
    heads = kv_ref.shape[1]
    own = pltpu.make_async_copy(requests_ref, table_ref.at[me], own_sem)

    def along(r, peer):
        return copy_to(requests_ref, table_ref.at[me], sems, r, {"space": peer})

    @pl.when(step == 0)
    def _():
        own.start()
        signal_all(peers, groups)

    standard, mean, inverse = norm_rows(tokens_ref[...])
    normed = standard.astype(BF16)
    stats_ref[...] = jnp.concatenate([mean, inverse], 1).T
    q = dot(normed, w_ref[0], ((1,), (0,))).astype(BF16)
    q_ref[...] = (q.astype(F32) * HEAD_DIM ** (-0.5)).astype(BF16)
    k = dot(normed, w_ref[1], ((1,), (0,))).astype(BF16)
    v = dot(normed, w_ref[2], ((1,), (0,))).astype(BF16)
    for h in range(heads):
        pair = jnp.concatenate([k[:, head_cut(h)], v[:, head_cut(h)]], 1)
        kv_ref[:, h] = pair.reshape(kv_ref.shape[0], kv_ref.shape[2], 2 * HEAD_DIM)

    @pl.when(step == 2)
    def _():
        pl.semaphore_wait(pltpu.get_barrier_semaphore(), peers + groups - 2)

        @pl.loop(1, peers)
        def _(r):
            along(r, lax.rem(me + r, peers)).start()

    @pl.when(step == pl.num_programs(0) - 1)
    def _():
        @pl.loop(1, peers)
        def _(r):
            along(r, lax.rem(me + r, peers)).wait()

        own.wait()
        source = lax.broadcasted_iota(jnp.int32, (peers, peers), 0)
        target = lax.broadcasted_iota(jnp.int32, (peers, peers), 1)
        found = []
        for c in range(SLOTS):
            asked = table_ref[:, c, :].astype(F32)
            found.append(jnp.sum(jnp.where(target == me, asked, 0.0), 1, keepdims=True))
        wanted_out_ref[...] = jnp.concatenate(found, 1).astype(jnp.int32)
        apart = jnp.abs(source - target)
        apart = jnp.minimum(apart, peers - apart).astype(F32)
        apart = jnp.where(table_ref[:, 1, :] >= 0, apart, 0.0)
        apart = jnp.max(jnp.max(apart, 1, keepdims=True), 0, keepdims=True)
        reach_ref[...] = apart.astype(jnp.int32)


def project(tokens, w3, requests, tile_rows, peers, groups, number):
    rows, width = tokens.shape
    cols = w3.shape[2]
    step = 256
    kv_block = (step // tile_rows, cols // HEAD_DIM, tile_rows, 2 * HEAD_DIM)
    return pl.pallas_call(
        functools.partial(project_kernel, peers, groups),
        grid=(rows // step,),
        in_specs=[
            pl.BlockSpec((step, width), lambda i: (i, 0)),
            pl.BlockSpec((3, width, cols), lambda i: (0, 0, 0)),
            pl.BlockSpec(memory_space=pl.ANY),
        ],
        out_specs=[
            pl.BlockSpec((step, cols), lambda i: (i, 0)),
            pl.BlockSpec(kv_block, lambda i: (i, 0, 0, 0)),
            pl.BlockSpec((2, step), lambda i: (0, i)),
            pl.BlockSpec((peers, SLOTS), lambda i: (0, 0)),
            pl.BlockSpec((1, 1), lambda i: (0, 0)),
        ],
        out_shape=[
            jax.ShapeDtypeStruct((rows, cols), BF16),
            jax.ShapeDtypeStruct((rows // tile_rows,) + kv_block[1:], BF16),
            jax.ShapeDtypeStruct((2, rows), F32),
            jax.ShapeDtypeStruct((peers, SLOTS), requests.dtype),
            jax.ShapeDtypeStruct((1, 1), requests.dtype),
        ],
        scratch_shapes=[
            pltpu.VMEM((peers,) + requests.shape, requests.dtype),
            pltpu.SemaphoreType.DMA((2, peers)),
            pltpu.SemaphoreType.DMA,
        ],
        compiler_params=pltpu.CompilerParams(
            collective_id=number, has_side_effects=True, vmem_limit_bytes=VMEM_BYTES
        ),
    )(tokens, w3, requests)


def copy_to(src, dst, sems, index, device):
    return pltpu.make_async_remote_copy(
        src_ref=src,
        dst_ref=dst,
        send_sem=sems.at[0, index],
        recv_sem=sems.at[1, index],
        device_id=device,
        device_id_type=pl.DeviceIdType.MESH,
    )


def greet(peers, groups):
    signal_all(peers, groups)
    pl.semaphore_wait(pltpu.get_barrier_semaphore(), peers + groups - 2)


def signal_all(peers, groups):
    barrier = pltpu.get_barrier_semaphore()
    me, group = lax.axis_index("space"), lax.axis_index("head")

    @pl.loop(1, peers)
    def _(r):
        pl.semaphore_signal(
            barrier,
            inc=1,
            device_id={"space": lax.rem(me + r, peers)},
            device_id_type=pl.DeviceIdType.MESH,
        )

    for k in range(1, groups):
        pl.semaphore_signal(
            barrier,
            inc=1,
            device_id={"head": lax.rem(group + k, groups)},
            device_id_type=pl.DeviceIdType.MESH,
        )


def axis_steps(q):
    far = 1 + 2 * lax.rem(q, 2)
    return (q // 2) * far, (1 - q // 2) * far


def corner_steps(q):
    return 1 + 2 * lax.rem(q, 2), 1 + 2 * lax.rem(lax.rem(q, 2) + q // 2, 2)


def across_steps(q):
    return 2 * q, 2 - 2 * q


def knight_steps(q):
    odd = lax.rem(q, 2)
    return 2 * odd + (1 - odd) * (1 + q), 2 * (1 - odd) + odd * q


def opposite_steps(q):
    return 2 + 0 * q, 2 + 0 * q


GROUPS = (
    (4, axis_steps),
    (4, corner_steps),
    (2, across_steps),
    (4, knight_steps),
    (1, opposite_steps),
)


def each_peer(act):
    act(0, (0, 0, 1))
    base = 1
    for size, steps in GROUPS:

        @pl.loop(0, 2 * size)
        def _(n, size=size, steps=steps, base=base):
            act(base + n, (*steps(lax.rem(n, size)), n // size))

        base += 2 * size


def torus_peer(me, step):
    z = lax.rem(me // 8 + step[0], 4)
    x = lax.rem(lax.rem(me // 2, 4) + step[1], 4)
    return z * 8 + x * 2 + lax.rem(lax.rem(me, 2) + step[2], 2)


def torus_source(me, step):
    return torus_peer(me, (4 - step[0], 4 - step[1], step[2]))


def second_ranges(peers, reach):
    if 2 * reach >= peers - 1:
        return [(1, peers)]
    return [(1, reach + 1), (peers - reach, peers)]


def core_kernel(peers, groups, reach, wanted_ref, entries_ref, perm_ref, same_ref, last_ref, q_ref, kv_ref, w_out_ref, cot_ref, grad_kv_ref, dq_ref, early_ref, atts_ref, staged0, staged1, got0, got1, landed0, landed1, held, near_runs, far_runs, running, total, cots, grad_att, att, part, kv_sems, back_sems, row_sems, own_sems):
    me, group = lax.axis_index("space"), lax.axis_index("head")
    staged, got, landed = (staged0, staged1), (got0, got1), (landed0, landed1)
    tiles, heads, span = kv_ref.shape[:3]
    cols = q_ref.shape[1]
    share = cot_ref.shape[1]
    rows = q_ref.shape[0]
    half_heads = heads // 2
    near_count = tiles * NEAR
    entry_count = tiles * NEIGHBOURS
    greet(peers, groups)

    def across(kind, k):
        peer = lax.rem(group + k, groups)
        source = cot_ref if kind == 0 else part.at[peer]
        target = (cots, atts_ref)[kind].at[group]
        return copy_to(source, target, row_sems, kind * groups + k, {"head": peer})

    def send(half, c, r, peer):
        return copy_to(
            staged[half].at[c * peers + r],
            got[half].at[me * SLOTS + c],
            kv_sems.at[half],
            c * peers + r,
            {"space": peer},
        )

    def give(half, c, r, peer):
        return copy_to(
            staged[half].at[c * peers + r],
            landed[half].at[c * peers + r],
            back_sems.at[half],
            c * peers + r,
            {"space": peer},
        )

    own_cot = pltpu.make_async_copy(cot_ref, cots.at[group], own_sems.at[0])
    own_cot.start()
    for k in range(1, groups):
        across(0, k).start()
    for half in range(2):
        cut = slice(half * half_heads, (half + 1) * half_heads)

        @each_peer
        def _(i, step, half=half, cut=cut):
            peer = torus_peer(me, step)
            staged[half][i] = kv_ref[jnp.maximum(wanted_ref[peer, 0], 0), cut]
            send(half, 0, i, peer).start()

        for low, high in second_ranges(peers, reach):

            @pl.loop(low, high)
            def _(r, half=half, cut=cut):
                peer = lax.rem(me + r, peers)
                tile = jnp.maximum(wanted_ref[peer, 1], 0)
                staged[half][peers + r] = kv_ref[tile, cut]
                send(half, 1, r, peer).start()

    for k in range(1, groups):
        across(0, k).wait()
    own_cot.wait()
    step_rows = 2 * span

    @pl.loop(0, rows // step_rows)
    def _(i):
        at = pl.ds(pl.multiple_of(i * step_rows, step_rows), step_rows)
        cot = jnp.concatenate([cots[g, at, :] for g in range(groups)], 1)
        grad_att[at, :] = dot(cot, w_out_ref[...], ((1,), (1,))).astype(BF16)

    left = lax.broadcasted_iota(jnp.int32, (128, 128), 1) < HEAD_DIM
    upper = lax.broadcasted_iota(jnp.int32, (128, 128), 0) < HEAD_DIM

    def attend(half):
        @pl.loop(0, tiles // AT_ONCE)
        def _(turn):
            def tile_rows(u):
                return pl.ds(pl.multiple_of((turn * AT_ONCE + u) * span, span), span)

            def begin(u, hh):
                h = half * half_heads + hh
                at = tile_rows(u)
                first = (turn * AT_ONCE + u) * NEIGHBOURS
                pair = jnp.concatenate([q_ref[at, head_cut(h)], grad_att[at, head_cut(h)]], 1)
                pair_t = pair.T
                zero = jnp.zeros_like(pair)
                stacked = jnp.concatenate(
                    [jnp.where(left, pair, zero), jnp.where(left, zero, pair)], 0
                )
                stacked_t = jnp.concatenate(
                    [jnp.where(upper, pair_t, zero), jnp.where(upper, zero, pair_t)], 1
                )
                keys = [kv_ref[entries_ref[first + j], h] for j in range(NEAR)]
                keys += [
                    got[half][jnp.maximum(entries_ref[first + j] - tiles, 0), hh]
                    for j in range(NEAR, NEIGHBOURS)
                ]
                kv = jnp.concatenate(keys, 0)
                return stacked_t, kv, dot(stacked, kv, ((1,), (1,)))

            mixed = {}
            order = [(u, hh) for u in range(AT_ONCE) for hh in range(half_heads)]
            following = begin(*order[0])
            for n, (u, hh) in enumerate(order):
                stacked_t, kv, both = following
                if n + 1 < len(order):
                    following = begin(*order[n + 1])
                scores = both[:128]
                grad_prob = both[128:]
                weights = jnp.exp(scores - jnp.max(scores, axis=1, keepdims=True))
                inverse = 1.0 / jnp.sum(weights, axis=1, keepdims=True)
                row_delta = jnp.sum(weights * grad_prob, axis=1, keepdims=True) * inverse
                likely = weights * inverse
                grad_score = likely * (grad_prob - row_delta)
                factors = jnp.concatenate([grad_score.astype(BF16), likely.astype(BF16)], 0)
                mixed[u, hh] = dot(factors, kv, ((1,), (0,)))
                grad_kv_t = dot(stacked_t, factors, ((1,), (0,)))
                first = (turn * AT_ONCE + u) * NEIGHBOURS
                for j in range(NEIGHBOURS):
                    held[first + j, hh] = grad_kv_t[:, j * 128 : (j + 1) * 128]
            lanes = slice(half * half_heads * HEAD_DIM, (half + 1) * half_heads * HEAD_DIM)
            for u in range(AT_ONCE):
                both = [mixed[u, hh] for hh in range(half_heads)]
                dq = jnp.concatenate([m[:128, :HEAD_DIM] for m in both], 1)
                dq_ref[tile_rows(u), lanes] = (dq * HEAD_DIM ** (-0.5)).astype(BF16)
                attended = jnp.concatenate([m[128:, HEAD_DIM:] for m in both], 1)
                att[tile_rows(u), lanes] = attended.astype(BF16)

        def run(i):
            keep = jnp.where(same_ref[i] > 0, 1.0, 0.0)
            value = running[...] * keep + held[perm_ref[i]]
            running[...] = value
            return value

        running[...] = jnp.zeros_like(running)

        @pl.loop(0, near_count)
        def _(i):
            near_runs[i] = run(i)

        @pl.loop(near_count, entry_count)
        def _(i):
            far_runs[i - near_count] = run(i).astype(BF16)

        @each_peer
        def _(i, step):
            peer = torus_peer(me, step)
            place = jnp.maximum(last_ref[tiles + peer * SLOTS] - near_count, 0)
            staged[half][i] = far_runs[place]
            give(half, 0, i, peer).start()

        for low, high in second_ranges(peers, reach):

            @pl.loop(low, high)
            def _(r):
                peer = lax.rem(me + r, peers)
                place = jnp.maximum(last_ref[tiles + peer * SLOTS + 1] - near_count, 0)
                staged[half][peers + r] = far_runs[place]
                give(half, 1, r, peer).start()

        @pl.loop(0, tiles)
        def _(t):
            total[half, t] = near_runs[jnp.maximum(last_ref[t], 0)]

    beside = lax.rem(me + 1, peers)
    for half in range(2):

        @pl.loop(0, (peers - 1))
        def _(i, half=half):
            send(half, 0, i, beside).wait()

        for low, high in second_ranges(peers, reach):

            @pl.loop(low, high)
            def _(r, half=half):
                send(half, 1, r, beside).wait()

        attend(half)

    own_att = pltpu.make_async_copy(part.at[group], atts_ref.at[group], own_sems.at[1])
    for g in range(groups):

        @pl.loop(0, rows // step_rows)
        def _(i, g=g):
            at = pl.ds(pl.multiple_of(i * step_rows, step_rows), step_rows)
            lanes = slice(g * share, (g + 1) * share)
            made = dot(att[at, :], w_out_ref[:, lanes], ((1,), (0,)))
            part[g, at, :] = made.astype(BF16)

    own_att.start()
    for k in range(1, groups):
        across(1, k).start()
    for g in range(groups):
        made = dot(cots[g], att[...], ((0,), (0,)))
        early_ref[g * share : (g + 1) * share, :] = made.astype(BF16)

    for half in range(2):

        def add(c, r, source, half=half):
            tile = wanted_ref[source, c]
            block = landed[half][c * peers + r].astype(F32)

            @pl.loop(0, tiles)
            def _(t):
                total[half, t] += block * jnp.where(tile == t, 1.0, 0.0)

        @each_peer
        def _(i, step, half=half, add=add):
            give(half, 0, i, torus_peer(me, step)).wait()
            add(0, i, torus_source(me, step))

        for low, high in second_ranges(peers, reach):

            @pl.loop(low, high)
            def _(r, half=half, add=add):
                give(half, 1, r, lax.rem(me + r, peers)).wait()
                add(1, r, lax.rem(me + peers - r, peers))

        grad_kv_ref[:, half * half_heads : (half + 1) * half_heads] = total[half].astype(BF16)
    for k in range(1, groups):
        across(1, k).wait()
    own_att.wait()


def core(wanted, entries, perm, same, last, q, kv, w_out, cot, peers, groups, reach, number):
    tiles, heads, span, mixed = kv.shape
    rows, cols = q.shape
    width = w_out.shape[1]
    half = (heads // 2, span, mixed)
    slots = pltpu.VMEM((peers * SLOTS,) + half, BF16)
    smem = pl.BlockSpec(memory_space=pltpu.SMEM)
    vmem = pl.BlockSpec(memory_space=pltpu.VMEM)
    whole = pl.BlockSpec(memory_space=pl.ANY)
    parts = (groups,) + cot.shape
    return pl.pallas_call(
        functools.partial(core_kernel, peers, groups, reach),
        in_specs=[smem] * 5 + [vmem] * 3 + [whole],
        out_specs=[vmem] * 3 + [whole],
        out_shape=[
            jax.ShapeDtypeStruct(kv.shape, BF16),
            jax.ShapeDtypeStruct(q.shape, BF16),
            jax.ShapeDtypeStruct((width, cols), BF16),
            jax.ShapeDtypeStruct(parts, BF16),
        ],
        scratch_shapes=[slots] * 6
        + [
            pltpu.VMEM((tiles * NEIGHBOURS,) + half, F32),
            pltpu.VMEM((tiles * NEAR,) + half, F32),
            pltpu.VMEM((tiles * (NEIGHBOURS - NEAR),) + half, BF16),
            pltpu.VMEM(half, F32),
            pltpu.VMEM((2, tiles) + half, F32),
            pltpu.VMEM(parts, BF16),
            pltpu.VMEM(q.shape, BF16),
            pltpu.VMEM(q.shape, BF16),
            pltpu.VMEM(parts, BF16),
            pltpu.SemaphoreType.DMA((2, 2, SLOTS * peers)),
            pltpu.SemaphoreType.DMA((2, 2, SLOTS * peers)),
            pltpu.SemaphoreType.DMA((2, 2 * groups)),
            pltpu.SemaphoreType.DMA((2,)),
        ],
        compiler_params=pltpu.CompilerParams(
            collective_id=number, has_side_effects=True, vmem_limit_bytes=CORE_VMEM
        ),
    )(wanted, entries, perm, same, last, q, kv, w_out, cot)


def finish_kernel(peers, groups, tokens_ref, dq_ref, grad_kv_ref, w_ref, early_ref, earlies_ref, lates_ref, parts_ref, sums_ref, grads, normed, part, late, sums, stats, sems, row_sems, own_sems):
    me, group = lax.axis_index("space"), lax.axis_index("head")
    signal_all(peers, groups)
    rows, width = tokens_ref.shape
    cols = dq_ref.shape[1]
    share = width // groups
    tiles, heads = grad_kv_ref.shape[:2]
    span = rows // tiles
    step = 256

    @pl.loop(0, rows // step)
    def _(i):
        at = pl.ds(pl.multiple_of(i * step, step), step)
        standard, mean, inverse = norm_rows(tokens_ref[at, :])
        normed[at, :] = standard.astype(BF16)
        stats[0, at, :] = jnp.broadcast_to(mean, (step, 128))
        stats[1, at, :] = jnp.broadcast_to(inverse, (step, 128))
        grads[at, :cols] = dq_ref[at, :]

    for t in range(tiles):
        pairs = [grad_kv_ref[t, h].T for h in range(heads)]
        at = slice(t * span, (t + 1) * span)
        grads[at, cols : 2 * cols] = jnp.concatenate([p[:, :HEAD_DIM] for p in pairs], 1)
        grads[at, 2 * cols :] = jnp.concatenate([p[:, HEAD_DIM:] for p in pairs], 1)

    def chunk(k):
        at_cols = pl.ds(pl.multiple_of(lax.rem(group + k, groups) * share, share), share)

        @pl.loop(0, rows // step)
        def _(i):
            at = pl.ds(pl.multiple_of(i * step, step), step)
            piece = dot(grads[at, :cols], w_ref[0, at_cols, :], ((1,), (1,)))
            for n in (1, 2):
                lanes = slice(n * cols, (n + 1) * cols)
                piece += dot(grads[at, lanes], w_ref[n, at_cols, :], ((1,), (1,)))
            part[k, at, :] = piece.astype(BF16)
            values = tokens_ref[at, at_cols].astype(F32)
            standard = (values - stats[0, at, :1]) * stats[1, at, :1]
            found = [
                jnp.sum(piece, 1, keepdims=True),
                jnp.sum(piece * standard, 1, keepdims=True),
            ]
            found = jnp.concatenate(found, 1).T
            if k == 2:
                sums[:, at] = found
            else:
                sums[:, at] += found

    def across(k):
        return copy_to(
            part.at[k], parts_ref.at[group], row_sems, k, {"head": lax.rem(group + k, groups)}
        )

    def across_sums(k):
        return copy_to(
            sums, sums_ref.at[group], row_sems, groups + k, {"head": lax.rem(group + k, groups)}
        )

    def along(kind, r, peer):
        source, target = ((early_ref, earlies_ref), (late, lates_ref))[kind]
        return copy_to(
            source.at[peer], target.at[me], sems, kind * peers + r, {"space": peer}
        )

    owns = [
        pltpu.make_async_copy(early_ref.at[me], earlies_ref.at[me], own_sems.at[0]),
        pltpu.make_async_copy(late.at[me], lates_ref.at[me], own_sems.at[1]),
        pltpu.make_async_copy(part.at[0], parts_ref.at[group], own_sems.at[2]),
        pltpu.make_async_copy(sums, sums_ref.at[group], own_sems.at[3]),
    ]
    owns[0].start()
    pl.semaphore_wait(pltpu.get_barrier_semaphore(), peers + groups - 2)
    each_peer(lambda r, torus: along(0, r, torus_peer(me, torus)).start())
    chunk(2)
    across(2).start()
    piece = width // 4
    for i in range(4):
        made = dot(normed[:, i * piece : (i + 1) * piece], grads[...], ((0,), (0,)))
        late[i * peers // 4 : (i + 1) * peers // 4] = made.astype(BF16).reshape(
            peers // 4, width // peers, 3 * cols
        )
    owns[1].start()
    each_peer(lambda r, torus: along(1, r, torus_peer(me, torus)).start())
    for k in (1, 3):
        chunk(k)
        across(k).start()
    chunk(0)
    owns[2].start()
    owns[3].start()
    for k in range(1, groups):
        across_sums(k).start()

    @pl.loop(0, (peers - 1))
    def _(r):
        along(0, r, lax.rem(me + 1, peers)).wait()
        along(1, r, lax.rem(me + 1, peers)).wait()

    for k in range(1, groups):
        across(k).wait()
        across_sums(k).wait()
    for own in owns:
        own.wait()


def finish(tokens, dq, grad_kv, w3, early, peers, groups, number):
    rows, width = tokens.shape
    cols = dq.shape[1]
    whole = pl.BlockSpec(memory_space=pl.ANY)
    vmem = pl.BlockSpec(memory_space=pltpu.VMEM)
    part = (groups, rows, width // groups)
    late = (peers, width // peers, 3 * cols)
    return pl.pallas_call(
        functools.partial(finish_kernel, peers, groups),
        in_specs=[vmem] * 4 + [whole],
        out_specs=[whole] * 4,
        out_shape=[
            jax.ShapeDtypeStruct(early.shape, BF16),
            jax.ShapeDtypeStruct(late, BF16),
            jax.ShapeDtypeStruct(part, BF16),
            jax.ShapeDtypeStruct((groups, 2, rows), F32),
        ],
        scratch_shapes=[
            pltpu.VMEM((rows, 3 * cols), BF16),
            pltpu.VMEM((rows, width), BF16),
            pltpu.VMEM(part, BF16),
            pltpu.VMEM(late, BF16),
            pltpu.VMEM((2, rows), F32),
            pltpu.VMEM((2, rows, 128), F32),
            pltpu.SemaphoreType.DMA((2, 2 * peers)),
            pltpu.SemaphoreType.DMA((2, 2 * groups)),
            pltpu.SemaphoreType.DMA((4,)),
        ],
        compiler_params=pltpu.CompilerParams(
            collective_id=number, has_side_effects=True, vmem_limit_bytes=VMEM_BYTES
        ),
    )(tokens, dq, grad_kv, w3, early)


def add_up(pieces):
    return sum(pieces[i].astype(F32) for i in range(pieces.shape[0]))


def on_device(tokens, w_qkv, w_out, neighbours, requests, cotangent):
    row_count, width = tokens.shape
    tiles = neighbours.shape[0]
    rows = row_count // tiles
    cols = w_qkv.shape[2]
    peers, groups = lax.axis_size("space"), lax.axis_size("head")
    share = cotangent.shape[1]
    column = lax.axis_index("head") * share
    w3 = jnp.transpose(w_qkv, (1, 0, 2))

    q, kv, stats, wanted, reach = project(
        tokens, w3, requests[0].T, rows, peers, groups, 2 * len(REACHES) + 3
    )
    level = sum((reach[0, 0] > r).astype(jnp.int32) for r in REACHES)
    reaches = (*REACHES, peers)

    entries = neighbours.reshape(-1)
    count = entries.shape[0]
    place = jnp.arange(count, dtype=jnp.int32)
    lower = entries[None, :] < entries[:, None]
    lower |= (entries[None, :] == entries[:, None]) & (place[None, :] < place[:, None])
    rank = jnp.sum(lower.astype(jnp.int32), 1)
    ranked = (rank[None, :] == place[:, None]).astype(jnp.int32)
    perm = jnp.sum(ranked * place[None, :], 1)
    keys = jnp.arange(tiles + peers * SLOTS, dtype=jnp.int32)
    below = (entries[None, :] < keys[:, None]).astype(jnp.int32)
    last = jnp.sum((entries[None, :] <= keys[:, None]).astype(jnp.int32), 1) - 1
    starts = jnp.sum(below, 1)
    same = 1 - jnp.max((starts[None, :] == place[:, None]).astype(jnp.int32), 1)
    grad_kv, dq, early, attended = lax.switch(
        level,
        [
            functools.partial(core, peers=peers, groups=groups, reach=r, number=n)
            for n, r in enumerate(reaches)
        ],
        *(wanted, entries, perm, same, last, q, kv, w_out, cotangent),
    )
    early = early.reshape(peers, width // peers, cols)
    early, late, part, sums = finish(
        tokens, dq, grad_kv, w3, early, peers, groups, 2 * len(reaches)
    )

    own_tokens = lax.dynamic_slice_in_dim(tokens, column, share, 1).astype(F32)
    layer_out = (own_tokens + add_up(attended)).astype(BF16)
    mean, inverse = stats[0][:, None], stats[1][:, None]
    own_standard = (own_tokens - mean) * inverse
    own_part = add_up(part)
    means = (add_up(sums) / width)[:, :, None]
    grad_tokens = (
        cotangent.astype(F32) + inverse * (own_part - means[0] - own_standard * means[1])
    ).astype(BF16)
    grad_w_out = jnp.sum(early.astype(F32), 0).T
    grad_w_qkv = jnp.sum(late.astype(F32), 0).reshape(-1, 3, cols)
    return (layer_out, grad_tokens, grad_w_qkv, grad_w_out)


def solution(mesh):
    placed = (
        P("space", None),
        P(None, None, "head"),
        P("head", None),
        P("space", None),
        P("space", None, None),
        P("space", "head"),
    )
    return jax.shard_map(
        on_device,
        mesh=mesh,
        in_specs=placed,
        out_specs=(
            P("space", "head"),
            P("space", "head"),
            P("space", None, "head"),
            P("head", "space"),
        ),
        check_vma=False,
    )
```
